128 devices in a mesh: gx: 2 (over z_lo), gy: 4 (over x), mem: 16 (over z_hi, y, core).
Axes of the slice: x: 4, y: 4, z: 4 (z_hi: 2, z_lo: 2; z = z_hi * 2 + z_lo), core: 2. Of those that a mesh axis runs over, the one named last changes fastest.
Arguments:
- prior_members: float32 [8, 512, 128, 512], P(None, 'mem', 'gx', 'gy'), may hold values from -30 to 30
- courant_x: float32 [128, 512], P('gx', 'gy'), may hold values from -0.4 to 0.4
- courant_y: float32 [128, 512], P('gx', 'gy'), may hold values from -0.4 to 0.4
- diffusion: float32 [128, 512], P('gx', 'gy'), may hold values from 0.01 to 0.05
- report_level: int32 [32, 4, 256], P('gx', 'gy'), may hold values from 0 to 3
- report_cell: int32 [32, 4, 256], P('gx', 'gy'), may hold values from 0 to 511
- report_value: float32 [32, 4, 256], P('gx', 'gy'), may hold values from -6 to 6
- report_precision: float32 [32, 4, 256], P('gx', 'gy'), may hold values from 0.5 to 4
- report_class: int32 [32, 4, 256], P('gx', 'gy'), may hold values from 0 to 7
- report_count: int32 [32, 4], P('gx', 'gy'), may hold values from 64 to 256, as said below
Outputs:
- analysis: float32 [8, 512, 128, 512], P(None, 'mem', 'gx', 'gy')
The draws below stay inside these ranges and needn't reach their ends.
Inputs may be any that keep to these rules, and one draw needn't show every extreme that they name: A tile uses observation slots 0 to report_count - 1; some tile uses all 256.
All inputs are finite; a program needn't handle non-finite values.
Results may differ from the reference program's by a relative error of at most 0.0003.
Values sent between devices are 32-bit elements; how exact they have to be, the bound alone decides.
No kernel may reach another device: no remote copies, remote signals or barrier semaphores. Data moves between devices by JAX's collectives and lax.ppermute only.
A program may use at most 192 MiB of HBM per device.

```python
import math
import jax
import jax.numpy as jnp
from jax import lax

MEMBER_COUNT = 512
LEVELS = 4
PROGNOSTIC_VARS = 8
PATCH_HEIGHT = 4
PATCH_WIDTH = 128
TILE_CELLS = 512
OBS_SLOTS = 256
CLASSES = 8
STEPS = 2
NEWTON = 8
GRID_X = 128
GRID_Y = 512


def draw_prior_members(key, part):
    key_member, key_scale = jax.random.split(key, 2)
    scales = jnp.exp(jax.random.uniform(key_scale, (1, MEMBER_COUNT, 1, 1), jnp.float32, math.log(0.3), math.log(3.0)))
    member_noise = jax.random.normal(key_member, (PROGNOSTIC_VARS, MEMBER_COUNT, GRID_X, GRID_Y), jnp.float32)
    values = member_noise * scales
    return jnp.clip(values, -30.0, 30.0)


def draw_report_count(key, part):
    key_counts, key_chosen = jax.random.split(jax.random.fold_in(key, 17))
    tiles_x = GRID_X // PATCH_HEIGHT
    tiles_y = GRID_Y // PATCH_WIDTH
    counts = jax.random.randint(key_counts, (tiles_x * tiles_y,), OBS_SLOTS // 4, OBS_SLOTS + 1)
    chosen = jax.random.randint(key_chosen, (), 0, tiles_x * tiles_y)
    flattened = jnp.where(jnp.arange(tiles_x * tiles_y) == chosen, OBS_SLOTS, counts)
    return flattened.reshape(tiles_x, tiles_y).astype(jnp.int32)


def touch_ends(values, key, smallest, top_value):
    longest = values.shape.index(max(values.shape))
    spots = []
    for shift in (0, 1):
        where = [jax.random.randint(jax.random.fold_in(key, axis), (), 0, length) for axis, length in enumerate(values.shape)]
        where[longest] = (where[longest] + shift) % values.shape[longest]
        spots.append(tuple(where))
    return values.at[spots[0]].set(smallest).at[spots[1]].set(top_value)


def block_scale(own_key, shape, pieces, smallest, high):
    def one(axis_at, blocks):
        draws = jax.random.uniform(jax.random.fold_in(jax.random.fold_in(own_key, 6), axis_at), (blocks,), jnp.float32, smallest / len(pieces), high / len(pieces))
        return jnp.repeat(jnp.exp(draws), shape[axis_at] // blocks).reshape((-1,) + (1,) * (len(shape) - axis_at - 1))

    gain = one(*pieces[0])
    for cut in pieces[1:]:
        gain = gain * one(*cut)
    return gain


def gaussian(key, shape, scale, most, pieces=(), kind=jnp.bfloat16):
    result = jax.random.normal(key, shape, jnp.float32) * scale
    if len(pieces) > 0:
        result = block_scale(key, shape, pieces, -0.22, 0.18) * result
    return jnp.clip(result, min=-most, max=most).astype(kind)


def setup_inputs(seed: int = 0) -> dict:
    key_of = jax.random.split(jax.random.key(seed), 11)
    return {
        "prior_members": draw_prior_members(jax.random.fold_in(key_of[10], 71), 0),
        "courant_x": jnp.clip(jax.random.uniform(key_of[1], (GRID_X, GRID_Y), jnp.float32, -0.4, 0.4) * block_scale(key_of[1], (GRID_X, GRID_Y), ((0, 2), (1, 4)), -0.4, 0.0), -0.4, 0.4),
        "courant_y": jnp.clip(jax.random.uniform(key_of[2], (GRID_X, GRID_Y), jnp.float32, -0.4, 0.4) * block_scale(key_of[2], (GRID_X, GRID_Y), ((0, 2), (1, 4)), -0.4, 0.0), -0.4, 0.4),
        "diffusion": jnp.clip(jnp.exp(math.log(0.05) - 1.609438 * jax.random.uniform(key_of[3], (GRID_X, GRID_Y), jnp.float32) ** block_scale(key_of[3], (GRID_X, GRID_Y), ((0, 2), (1, 4)), -0.2, 0.2)), 0.01, 0.05),
        "report_level": touch_ends(jax.random.randint(key_of[4], (GRID_X // PATCH_HEIGHT, GRID_Y // PATCH_WIDTH, OBS_SLOTS), 0, LEVELS), jax.random.fold_in(key_of[4], 1), 0, LEVELS - 1).astype(jnp.int32),
        "report_cell": touch_ends(jax.random.randint(key_of[5], (GRID_X // PATCH_HEIGHT, GRID_Y // PATCH_WIDTH, OBS_SLOTS), 0, TILE_CELLS), jax.random.fold_in(key_of[5], 1), 0, TILE_CELLS - 1).astype(jnp.int32),
        "report_value": gaussian(key_of[6], (GRID_X // PATCH_HEIGHT, GRID_Y // PATCH_WIDTH, OBS_SLOTS), 1.5, 6.0, ((0, 2), (1, 4)), jnp.float32),
        "report_precision": jnp.clip(jnp.exp(math.log(4.0) - 2.0794415 * jax.random.uniform(key_of[7], (GRID_X // PATCH_HEIGHT, GRID_Y // PATCH_WIDTH, OBS_SLOTS), jnp.float32) ** block_scale(key_of[7], (GRID_X // PATCH_HEIGHT, GRID_Y // PATCH_WIDTH, OBS_SLOTS), ((0, 2), (1, 4)), -0.2, 0.2)), 0.5, 4.0),
        "report_class": touch_ends(jax.random.randint(key_of[8], (GRID_X // PATCH_HEIGHT, GRID_Y // PATCH_WIDTH, OBS_SLOTS), 0, CLASSES), jax.random.fold_in(key_of[8], 1), 0, CLASSES - 1).astype(jnp.int32),
        "report_count": draw_report_count(jax.random.fold_in(key_of[10], 71), 0),
    }


def update(centre, western, eastern, southern, northern, plus_x, minus_x, plus_y, minus_y, spread):
    moved = centre - plus_x * (centre - western) - minus_x * (eastern - centre)
    moved = moved - plus_y * (centre - southern) - minus_y * (northern - centre)
    return moved + spread * (eastern + western + northern + southern - 4.0 * centre)

def mixing_matrix(raw_values, report_value, report_precision, report_class, slot_count):
    members = raw_values.shape[0]
    slots = raw_values.shape[1]
    centre_obs = lax.optimization_barrier(jnp.sum(raw_values, axis=0)) / members
    observed = raw_values - centre_obs
    innovation = report_value - centre_obs
    usable = (jnp.arange(slots) < slot_count).astype(jnp.float32)
    weight = usable * report_precision / (1.0 + report_class.astype(jnp.float32))
    identity = jnp.eye(members, dtype=jnp.float32)
    gram_matrix = jnp.dot(observed * weight, observed.T, precision=lax.Precision.HIGHEST) + (members - 1.0) * identity
    norm_scale = jnp.sqrt(jnp.sum(gram_matrix * gram_matrix))
    root_y = gram_matrix / norm_scale
    root_z = identity
    for iteration in range(NEWTON):
        factor = 1.5 * identity - 0.5 * jnp.dot(root_z, root_y, precision=lax.Precision.HIGHEST)
        new_z = jnp.dot(factor, root_z, precision=lax.Precision.HIGHEST)
        if iteration + 1 < NEWTON:
            root_y = jnp.dot(root_y, factor, precision=lax.Precision.HIGHEST)
        root_z = new_z
    driven = jnp.dot(observed, weight * innovation, precision=lax.Precision.HIGHEST)
    mean_shift = jnp.dot(root_z, jnp.dot(root_z, driven, precision=lax.Precision.HIGHEST), precision=lax.Precision.HIGHEST) / norm_scale
    return jnp.sqrt((members - 1.0) / norm_scale) * root_z + mean_shift[:, None]

def transform(taper_patch, mixing):
    members = taper_patch.shape[1]
    centre = lax.optimization_barrier(jnp.sum(taper_patch, axis=1, keepdims=True)) / members
    anomaly = taper_patch - centre
    return centre + jnp.einsum('fjc,jk->fkc', anomaly, mixing, precision=lax.Precision.HIGHEST)

def reference(prior_members, courant_x, courant_y, diffusion, report_level, report_cell, report_value, report_precision, report_class, report_count):
    plus_x = jnp.maximum(courant_x, 0.0)
    minus_x = jnp.minimum(courant_x, 0.0)
    plus_y = jnp.maximum(courant_y, 0.0)
    minus_y = jnp.minimum(courant_y, 0.0)

    def projected_grid(model_fields):
        for number in range(STEPS):
            eastern = jnp.roll(model_fields, -1, axis=1)
            western = jnp.roll(model_fields, 1, axis=1)
            northern = jnp.roll(model_fields, -1, axis=2)
            southern = jnp.roll(model_fields, 1, axis=2)
            model_fields = update(model_fields, western, eastern, southern, northern, plus_x, minus_x, plus_y, minus_y, diffusion)
        return model_fields
    propagated_members = lax.map(projected_grid, prior_members)
    tiles_x = GRID_X // PATCH_HEIGHT
    tiles_y = GRID_Y // PATCH_WIDTH

    def analyse_tile(position):
        tile_row = (position // tiles_y).astype(jnp.int32)
        tile_column = (position % tiles_y).astype(jnp.int32)
        patch_corners = (jnp.int32(0), jnp.int32(0), (tile_row * PATCH_HEIGHT).astype(jnp.int32), (tile_column * PATCH_WIDTH).astype(jnp.int32))
        taper_patch = lax.dynamic_slice(propagated_members, patch_corners, (PROGNOSTIC_VARS, MEMBER_COUNT, PATCH_HEIGHT, PATCH_WIDTH)).reshape(PROGNOSTIC_VARS, MEMBER_COUNT, PATCH_HEIGHT * PATCH_WIDTH)
        level_index = report_level[tile_row, tile_column]
        cell_index = report_cell[tile_row, tile_column]
        raw_values = taper_patch[level_index, :, cell_index].T
        mixing = mixing_matrix(raw_values, report_value[tile_row, tile_column], report_precision[tile_row, tile_column], report_class[tile_row, tile_column], report_count[tile_row, tile_column])
        return transform(taper_patch, mixing)
    analysed = lax.map(analyse_tile, jnp.arange(tiles_x * tiles_y, dtype=jnp.int32))
    analysed = analysed.reshape(tiles_x, tiles_y, PROGNOSTIC_VARS, MEMBER_COUNT, PATCH_HEIGHT, PATCH_WIDTH)
    analysed = analysed.transpose(2, 3, 0, 4, 1, 5)
    return analysed.reshape(PROGNOSTIC_VARS, MEMBER_COUNT, GRID_X, GRID_Y)
```

```python
import functools

import jax
import jax.numpy as jnp
from jax import lax
from jax.experimental import pallas as pl
from jax.experimental.pallas import tpu as pltpu
from jax.sharding import PartitionSpec as P

NEWTON = 8
LANES = 128
VMEM_LIMIT = 58 * 1024 * 1024
PACK_LIMIT = 58 * 1024 * 1024


def iota(shape, dim):
    return lax.broadcasted_iota(jnp.int32, shape, dim)


HEIGHT = 4
SPREAD = 32
PITCH = 8
OFFSETS = (
    (0, 0, 0),
    (0, 0, 1),
    (1, 0, 0),
    (0, 2, 0),
    (1, 0, 1),
    (0, 2, 1),
    (1, 1, 0),
    (0, 3, 0),
    (1, 1, 1),
    (0, 3, 1),
    (1, 3, 0),
    (0, 1, 0),
    (1, 3, 1),
    (0, 1, 1),
    (1, 2, 0),
    (1, 2, 1),
)
COUNT = len(OFFSETS)


def shifted(index, offset, sign=1):
    z, y, core = index // 8, index // 2 % 4, index % 2
    dz, dy, dc = offset
    return (z + dz) % 2 * 8 + (y + sign * dy + 4) % 4 * 2 + (core + dc) % 2


def pack_kernel(first, fields, rows, members, x_ref, cx_ref, cy_ref, df_ref, edge_ref, row_ref, corner_ref, held, sems):
    step = pl.program_id(0)
    pitch = rows + PITCH
    picked = (0, 1, rows - 2, rows - 1)
    groups = rows // SPREAD

    def copy(field):
        return pltpu.make_async_copy(
            x_ref.at[first + field], held.at[field, :, pl.ds(0, rows), :], sems.at[field]
        )

    @pl.when(step == 0)
    def _():
        for field in range(fields):
            copy(field).start()

    def gather(read, tall):
        lane = iota((tall, LANES), 1)
        packed = []
        for group in range(groups):
            parts = [jnp.zeros((tall, LANES), jnp.float32) for _ in range(4)]
            for i in range(SPREAD):
                moved = pltpu.roll(read(group * SPREAD + i), (4 * i + 2) % LANES, 1)
                parts[i % 4] = jnp.where(lane // 4 == i, moved, parts[i % 4])
            packed.append((parts[0] + parts[1]) + (parts[2] + parts[3]))
            edge_ref[0, group, 0:tall, :] = packed[group]
        corner_ref[0, 0:tall, :] = jnp.where(lane < LANES // 2, packed[0], packed[-1])

    for field in range(fields):

        @pl.when(step == field)
        def _():
            copy(field).wait()
            flat = held.at[field].reshape(members * pitch, LANES)

            def read(row):
                value = flat[pl.ds(row, members, stride=pitch), :]
                if row in picked:
                    row_ref[0, picked.index(row)] = value
                return value

            gather(read, members)

    @pl.when(step == fields)
    def _():
        sub = iota((8, LANES), 0)
        row_ref[0] = jnp.zeros((4, members, LANES), jnp.float32)
        edge_ref[0] = jnp.zeros((groups, members, LANES), jnp.float32)
        corner_ref[0] = jnp.zeros((members, LANES), jnp.float32)

        def read(row):
            at = slice(row, row + 1)
            value = jnp.where(
                sub == 0, cx_ref[at, :], jnp.where(sub == 1, cy_ref[at, :], df_ref[at, :])
            )
            if row in picked:
                row_ref[0, picked.index(row), 0:8, :] = value
            return value

        gather(read, 8)


def pack(x, coefficients, first, fields):
    _, members, rows, _ = x.shape
    small = pl.BlockSpec((rows, LANES), lambda i: (0, 0))
    groups = rows // SPREAD
    return pl.pallas_call(
        functools.partial(pack_kernel, first, fields, rows, members),
        grid=(fields + 1,),
        in_specs=[pl.BlockSpec(memory_space=pl.ANY), small, small, small],
        out_specs=[
            pl.BlockSpec((1, groups, members, LANES), lambda i: (i, 0, 0, 0)),
            pl.BlockSpec((1, 4, members, LANES), lambda i: (i, 0, 0, 0)),
            pl.BlockSpec((1, members, LANES), lambda i: (i, 0, 0)),
        ],
        out_shape=[
            jax.ShapeDtypeStruct((fields + 1, groups, members, LANES), jnp.float32),
            jax.ShapeDtypeStruct((fields + 1, 4, members, LANES), jnp.float32),
            jax.ShapeDtypeStruct((fields + 1, members, LANES), jnp.float32),
        ],
        scratch_shapes=[
            pltpu.VMEM((fields, members, rows + PITCH, LANES), jnp.float32),
            pltpu.SemaphoreType.DMA((fields,)),
        ],
        compiler_params=pltpu.CompilerParams(vmem_limit_bytes=PACK_LIMIT),
        cost_estimate=pl.CostEstimate(
            flops=fields * members * rows * LANES * 2,
            bytes_accessed=fields * members * rows * LANES * 8,
            transcendentals=0,
        ),
        name="pack_edges",
    )(x, *coefficients)


def exchange(packed):
    edge, row, corner = packed
    nx, ny = lax.axis_size("gx"), lax.axis_size("gy")
    right = [(i, (i + 1) % ny) for i in range(ny)]
    left = [(i, (i - 1) % ny) for i in range(ny)]

    def diagonal(step):
        return [
            (a * ny + b, ((a + 1) % nx) * ny + (b + step) % ny) for a in range(nx) for b in range(ny)
        ]

    return (
        lax.ppermute(row, "gx", [(i, (i + 1) % nx) for i in range(nx)]),
        lax.ppermute(edge, "gy", right),
        lax.ppermute(edge, "gy", left),
        lax.ppermute(corner, ("gx", "gy"), diagonal(1)),
        lax.ppermute(corner, ("gx", "gy"), diagonal(-1)),
    )


def weights_of(cx, cy, spread):
    plus_x, minus_x = jnp.maximum(cx, 0.0), jnp.minimum(cx, 0.0)
    plus_y, minus_y = jnp.maximum(cy, 0.0), jnp.minimum(cy, 0.0)
    centre = 1.0 - (plus_x - minus_x) - (plus_y - minus_y) - 4.0 * spread
    return centre, plus_x + spread, spread - minus_x, plus_y + spread, spread - minus_y


def stencil(k, centre, west, east, south, north):
    return k[0] * centre + k[1] * west + k[2] * east + k[3] * south + k[4] * north


def forecast_kernel(first, fields, rows, members, dest_ref, x_hbm, cx_ref, cy_ref, df_ref, own_ref, left_ref, right_ref, left_k_ref, right_k_ref, row_ref, row_k_ref, dl_ref, dr_ref, *refs):
    out_refs, (k_main, k_edge, k_row, edge_s, first_s, x_s, second_s, beside_s, held, sems) = refs[:COUNT], refs[COUNT:]
    step = pl.program_id(0)
    pitch = rows + PITCH

    def copy(field):
        slot = lax.rem(field, 2)
        return pltpu.make_async_copy(
            x_hbm.at[first + field], held.at[slot, :, pl.ds(0, rows), :], sems.at[slot]
        )

    @pl.when(step == 0)
    def _():
        copy(step).start()

    @pl.when(step + 1 < fields)
    def _():
        copy(step + 1).start()

    copy(step).wait()
    flat = held.at[lax.rem(step, 2)].reshape(members * pitch, LANES)
    for row in range(rows):
        x_s[row] = flat[pl.ds(row, members, stride=pitch), :]
    lane = iota((members, LANES), 1)
    from_left = lane % 4 < 2
    groups = rows // SPREAD

    @pl.when(pl.program_id(0) == 0)
    def _():
        for i, w in enumerate(weights_of(cx_ref[...], cy_ref[...], df_ref[...])):
            k_main[i] = w
        for group in range(groups):
            both = jnp.where(from_left[0:8], left_k_ref[0, group, 0:8, :], right_k_ref[0, group, 0:8, :])
            for i, w in enumerate(weights_of(*[both[j : j + 1, :] for j in range(3)])):
                k_edge[group, i : i + 1, :] = w
        for side, at in ((0, 3), (1, 0)):
            for i, w in enumerate(weights_of(*[row_k_ref[0, at, j : j + 1, :] for j in range(3)])):
                k_row[side, i : i + 1, :] = w

    edges = [jnp.where(from_left, left_ref[0, g], right_ref[0, g]) for g in range(groups)]
    corner = jnp.where(from_left, dl_ref[0], dr_ref[0])
    chain = [corner] + edges + [corner]
    up = [pltpu.roll(v, 4, 1) for v in chain]
    down = [pltpu.roll(v, LANES - 4, 1) for v in chain]
    for group, edge in enumerate(edges):
        own = own_ref[0, group]
        edge_s[0, group] = edge
        edge_s[1, group] = stencil(
            [k_edge[group, i : i + 1, :] for i in range(5)],
            edge,
            jnp.where(lane < 4, up[group], up[group + 1]),
            jnp.where(lane >= LANES - 4, down[group + 2], down[group + 1]),
            pltpu.roll(jnp.where(lane % 4 == 0, edge, own), 1, 1),
            pltpu.roll(jnp.where(lane % 4 == 3, edge, own), LANES - 1, 1),
        )

    def sides(centre, beside):
        return (
            pltpu.roll(jnp.where(lane == LANES - 1, beside, centre), 1, 1),
            pltpu.roll(jnp.where(lane == 0, beside, centre), LANES - 1, 1),
        )

    for side, (centre, west, east, turn, at) in enumerate(
        (
            (row_ref[0, 3], row_ref[0, 2], x_s[0], 2, 0),
            (row_ref[0, 0], x_s[rows - 1], row_ref[0, 1], LANES - 2, rows + 1),
        )
    ):
        k = [k_row[side, i : i + 1, :] for i in range(5)]
        first_s[at] = stencil(k, centre, west, east, *sides(centre, pltpu.roll(corner, turn, 1)))

    def lay_sides(stage):
        for row in range(rows):
            turn = (126 - row % SPREAD * 4) % LANES
            beside_s[row] = pltpu.roll(edge_s[stage, row // SPREAD], turn, 1)

    def one(row, centre, west, east):
        k = [k_main[i, row : row + 1, :] for i in range(5)]
        return stencil(k, centre, west, east, *sides(centre, beside_s[row]))

    lay_sides(0)
    for row in range(rows):
        west = row_ref[0, 3] if row == 0 else x_s[row - 1]
        east = row_ref[0, 0] if row == rows - 1 else x_s[row + 1]
        first_s[row + 1] = one(row, x_s[row], west, east)
    lay_sides(1)
    for row in range(rows):
        second_s[row] = one(row, first_s[row + 1], first_s[row], first_s[row + 2])
    for i in range(COUNT):
        base = dest_ref[i] * HEIGHT
        for r in range(HEIGHT):
            out_refs[i][0, r * members : (r + 1) * members, :] = second_s[base + r]


def forecast(x, coefficients, edge, moved, moved_k, dest, first, fields):
    _, members, rows, _ = x.shape
    row, left, right, corner_l, corner_r = moved
    row_k, left_k, right_k = moved_k
    last = row_k.shape[0] - 1
    groups = rows // SPREAD
    small = pl.BlockSpec((rows, LANES), lambda i: (0, 0))
    edge_spec = pl.BlockSpec((1, groups, members, LANES), lambda i: (i, 0, 0, 0))
    edge_last = pl.BlockSpec((1, groups, members, LANES), lambda i: (last, 0, 0, 0))
    corner_spec = pl.BlockSpec((1, members, LANES), lambda i: (i, 0, 0))
    piece = HEIGHT * members
    return pl.pallas_call(
        functools.partial(forecast_kernel, first, fields, rows, members),
        grid=(fields,),
        in_specs=[
            pl.BlockSpec(memory_space=pltpu.SMEM),
            pl.BlockSpec(memory_space=pl.ANY),
            small,
            small,
            small,
            edge_spec,
            edge_spec,
            edge_spec,
            edge_last,
            edge_last,
            pl.BlockSpec((1, 4, members, LANES), lambda i: (i, 0, 0, 0)),
            pl.BlockSpec((1, 4, members, LANES), lambda i: (last, 0, 0, 0)),
            corner_spec,
            corner_spec,
        ],
        out_specs=[pl.BlockSpec((1, piece, LANES), lambda i: (i, 0, 0))] * COUNT,
        out_shape=[jax.ShapeDtypeStruct((fields, piece, LANES), jnp.float32)] * COUNT,
        scratch_shapes=[
            pltpu.VMEM((5, rows, LANES), jnp.float32),
            pltpu.VMEM((groups, 8, LANES), jnp.float32),
            pltpu.VMEM((2, 8, LANES), jnp.float32),
            pltpu.VMEM((2, groups, members, LANES), jnp.float32),
            pltpu.VMEM((rows + 2, members, LANES), jnp.float32),
            pltpu.VMEM((rows, members, LANES), jnp.float32),
            pltpu.VMEM((rows, members, LANES), jnp.float32),
            pltpu.VMEM((rows, members, LANES), jnp.float32),
            pltpu.VMEM((2, members, rows + PITCH, LANES), jnp.float32),
            pltpu.SemaphoreType.DMA((2,)),
        ],
        compiler_params=pltpu.CompilerParams(vmem_limit_bytes=PACK_LIMIT),
        cost_estimate=pl.CostEstimate(
            flops=fields * rows * members * LANES * 18,
            bytes_accessed=fields * rows * members * LANES * 8,
            transcendentals=0,
        ),
        name="forecast",
    )(dest, x, *coefficients, edge, left, right, left_k, right_k, row, row_k, corner_l, corner_r)


def halves(value):
    high = value.astype(jnp.bfloat16)
    return high, (value - high.astype(jnp.float32)).astype(jnp.bfloat16)


def dot(a, b):
    return jnp.dot(a, b, preferred_element_type=jnp.float32)


def tile_rows(refs, r):
    tall = refs[0].shape[1] // HEIGHT
    return jnp.concatenate([ref[0, r * tall : (r + 1) * tall, :] for ref in refs], axis=0)


def sample_kernel(place_ref, *refs):
    step = pl.program_id(0)
    x_refs, out_ref = refs[:COUNT], refs[COUNT]
    slots = place_ref.shape[1]
    cells = HEIGHT * LANES
    x = jnp.concatenate([tile_rows(x_refs, r) for r in range(HEIGHT)], axis=1)
    chosen = (iota((cells, slots), 0) + step * cells == place_ref[0:1, :]).astype(jnp.bfloat16)
    high = x.astype(jnp.bfloat16)
    middle, low = halves(x - high.astype(jnp.float32))
    got = dot(high, chosen) + dot(middle, chosen) + dot(low, chosen)

    @pl.when(step == 0)
    def _():
        out_ref[...] = got

    @pl.when(step > 0)
    def _():
        out_ref[...] += got


def sample(pieces, place):
    fields, piece, _ = pieces[0].shape
    members = COUNT * piece // HEIGHT
    slots = place.shape[1]
    return pl.pallas_call(
        sample_kernel,
        grid=(fields,),
        in_specs=[pl.BlockSpec((1, slots), lambda i: (0, 0))]
        + [pl.BlockSpec((1, piece, LANES), lambda i: (i, 0, 0))] * COUNT,
        out_specs=pl.BlockSpec((members, slots), lambda i: (0, 0)),
        out_shape=jax.ShapeDtypeStruct((members, slots), jnp.float32),
        compiler_params=pltpu.CompilerParams(vmem_limit_bytes=VMEM_LIMIT),
        cost_estimate=pl.CostEstimate(
            flops=fields * members * HEIGHT * LANES * slots * 6,
            bytes_accessed=fields * members * HEIGHT * LANES * 4,
            transcendentals=0,
        ),
        name="sample",
    )(place, *pieces)


def transform_kernel(mix_ref, *refs):
    x_refs, out_refs, (high_s, low_s) = refs[:COUNT], refs[COUNT : 2 * COUNT], refs[2 * COUNT :]

    @pl.when(pl.program_id(0) == 0)
    def _():
        high_s[...], low_s[...] = halves(mix_ref[...])

    tall = x_refs[0].shape[1] // HEIGHT
    members = COUNT * tall
    for half in range(HEIGHT // 2):
        x = jnp.concatenate([tile_rows(x_refs, 2 * half + i) for i in range(2)], axis=1)
        centre = jnp.sum(x, axis=0, keepdims=True) / members
        high, low = halves(x - centre)
        result = dot(high_s[...], high) + (dot(high_s[...], low) + dot(low_s[...], high)) + centre
        for i in range(2):
            at = (2 * half + i) * tall
            for o in range(COUNT):
                out_refs[o][0, at : at + tall, :] = result[
                    o * tall : (o + 1) * tall, i * LANES : (i + 1) * LANES
                ]


def transform(pieces, mixing_t):
    fields, piece, _ = pieces[0].shape
    members = mixing_t.shape[0]
    block = pl.BlockSpec((1, piece, LANES), lambda i: (i, 0, 0))
    return pl.pallas_call(
        transform_kernel,
        grid=(fields,),
        in_specs=[pl.BlockSpec((members, members), lambda i: (0, 0))] + [block] * COUNT,
        out_specs=[block] * COUNT,
        out_shape=[jax.ShapeDtypeStruct(pieces[0].shape, jnp.float32)] * COUNT,
        scratch_shapes=[
            pltpu.VMEM((members, members), jnp.bfloat16),
            pltpu.VMEM((members, members), jnp.bfloat16),
        ],
        compiler_params=pltpu.CompilerParams(vmem_limit_bytes=VMEM_LIMIT),
        cost_estimate=pl.CostEstimate(
            flops=fields * members * members * HEIGHT * LANES * 6,
            bytes_accessed=fields * members * HEIGHT * LANES * 8,
            transcendentals=0,
        ),
        name="transform",
    )(mixing_t, *pieces)


def unpack_kernel(members, rows, dest_ref, *refs):
    x_refs, out_ref, held = refs[:COUNT], refs[-2], refs[-1]
    pitch = rows + 4
    for i in range(COUNT):
        base = dest_ref[i] * HEIGHT
        for r in range(HEIGHT):
            held[pl.ds(base + r, members, stride=pitch), :] = x_refs[i][0, r * members : (r + 1) * members, :]
    for m in range(members):
        out_ref[0, m * rows : (m + 1) * rows, :] = held[m * pitch : m * pitch + rows, :]


def unpack(pieces, so_far, dest, first, total, members, rows):
    fields, piece, _ = pieces[0].shape
    flat = members * rows
    more = () if so_far is None else (so_far,)
    return pl.pallas_call(
        functools.partial(unpack_kernel, members, rows),
        grid=(fields,),
        in_specs=[pl.BlockSpec(memory_space=pltpu.SMEM)]
        + [pl.BlockSpec((1, piece, LANES), lambda i: (i, 0, 0))] * COUNT
        + [pl.BlockSpec(memory_space=pl.ANY) for _ in more],
        out_specs=pl.BlockSpec((1, flat, LANES), lambda i: (first + i, 0, 0)),
        out_shape=jax.ShapeDtypeStruct((total, flat, LANES), jnp.float32),
        scratch_shapes=[pltpu.VMEM((members * (rows + 4), LANES), jnp.float32)],
        input_output_aliases={COUNT + 1: 0} if more else {},
        compiler_params=pltpu.CompilerParams(vmem_limit_bytes=VMEM_LIMIT),
        cost_estimate=pl.CostEstimate(
            flops=0, bytes_accessed=fields * flat * LANES * 8, transcendentals=0
        ),
        name="unpack",
    )(dest, *pieces, *more)


def swap(pieces, sign):
    return [
        p
        if not any(o)
        else lax.ppermute(p, "mem", [(i, shifted(i, o, sign)) for i in range(COUNT)])
        for p, o in zip(pieces, OFFSETS)
    ]


def mixing_transposed(raw_values, report_value, report_precision, report_class, slot_count):
    members, slots = raw_values.shape
    exact = lax.Precision.HIGH
    centre_obs = jnp.sum(raw_values, axis=0) / members
    observed = raw_values - centre_obs
    innovation = report_value - centre_obs
    usable = (jnp.arange(slots) < slot_count).astype(jnp.float32)
    weight = usable * report_precision / (1.0 + report_class.astype(jnp.float32))
    identity = jnp.eye(members, dtype=jnp.float32)
    gram_matrix = (
        jnp.dot(observed * weight, observed.T, precision=lax.Precision.HIGHEST)
        + (members - 1.0) * identity
    )
    norm_scale = jnp.sqrt(jnp.sum(gram_matrix * gram_matrix))
    root_y = gram_matrix / norm_scale
    root_z = identity
    for iteration in range(NEWTON):
        if iteration == 0:
            factor = 1.5 * identity - 0.5 * root_y
            new_z = factor
        else:
            factor = 1.5 * identity - 0.5 * jnp.dot(root_z, root_y, precision=exact)
            new_z = jnp.dot(factor, root_z, precision=exact)
        if iteration + 1 < NEWTON:
            root_y = jnp.dot(root_y, factor, precision=exact)
        root_z = new_z
    driven = jnp.dot(observed, weight * innovation, precision=lax.Precision.HIGHEST)
    inner = jnp.dot(root_z, driven, precision=lax.Precision.HIGHEST)
    mean_shift = jnp.dot(root_z, inner, precision=lax.Precision.HIGHEST) / norm_scale
    return jnp.sqrt((members - 1.0) / norm_scale) * root_z.T + mean_shift[None, :]


def own_row(table, tile):
    flat_table = table.reshape((table.shape[0] * table.shape[1],) + table.shape[2:])
    return lax.dynamic_index_in_dim(flat_table, tile, 0, keepdims=False)


def on_device(
    prior_members,
    courant_x,
    courant_y,
    diffusion,
    report_level,
    report_cell,
    report_value,
    report_precision,
    report_class,
    report_count,
):
    total, members, rows, _ = prior_members.shape
    coefficients = (courant_x, courant_y, diffusion)
    tile = lax.axis_index("mem")
    dest = jnp.stack([shifted(tile, o) for o in OFFSETS]).astype(jnp.int32)
    half = total // 2

    packed = [pack(prior_members, coefficients, first, half) for first in (0, half)]
    moved = [exchange(p) for p in packed]
    sent = [
        forecast(prior_members, coefficients, packed[i][0], moved[i], moved[0][:3], dest, i * half, half)
        for i in range(2)
    ]
    gathered = [swap(s, 1) for s in sent]

    level, cell = own_row(report_level, tile), own_row(report_cell, tile)
    place = (level * (HEIGHT * LANES) + cell)[None, :]
    mixing_t = mixing_transposed(
        sample(gathered[0], place),
        own_row(report_value, tile),
        own_row(report_precision, tile),
        own_row(report_class, tile),
        own_row(report_count, tile),
    )
    returned = [swap(transform(g, mixing_t), -1) for g in gathered]
    result = unpack(returned[0], None, dest, 0, total, members, rows)
    result = unpack(returned[1], result, dest, half, total, members, rows)
    return result.reshape(prior_members.shape)


def solution(mesh):
    in_specs = (
        P(None, "mem", "gx", "gy"),
        P("gx", "gy"),
        P("gx", "gy"),
        P("gx", "gy"),
        P("gx", "gy", None),
        P("gx", "gy", None),
        P("gx", "gy", None),
        P("gx", "gy", None),
        P("gx", "gy", None),
        P("gx", "gy"),
    )
    out_specs = P(None, "mem", "gx", "gy")
    return jax.shard_map(
        on_device, mesh=mesh, in_specs=in_specs, out_specs=out_specs, check_vma=False
    )
```

```python
import functools

import jax
import jax.numpy as jnp
from jax import lax
from jax.experimental import pallas as pl
from jax.experimental.pallas import tpu as pltpu
from jax.sharding import PartitionSpec as P

NEWTON = 8
LANES = 128
VMEM_LIMIT = 58 * 1024 * 1024
PACK_LIMIT = 58 * 1024 * 1024


def iota(shape, dim):
    return lax.broadcasted_iota(jnp.int32, shape, dim)


HEIGHT = 4
SPREAD = 32
PITCH = 8
OFFSETS = (
    (0, 0, 0),
    (0, 0, 1),
    (1, 0, 0),
    (0, 2, 0),
    (1, 0, 1),
    (0, 2, 1),
    (1, 1, 0),
    (0, 3, 0),
    (1, 1, 1),
    (0, 3, 1),
    (1, 3, 0),
    (0, 1, 0),
    (1, 3, 1),
    (0, 1, 1),
    (1, 2, 0),
    (1, 2, 1),
)
COUNT = len(OFFSETS)
EARLY, LATE = 6, 12


def shifted(index, offset, sign=1):
    z, y, core = index // 8, index // 2 % 4, index % 2
    dz, dy, dc = offset
    return (z + dz) % 2 * 8 + (y + sign * dy + 4) % 4 * 2 + (core + dc) % 2


def pack_kernel(first, fields, rows, members, x_ref, cx_ref, cy_ref, df_ref, *refs):
    edge_ref, row_ref, corner_ref, held, sems = refs[-5:]
    step = pl.program_id(0)
    pitch = rows + PITCH
    picked = (0, 1, rows - 2, rows - 1)
    groups = rows // SPREAD

    def copy(field):
        return pltpu.make_async_copy(
            x_ref.at[first + field], held.at[field, :, pl.ds(0, rows), :], sems.at[field]
        )

    @pl.when(step == 0)
    def _():
        for field in range(fields):
            copy(field).start()

    def gather(read, tall):
        lane = iota((tall, LANES), 1)
        packed = []
        for group in range(groups):
            parts = [jnp.zeros((tall, LANES), jnp.float32) for _ in range(4)]
            for i in range(SPREAD):
                moved = pltpu.roll(read(group * SPREAD + i), (4 * i + 2) % LANES, 1)
                parts[i % 4] = jnp.where(lane // 4 == i, moved, parts[i % 4])
            packed.append((parts[0] + parts[1]) + (parts[2] + parts[3]))
            edge_ref[0, group, 0:tall, :] = packed[group]
        corner_ref[0, 0:tall, :] = jnp.where(lane < LANES // 2, packed[0], packed[-1])

    for field in range(fields):

        @pl.when(step == field)
        def _():
            copy(field).wait()
            flat = held.at[field].reshape(members * pitch, LANES)

            def read(row):
                value = flat[pl.ds(row, members, stride=pitch), :]
                if row in picked:
                    row_ref[0, picked.index(row)] = value
                return value

            gather(read, members)

    @pl.when(step == fields)
    def _():
        sub = iota((8, LANES), 0)
        row_ref[0] = jnp.zeros((4, members, LANES), jnp.float32)
        edge_ref[0] = jnp.zeros((groups, members, LANES), jnp.float32)
        corner_ref[0] = jnp.zeros((members, LANES), jnp.float32)

        def read(row):
            at = slice(row, row + 1)
            value = jnp.where(
                sub == 0, cx_ref[at, :], jnp.where(sub == 1, cy_ref[at, :], df_ref[at, :])
            )
            if row in picked:
                row_ref[0, picked.index(row), 0:8, :] = value
            return value

        gather(read, 8)


def pack(x, coefficients, first, fields, after=()):
    _, members, rows, _ = x.shape
    small = pl.BlockSpec((rows, LANES), lambda i: (0, 0))
    groups = rows // SPREAD
    return pl.pallas_call(
        functools.partial(pack_kernel, first, fields, rows, members),
        grid=(fields + 1,),
        in_specs=[pl.BlockSpec(memory_space=pl.ANY), small, small, small]
        + [pl.BlockSpec(memory_space=pl.ANY) for _ in after],
        out_specs=[
            pl.BlockSpec((1, groups, members, LANES), lambda i: (i, 0, 0, 0)),
            pl.BlockSpec((1, 4, members, LANES), lambda i: (i, 0, 0, 0)),
            pl.BlockSpec((1, members, LANES), lambda i: (i, 0, 0)),
        ],
        out_shape=[
            jax.ShapeDtypeStruct((fields + 1, groups, members, LANES), jnp.float32),
            jax.ShapeDtypeStruct((fields + 1, 4, members, LANES), jnp.float32),
            jax.ShapeDtypeStruct((fields + 1, members, LANES), jnp.float32),
        ],
        scratch_shapes=[
            pltpu.VMEM((fields, members, rows + PITCH, LANES), jnp.float32),
            pltpu.SemaphoreType.DMA((fields,)),
        ],
        compiler_params=pltpu.CompilerParams(vmem_limit_bytes=PACK_LIMIT),
        cost_estimate=pl.CostEstimate(
            flops=fields * members * rows * LANES * 2,
            bytes_accessed=fields * members * rows * LANES * 8,
            transcendentals=0,
        ),
        name="pack_edges",
    )(x, *coefficients, *after)


def exchange(packed):
    edge, row, corner = packed
    nx, ny = lax.axis_size("gx"), lax.axis_size("gy")
    right = [(i, (i + 1) % ny) for i in range(ny)]
    left = [(i, (i - 1) % ny) for i in range(ny)]

    def diagonal(step):
        return [
            (a * ny + b, ((a + 1) % nx) * ny + (b + step) % ny) for a in range(nx) for b in range(ny)
        ]

    return (
        lax.ppermute(row, "gx", [(i, (i + 1) % nx) for i in range(nx)]),
        lax.ppermute(edge, "gy", right),
        lax.ppermute(edge, "gy", left),
        lax.ppermute(corner, ("gx", "gy"), diagonal(1)),
        lax.ppermute(corner, ("gx", "gy"), diagonal(-1)),
    )


def weights_of(cx, cy, spread):
    plus_x, minus_x = jnp.maximum(cx, 0.0), jnp.minimum(cx, 0.0)
    plus_y, minus_y = jnp.maximum(cy, 0.0), jnp.minimum(cy, 0.0)
    centre = 1.0 - (plus_x - minus_x) - (plus_y - minus_y) - 4.0 * spread
    return centre, plus_x + spread, spread - minus_x, plus_y + spread, spread - minus_y


def stencil(k, centre, west, east, south, north):
    return k[0] * centre + k[1] * west + k[2] * east + k[3] * south + k[4] * north


def forecast_kernel(first, fields, rows, members, dest_ref, x_hbm, cx_ref, cy_ref, df_ref, own_ref, left_ref, right_ref, left_k_ref, right_k_ref, row_ref, row_k_ref, dl_ref, dr_ref, *refs):
    out_refs, (k_main, k_edge, k_row, edge_s, first_s, x_s, second_s, beside_s, held, sems) = refs[:COUNT], refs[COUNT:]
    step = pl.program_id(0)
    pitch = rows + PITCH

    def copy(field):
        slot = lax.rem(field, 2)
        return pltpu.make_async_copy(
            x_hbm.at[first + field], held.at[slot, :, pl.ds(0, rows), :], sems.at[slot]
        )

    @pl.when(step == 0)
    def _():
        copy(step).start()

    @pl.when(step + 1 < fields)
    def _():
        copy(step + 1).start()

    copy(step).wait()
    flat = held.at[lax.rem(step, 2)].reshape(members * pitch, LANES)
    for row in range(rows):
        x_s[row] = flat[pl.ds(row, members, stride=pitch), :]
    lane = iota((members, LANES), 1)
    from_left = lane % 4 < 2
    groups = rows // SPREAD

    @pl.when(pl.program_id(0) == 0)
    def _():
        for i, w in enumerate(weights_of(cx_ref[...], cy_ref[...], df_ref[...])):
            k_main[i] = w
        for group in range(groups):
            both = jnp.where(from_left[0:8], left_k_ref[0, group, 0:8, :], right_k_ref[0, group, 0:8, :])
            for i, w in enumerate(weights_of(*[both[j : j + 1, :] for j in range(3)])):
                k_edge[group, i : i + 1, :] = w
        for side, at in ((0, 3), (1, 0)):
            for i, w in enumerate(weights_of(*[row_k_ref[0, at, j : j + 1, :] for j in range(3)])):
                k_row[side, i : i + 1, :] = w

    edges = [jnp.where(from_left, left_ref[0, g], right_ref[0, g]) for g in range(groups)]
    corner = jnp.where(from_left, dl_ref[0], dr_ref[0])
    chain = [corner] + edges + [corner]
    up = [pltpu.roll(v, 4, 1) for v in chain]
    down = [pltpu.roll(v, LANES - 4, 1) for v in chain]
    for group, edge in enumerate(edges):
        own = own_ref[0, group]
        edge_s[0, group] = edge
        edge_s[1, group] = stencil(
            [k_edge[group, i : i + 1, :] for i in range(5)],
            edge,
            jnp.where(lane < 4, up[group], up[group + 1]),
            jnp.where(lane >= LANES - 4, down[group + 2], down[group + 1]),
            pltpu.roll(jnp.where(lane % 4 == 0, edge, own), 1, 1),
            pltpu.roll(jnp.where(lane % 4 == 3, edge, own), LANES - 1, 1),
        )

    def sides(centre, beside):
        return (
            pltpu.roll(jnp.where(lane == LANES - 1, beside, centre), 1, 1),
            pltpu.roll(jnp.where(lane == 0, beside, centre), LANES - 1, 1),
        )

    for side, (centre, west, east, turn, at) in enumerate(
        (
            (row_ref[0, 3], row_ref[0, 2], x_s[0], 2, 0),
            (row_ref[0, 0], x_s[rows - 1], row_ref[0, 1], LANES - 2, rows + 1),
        )
    ):
        k = [k_row[side, i : i + 1, :] for i in range(5)]
        first_s[at] = stencil(k, centre, west, east, *sides(centre, pltpu.roll(corner, turn, 1)))

    def lay_sides(stage):
        for row in range(rows):
            turn = (126 - row % SPREAD * 4) % LANES
            beside_s[row] = pltpu.roll(edge_s[stage, row // SPREAD], turn, 1)

    def one(row, centre, west, east):
        k = [k_main[i, row : row + 1, :] for i in range(5)]
        return stencil(k, centre, west, east, *sides(centre, beside_s[row]))

    lay_sides(0)
    for row in range(rows):
        west = row_ref[0, 3] if row == 0 else x_s[row - 1]
        east = row_ref[0, 0] if row == rows - 1 else x_s[row + 1]
        first_s[row + 1] = one(row, x_s[row], west, east)
    lay_sides(1)
    for row in range(rows):
        second_s[row] = one(row, first_s[row + 1], first_s[row], first_s[row + 2])
    for i in range(COUNT):
        base = dest_ref[i] * HEIGHT
        for r in range(HEIGHT):
            out_refs[i][0, r * members : (r + 1) * members, :] = second_s[base + r]


def forecast(x, coefficients, edge, moved, moved_k, dest, first, fields):
    _, members, rows, _ = x.shape
    row, left, right, corner_l, corner_r = moved
    row_k, left_k, right_k = moved_k
    last = row_k.shape[0] - 1
    groups = rows // SPREAD
    small = pl.BlockSpec((rows, LANES), lambda i: (0, 0))
    edge_spec = pl.BlockSpec((1, groups, members, LANES), lambda i: (i, 0, 0, 0))
    edge_last = pl.BlockSpec((1, groups, members, LANES), lambda i: (last, 0, 0, 0))
    corner_spec = pl.BlockSpec((1, members, LANES), lambda i: (i, 0, 0))
    piece = HEIGHT * members
    return pl.pallas_call(
        functools.partial(forecast_kernel, first, fields, rows, members),
        grid=(fields,),
        in_specs=[
            pl.BlockSpec(memory_space=pltpu.SMEM),
            pl.BlockSpec(memory_space=pl.ANY),
            small,
            small,
            small,
            edge_spec,
            edge_spec,
            edge_spec,
            edge_last,
            edge_last,
            pl.BlockSpec((1, 4, members, LANES), lambda i: (i, 0, 0, 0)),
            pl.BlockSpec((1, 4, members, LANES), lambda i: (last, 0, 0, 0)),
            corner_spec,
            corner_spec,
        ],
        out_specs=[pl.BlockSpec((1, piece, LANES), lambda i: (i, 0, 0))] * COUNT,
        out_shape=[jax.ShapeDtypeStruct((fields, piece, LANES), jnp.float32)] * COUNT,
        scratch_shapes=[
            pltpu.VMEM((5, rows, LANES), jnp.float32),
            pltpu.VMEM((groups, 8, LANES), jnp.float32),
            pltpu.VMEM((2, 8, LANES), jnp.float32),
            pltpu.VMEM((2, groups, members, LANES), jnp.float32),
            pltpu.VMEM((rows + 2, members, LANES), jnp.float32),
            pltpu.VMEM((rows, members, LANES), jnp.float32),
            pltpu.VMEM((rows, members, LANES), jnp.float32),
            pltpu.VMEM((rows, members, LANES), jnp.float32),
            pltpu.VMEM((2, members, rows + PITCH, LANES), jnp.float32),
            pltpu.SemaphoreType.DMA((2,)),
        ],
        compiler_params=pltpu.CompilerParams(vmem_limit_bytes=PACK_LIMIT),
        cost_estimate=pl.CostEstimate(
            flops=fields * rows * members * LANES * 18,
            bytes_accessed=fields * rows * members * LANES * 8,
            transcendentals=0,
        ),
        name="forecast",
    )(dest, x, *coefficients, edge, left, right, left_k, right_k, row, row_k, corner_l, corner_r)


def halves(value):
    high = value.astype(jnp.bfloat16)
    return high, (value - high.astype(jnp.float32)).astype(jnp.bfloat16)


def dot(a, b):
    return jnp.dot(a, b, preferred_element_type=jnp.float32)


def tile_rows(refs, r):
    tall = refs[0].shape[1] // HEIGHT
    return jnp.concatenate([ref[0, r * tall : (r + 1) * tall, :] for ref in refs], axis=0)


def sample_kernel(place_ref, *refs):
    step = pl.program_id(0)
    x_refs, out_ref = refs[:COUNT], refs[-1]
    slots = place_ref.shape[1]
    cells = HEIGHT * LANES
    x = jnp.concatenate([tile_rows(x_refs, r) for r in range(HEIGHT)], axis=1)
    chosen = (iota((cells, slots), 0) + step * cells == place_ref[0:1, :]).astype(jnp.bfloat16)
    high = x.astype(jnp.bfloat16)
    middle, low = halves(x - high.astype(jnp.float32))
    got = dot(high, chosen) + dot(middle, chosen) + dot(low, chosen)

    @pl.when(step == 0)
    def _():
        out_ref[...] = got

    @pl.when(step > 0)
    def _():
        out_ref[...] += got


def sample(pieces, place, after):
    fields, piece, _ = pieces[0].shape
    members = COUNT * piece // HEIGHT
    slots = place.shape[1]
    return pl.pallas_call(
        sample_kernel,
        grid=(fields,),
        in_specs=[pl.BlockSpec((1, slots), lambda i: (0, 0))]
        + [pl.BlockSpec((1, piece, LANES), lambda i: (i, 0, 0))] * COUNT
        + [pl.BlockSpec(memory_space=pl.ANY) for _ in after],
        out_specs=pl.BlockSpec((members, slots), lambda i: (0, 0)),
        out_shape=jax.ShapeDtypeStruct((members, slots), jnp.float32),
        compiler_params=pltpu.CompilerParams(vmem_limit_bytes=VMEM_LIMIT),
        cost_estimate=pl.CostEstimate(
            flops=fields * members * HEIGHT * LANES * slots * 6,
            bytes_accessed=fields * members * HEIGHT * LANES * 4,
            transcendentals=0,
        ),
        name="sample",
    )(place, *pieces, *after)


def transform_kernel(mix_ref, *refs):
    x_refs, out_refs, (high_s, low_s) = refs[:COUNT], refs[COUNT : 2 * COUNT], refs[2 * COUNT :]

    @pl.when(pl.program_id(0) == 0)
    def _():
        high_s[...], low_s[...] = halves(mix_ref[...])

    tall = x_refs[0].shape[1] // HEIGHT
    members = COUNT * tall
    for half in range(HEIGHT // 2):
        x = jnp.concatenate([tile_rows(x_refs, 2 * half + i) for i in range(2)], axis=1)
        centre = jnp.sum(x, axis=0, keepdims=True) / members
        high, low = halves(x - centre)
        result = dot(high_s[...], high) + (dot(high_s[...], low) + dot(low_s[...], high)) + centre
        for i in range(2):
            at = (2 * half + i) * tall
            for o in range(COUNT):
                out_refs[o][0, at : at + tall, :] = result[
                    o * tall : (o + 1) * tall, i * LANES : (i + 1) * LANES
                ]


def transform(pieces, mixing_t):
    fields, piece, _ = pieces[0].shape
    members = mixing_t.shape[0]
    block = pl.BlockSpec((1, piece, LANES), lambda i: (i, 0, 0))
    return pl.pallas_call(
        transform_kernel,
        grid=(fields,),
        in_specs=[pl.BlockSpec((members, members), lambda i: (0, 0))] + [block] * COUNT,
        out_specs=[block] * COUNT,
        out_shape=[jax.ShapeDtypeStruct(pieces[0].shape, jnp.float32)] * COUNT,
        scratch_shapes=[
            pltpu.VMEM((members, members), jnp.bfloat16),
            pltpu.VMEM((members, members), jnp.bfloat16),
        ],
        compiler_params=pltpu.CompilerParams(vmem_limit_bytes=VMEM_LIMIT),
        cost_estimate=pl.CostEstimate(
            flops=fields * members * members * HEIGHT * LANES * 6,
            bytes_accessed=fields * members * HEIGHT * LANES * 8,
            transcendentals=0,
        ),
        name="transform",
    )(mixing_t, *pieces)


def unpack_kernel(members, rows, dest_ref, *refs):
    x_refs, out_ref, held = refs[:COUNT], refs[-2], refs[-1]
    pitch = rows + 4
    for i in range(COUNT):
        base = dest_ref[i] * HEIGHT
        for r in range(HEIGHT):
            held[pl.ds(base + r, members, stride=pitch), :] = x_refs[i][0, r * members : (r + 1) * members, :]
    for m in range(members):
        out_ref[0, m * rows : (m + 1) * rows, :] = held[m * pitch : m * pitch + rows, :]


def unpack(pieces, so_far, dest, first, total, members, rows):
    fields, piece, _ = pieces[0].shape
    flat = members * rows
    more = () if so_far is None else (so_far,)
    return pl.pallas_call(
        functools.partial(unpack_kernel, members, rows),
        grid=(fields,),
        in_specs=[pl.BlockSpec(memory_space=pltpu.SMEM)]
        + [pl.BlockSpec((1, piece, LANES), lambda i: (i, 0, 0))] * COUNT
        + [pl.BlockSpec(memory_space=pl.ANY) for _ in more],
        out_specs=pl.BlockSpec((1, flat, LANES), lambda i: (first + i, 0, 0)),
        out_shape=jax.ShapeDtypeStruct((total, flat, LANES), jnp.float32),
        scratch_shapes=[pltpu.VMEM((members * (rows + 4), LANES), jnp.float32)],
        input_output_aliases={COUNT + 1: 0} if more else {},
        compiler_params=pltpu.CompilerParams(vmem_limit_bytes=VMEM_LIMIT),
        cost_estimate=pl.CostEstimate(
            flops=0, bytes_accessed=fields * flat * LANES * 8, transcendentals=0
        ),
        name="unpack",
    )(dest, *pieces, *more)


def swap(pieces, sign, skip=0):
    return [
        p
        if not any(o)
        else lax.ppermute(p, "mem", [(i, shifted(i, o, sign)) for i in range(COUNT)])
        for p, o in zip(pieces, OFFSETS[skip:])
    ]


def dot3(a, b, dims=(1, 0)):
    (ah, al), (bh, bl) = halves(a), halves(b)

    def one(u, v):
        return lax.dot_general(
            u, v, (((dims[0],), (dims[1],)), ((), ())), preferred_element_type=jnp.float32
        )

    return one(ah, bh) + (one(ah, bl) + one(al, bh))


def mixing_kernel(count_ref, raw_ref, value_ref, precision_ref, class_ref, out_ref):
    members, slots = raw_ref.shape
    raw = raw_ref[...]
    centre_obs = jnp.sum(raw, axis=0, keepdims=True) / members
    usable = iota((1, slots), 1) < count_ref[0]
    weight = jnp.where(usable, precision_ref[...] / (1.0 + class_ref[...].astype(jnp.float32)), 0.0)
    root_weight = jnp.sqrt(weight)
    spread = (raw - centre_obs) * root_weight
    small = dot3(spread, spread, (0, 0))
    inflation = members - 1.0
    scale = jnp.sqrt(
        inflation * inflation * members
        + 2.0 * inflation * jnp.sum(spread * spread, keepdims=True)
        + jnp.sum(small * small, keepdims=True)
    )
    eye = (iota((slots, slots), 0) == iota((slots, slots), 1)).astype(jnp.float32)
    start = inflation / scale
    y, z = start, jnp.ones_like(start)
    root_y = start * eye + small / scale
    factor = 1.5 * eye - 0.5 * root_y
    p = 1.5 - 0.5 * y
    root_z, part_z, z = factor, -0.5 * eye, p
    root_y, y = dot3(root_y, factor), y * p
    for iteration in range(1, NEWTON):
        both = dot3(jnp.concatenate([root_z, part_z], axis=0), root_y)
        part = z * (start * part_z + root_z) + both[slots:]
        factor = 1.5 * eye - 0.5 * both[:slots]
        p = 1.5 - 0.5 * z * y
        both = dot3(jnp.concatenate([factor, -0.5 * part], axis=0), root_z)
        if iteration + 1 < NEWTON:
            root_y, y = dot3(root_y, factor), y * p
        root_z, part_z, z = both[:slots], p * part_z + both[slots:], z * p
    driven = jnp.broadcast_to(root_weight * (value_ref[...] - centre_obs), (8, slots))
    driven = dot3(dot3(driven, root_z), root_z)
    shift = dot3(driven, spread, (1, 1))[0:1] / scale
    gain = jnp.sqrt(inflation / scale)
    low_rank = dot3(dot3(spread, part_z * (gain / scale)), spread, (1, 1))
    whole = iota((members, members), 0) == iota((members, members), 1)
    out_ref[...] = low_rank + jnp.where(whole, gain * z, 0.0) + shift


def mixing_transposed(raw_values, report_value, report_precision, report_class, slot_count):
    members, slots = raw_values.shape
    row = pl.BlockSpec((1, slots), lambda: (0, 0))
    return pl.pallas_call(
        mixing_kernel,
        in_specs=[
            pl.BlockSpec(memory_space=pltpu.SMEM),
            pl.BlockSpec((members, slots), lambda: (0, 0)),
            row,
            row,
            row,
        ],
        out_specs=pl.BlockSpec((members, members), lambda: (0, 0)),
        out_shape=jax.ShapeDtypeStruct((members, members), jnp.float32),
        compiler_params=pltpu.CompilerParams(vmem_limit_bytes=VMEM_LIMIT),
        cost_estimate=pl.CostEstimate(
            flops=NEWTON * 5 * 6 * slots**3, bytes_accessed=4 * members * members, transcendentals=0
        ),
        name="mixing",
    )(
        slot_count.reshape(1),
        raw_values,
        report_value[None, :],
        report_precision[None, :],
        report_class[None, :],
    )


def own_row(table, tile):
    flat_table = table.reshape((table.shape[0] * table.shape[1],) + table.shape[2:])
    return lax.dynamic_index_in_dim(flat_table, tile, 0, keepdims=False)


def on_device(
    prior_members,
    courant_x,
    courant_y,
    diffusion,
    report_level,
    report_cell,
    report_value,
    report_precision,
    report_class,
    report_count,
):
    total, members, rows, _ = prior_members.shape
    coefficients = (courant_x, courant_y, diffusion)
    tile = lax.axis_index("mem")
    dest = jnp.stack([shifted(tile, o) for o in OFFSETS]).astype(jnp.int32)
    half = total // 2

    def fields_sent(packed, moved, moved_k, first):
        return list(
            forecast(prior_members, coefficients, packed[0], moved, moved_k, dest, first, half)
        )

    packed = pack(prior_members, coefficients, 0, half)
    moved_k = exchange(packed)
    sent = fields_sent(packed, moved_k, moved_k[:3], 0)
    gathered = swap(sent[:EARLY], 1)
    later = pack(prior_members, coefficients, half, half, gathered[1:2])
    later, sent[EARLY:] = lax.optimization_barrier((later, sent[EARLY:]))
    moved = exchange(later)
    moved, sent[LATE:] = lax.optimization_barrier((moved, sent[LATE:]))
    gathered = [gathered + swap(sent[EARLY:], 1, EARLY)]
    sent = fields_sent(later, moved, moved_k[:3], half)
    gathered.append(swap(sent, 1))

    level, cell = own_row(report_level, tile), own_row(report_cell, tile)
    place = (level * (HEIGHT * LANES) + cell)[None, :]
    mixing_t = mixing_transposed(
        sample(gathered[0], place, sent[:1]),
        own_row(report_value, tile),
        own_row(report_precision, tile),
        own_row(report_class, tile),
        own_row(report_count, tile),
    )
    returned = [swap(transform(g, mixing_t), -1) for g in gathered]
    result = unpack(returned[0], None, dest, 0, total, members, rows)
    result = unpack(returned[1], result, dest, half, total, members, rows)
    return result.reshape(prior_members.shape)


def solution(mesh):
    in_specs = (
        P(None, "mem", "gx", "gy"),
        P("gx", "gy"),
        P("gx", "gy"),
        P("gx", "gy"),
        P("gx", "gy", None),
        P("gx", "gy", None),
        P("gx", "gy", None),
        P("gx", "gy", None),
        P("gx", "gy", None),
        P("gx", "gy"),
    )
    out_specs = P(None, "mem", "gx", "gy")
    return jax.shard_map(
        on_device, mesh=mesh, in_specs=in_specs, out_specs=out_specs, check_vma=False
    )
```

```python
import functools

import jax
import jax.numpy as jnp
from jax import lax
from jax.experimental import pallas as pl
from jax.experimental.pallas import tpu as pltpu
from jax.sharding import PartitionSpec as P

NEWTON = 8
LANES = 128
VMEM_LIMIT = 58 * 1024 * 1024
PACK_LIMIT = 58 * 1024 * 1024


def iota(shape, dim):
    return lax.broadcasted_iota(jnp.int32, shape, dim)


HEIGHT = 4
SPREAD = 32
PITCH = 8
CHIPS = ((0, 0), (1, 0), (0, 2), (1, 1), (0, 3), (1, 3), (0, 1), (1, 2))
OFFSETS = tuple(chip + (core,) for chip in CHIPS for core in range(2))
COUNT = len(OFFSETS)
EARLY, LATE = 5, 7
GROUPS = ((0,), (1, 2), (3, 4), (5, 6), (7,))


def shifted(index, offset, sign=1):
    z, y, core = index // 8, index // 2 % 4, index % 2
    dz, dy, dc = offset
    return (z + dz) % 2 * 8 + (y + sign * dy + 4) % 4 * 2 + (core + dc) % 2


def pair_spec(piece):
    return pl.BlockSpec((2, 1, piece, LANES), lambda i: (0, i, 0, 0))


def piece_specs(pieces):
    def spec(array, lead):
        return pl.BlockSpec((1, 1) + array.shape[2:], lambda i: (lead, i, 0, 0))

    return [spec(*p) for p in pieces]


def arrays(pieces):
    return [p[0] for p in pieces]


def pack_kernel(first, fields, rows, members, x_ref, cx_ref, cy_ref, df_ref, *refs):
    edge_ref, row_ref, corner_ref, held, sems = refs[-5:]
    step = pl.program_id(0)
    pitch = rows + PITCH
    picked = (0, 1, rows - 2, rows - 1)
    groups = rows // SPREAD

    def copy(field):
        return pltpu.make_async_copy(
            x_ref.at[first + field], held.at[field, :, pl.ds(0, rows), :], sems.at[field]
        )

    @pl.when(step == 0)
    def _():
        for field in range(fields):
            copy(field).start()

    def gather(read, tall):
        lane = iota((tall, LANES), 1)
        packed = []
        for group in range(groups):
            parts = [jnp.zeros((tall, LANES), jnp.float32) for _ in range(4)]
            for i in range(SPREAD):
                moved = pltpu.roll(read(group * SPREAD + i), (4 * i + 2) % LANES, 1)
                parts[i % 4] = jnp.where(lane // 4 == i, moved, parts[i % 4])
            packed.append((parts[0] + parts[1]) + (parts[2] + parts[3]))
            edge_ref[0, group, 0:tall, :] = packed[group]
        corner_ref[0, 0:tall, :] = jnp.where(lane < LANES // 2, packed[0], packed[-1])

    for field in range(fields):

        @pl.when(step == field)
        def _():
            copy(field).wait()
            flat = held.at[field].reshape(members * pitch, LANES)

            def read(row):
                value = flat[pl.ds(row, members, stride=pitch), :]
                if row in picked:
                    row_ref[0, picked.index(row)] = value
                return value

            gather(read, members)

    @pl.when(step == fields)
    def _():
        sub = iota((8, LANES), 0)
        row_ref[0] = jnp.zeros((4, members, LANES), jnp.float32)
        edge_ref[0] = jnp.zeros((groups, members, LANES), jnp.float32)
        corner_ref[0] = jnp.zeros((members, LANES), jnp.float32)

        def read(row):
            at = slice(row, row + 1)
            value = jnp.where(
                sub == 0, cx_ref[at, :], jnp.where(sub == 1, cy_ref[at, :], df_ref[at, :])
            )
            if row in picked:
                row_ref[0, picked.index(row), 0:8, :] = value
            return value

        gather(read, 8)


def pack(x, coefficients, first, fields, after=()):
    _, members, rows, _ = x.shape
    small = pl.BlockSpec((rows, LANES), lambda i: (0, 0))
    groups = rows // SPREAD
    return pl.pallas_call(
        functools.partial(pack_kernel, first, fields, rows, members),
        grid=(fields + 1,),
        in_specs=[pl.BlockSpec(memory_space=pl.ANY), small, small, small]
        + [pl.BlockSpec(memory_space=pl.ANY) for _ in after],
        out_specs=[
            pl.BlockSpec((1, groups, members, LANES), lambda i: (i, 0, 0, 0)),
            pl.BlockSpec((1, 4, members, LANES), lambda i: (i, 0, 0, 0)),
            pl.BlockSpec((1, members, LANES), lambda i: (i, 0, 0)),
        ],
        out_shape=[
            jax.ShapeDtypeStruct((fields + 1, groups, members, LANES), jnp.float32),
            jax.ShapeDtypeStruct((fields + 1, 4, members, LANES), jnp.float32),
            jax.ShapeDtypeStruct((fields + 1, members, LANES), jnp.float32),
        ],
        scratch_shapes=[
            pltpu.VMEM((fields, members, rows + PITCH, LANES), jnp.float32),
            pltpu.SemaphoreType.DMA((fields,)),
        ],
        compiler_params=pltpu.CompilerParams(vmem_limit_bytes=PACK_LIMIT),
        cost_estimate=pl.CostEstimate(
            flops=fields * members * rows * LANES * 2,
            bytes_accessed=fields * members * rows * LANES * 8,
            transcendentals=0,
        ),
        name="pack_edges",
    )(x, *coefficients, *after)


def exchange(packed):
    edge, row, corner = packed
    nx, ny = lax.axis_size("gx"), lax.axis_size("gy")
    right = [(i, (i + 1) % ny) for i in range(ny)]
    left = [(i, (i - 1) % ny) for i in range(ny)]

    def diagonal(step):
        return [
            (a * ny + b, ((a + 1) % nx) * ny + (b + step) % ny) for a in range(nx) for b in range(ny)
        ]

    return (
        lax.ppermute(row, "gx", [(i, (i + 1) % nx) for i in range(nx)]),
        lax.ppermute(edge, "gy", right),
        lax.ppermute(edge, "gy", left),
        lax.ppermute(corner, ("gx", "gy"), diagonal(1)),
        lax.ppermute(corner, ("gx", "gy"), diagonal(-1)),
    )


def weights_of(cx, cy, spread):
    plus_x, minus_x = jnp.maximum(cx, 0.0), jnp.minimum(cx, 0.0)
    plus_y, minus_y = jnp.maximum(cy, 0.0), jnp.minimum(cy, 0.0)
    centre = 1.0 - (plus_x - minus_x) - (plus_y - minus_y) - 4.0 * spread
    return centre, plus_x + spread, spread - minus_x, plus_y + spread, spread - minus_y


def stencil(k, centre, west, east, south, north):
    return k[0] * centre + k[1] * west + k[2] * east + k[3] * south + k[4] * north


def forecast_kernel(first, fields, rows, members, dest_ref, x_hbm, cx_ref, cy_ref, df_ref, own_ref, left_ref, right_ref, left_k_ref, right_k_ref, row_ref, row_k_ref, dl_ref, dr_ref, *refs):
    out_refs = refs[: len(CHIPS)]
    k_main, k_edge, k_row, edge_s, first_s, x_s, second_s, beside_s, held, sems = refs[len(CHIPS) :]
    step = pl.program_id(0)
    pitch = rows + PITCH

    def copy(field):
        slot = lax.rem(field, 2)
        return pltpu.make_async_copy(
            x_hbm.at[first + field], held.at[slot, :, pl.ds(0, rows), :], sems.at[slot]
        )

    @pl.when(step == 0)
    def _():
        copy(step).start()

    @pl.when(step + 1 < fields)
    def _():
        copy(step + 1).start()

    copy(step).wait()
    flat = held.at[lax.rem(step, 2)].reshape(members * pitch, LANES)
    for row in range(rows):
        x_s[row] = flat[pl.ds(row, members, stride=pitch), :]
    lane = iota((members, LANES), 1)
    from_left = lane % 4 < 2
    groups = rows // SPREAD

    @pl.when(pl.program_id(0) == 0)
    def _():
        for i, w in enumerate(weights_of(cx_ref[...], cy_ref[...], df_ref[...])):
            k_main[i] = w
        for group in range(groups):
            both = jnp.where(from_left[0:8], left_k_ref[0, group, 0:8, :], right_k_ref[0, group, 0:8, :])
            for i, w in enumerate(weights_of(*[both[j : j + 1, :] for j in range(3)])):
                k_edge[group, i : i + 1, :] = w
        for side, at in ((0, 3), (1, 0)):
            for i, w in enumerate(weights_of(*[row_k_ref[0, at, j : j + 1, :] for j in range(3)])):
                k_row[side, i : i + 1, :] = w

    edges = [jnp.where(from_left, left_ref[0, g], right_ref[0, g]) for g in range(groups)]
    corner = jnp.where(from_left, dl_ref[0], dr_ref[0])
    chain = [corner] + edges + [corner]
    up = [pltpu.roll(v, 4, 1) for v in chain]
    down = [pltpu.roll(v, LANES - 4, 1) for v in chain]
    for group, edge in enumerate(edges):
        own = own_ref[0, group]
        edge_s[0, group] = edge
        edge_s[1, group] = stencil(
            [k_edge[group, i : i + 1, :] for i in range(5)],
            edge,
            jnp.where(lane < 4, up[group], up[group + 1]),
            jnp.where(lane >= LANES - 4, down[group + 2], down[group + 1]),
            pltpu.roll(jnp.where(lane % 4 == 0, edge, own), 1, 1),
            pltpu.roll(jnp.where(lane % 4 == 3, edge, own), LANES - 1, 1),
        )

    def sides(centre, beside):
        return (
            pltpu.roll(jnp.where(lane == LANES - 1, beside, centre), 1, 1),
            pltpu.roll(jnp.where(lane == 0, beside, centre), LANES - 1, 1),
        )

    for side, (centre, west, east, turn, at) in enumerate(
        (
            (row_ref[0, 3], row_ref[0, 2], x_s[0], 2, 0),
            (row_ref[0, 0], x_s[rows - 1], row_ref[0, 1], LANES - 2, rows + 1),
        )
    ):
        k = [k_row[side, i : i + 1, :] for i in range(5)]
        first_s[at] = stencil(k, centre, west, east, *sides(centre, pltpu.roll(corner, turn, 1)))

    def lay_sides(stage):
        for row in range(rows):
            turn = (126 - row % SPREAD * 4) % LANES
            beside_s[row] = pltpu.roll(edge_s[stage, row // SPREAD], turn, 1)

    def one(row, centre, west, east):
        k = [k_main[i, row : row + 1, :] for i in range(5)]
        return stencil(k, centre, west, east, *sides(centre, beside_s[row]))

    lay_sides(0)
    for row in range(rows):
        west = row_ref[0, 3] if row == 0 else x_s[row - 1]
        east = row_ref[0, 0] if row == rows - 1 else x_s[row + 1]
        first_s[row + 1] = one(row, x_s[row], west, east)
    lay_sides(1)
    for row in range(rows):
        second_s[row] = one(row, first_s[row + 1], first_s[row], first_s[row + 2])
    for i in range(COUNT):
        base = dest_ref[i] * HEIGHT
        for r in range(HEIGHT):
            out_refs[i // 2][i % 2, 0, r * members : (r + 1) * members, :] = second_s[base + r]


def forecast(x, coefficients, edge, moved, moved_k, dest, first, fields):
    _, members, rows, _ = x.shape
    row, left, right, corner_l, corner_r = moved
    row_k, left_k, right_k = moved_k
    last = row_k.shape[0] - 1
    groups = rows // SPREAD
    small = pl.BlockSpec((rows, LANES), lambda i: (0, 0))
    edge_spec = pl.BlockSpec((1, groups, members, LANES), lambda i: (i, 0, 0, 0))
    edge_last = pl.BlockSpec((1, groups, members, LANES), lambda i: (last, 0, 0, 0))
    corner_spec = pl.BlockSpec((1, members, LANES), lambda i: (i, 0, 0))
    piece = HEIGHT * members
    return pl.pallas_call(
        functools.partial(forecast_kernel, first, fields, rows, members),
        grid=(fields,),
        in_specs=[
            pl.BlockSpec(memory_space=pltpu.SMEM),
            pl.BlockSpec(memory_space=pl.ANY),
            small,
            small,
            small,
            edge_spec,
            edge_spec,
            edge_spec,
            edge_last,
            edge_last,
            pl.BlockSpec((1, 4, members, LANES), lambda i: (i, 0, 0, 0)),
            pl.BlockSpec((1, 4, members, LANES), lambda i: (last, 0, 0, 0)),
            corner_spec,
            corner_spec,
        ],
        out_specs=[pair_spec(piece)] * len(CHIPS),
        out_shape=[jax.ShapeDtypeStruct((2, fields, piece, LANES), jnp.float32)] * len(CHIPS),
        scratch_shapes=[
            pltpu.VMEM((5, rows, LANES), jnp.float32),
            pltpu.VMEM((groups, 8, LANES), jnp.float32),
            pltpu.VMEM((2, 8, LANES), jnp.float32),
            pltpu.VMEM((2, groups, members, LANES), jnp.float32),
            pltpu.VMEM((rows + 2, members, LANES), jnp.float32),
            pltpu.VMEM((rows, members, LANES), jnp.float32),
            pltpu.VMEM((rows, members, LANES), jnp.float32),
            pltpu.VMEM((rows, members, LANES), jnp.float32),
            pltpu.VMEM((2, members, rows + PITCH, LANES), jnp.float32),
            pltpu.SemaphoreType.DMA((2,)),
        ],
        compiler_params=pltpu.CompilerParams(vmem_limit_bytes=PACK_LIMIT),
        cost_estimate=pl.CostEstimate(
            flops=fields * rows * members * LANES * 18,
            bytes_accessed=fields * rows * members * LANES * 8,
            transcendentals=0,
        ),
        name="forecast",
    )(dest, x, *coefficients, edge, left, right, left_k, right_k, row, row_k, corner_l, corner_r)


def halves(value):
    high = value.astype(jnp.bfloat16)
    return high, (value - high.astype(jnp.float32)).astype(jnp.bfloat16)


def dot(a, b):
    return jnp.dot(a, b, preferred_element_type=jnp.float32)


def tile_rows(refs, r):
    tall = refs[0].shape[2] // HEIGHT
    return jnp.concatenate([ref[0, 0, r * tall : (r + 1) * tall, :] for ref in refs], axis=0)


def sample_kernel(place_ref, *refs):
    step = pl.program_id(0)
    x_refs, out_ref = refs[:COUNT], refs[-1]
    slots = place_ref.shape[1]
    cells = HEIGHT * LANES
    x = jnp.concatenate([tile_rows(x_refs, r) for r in range(HEIGHT)], axis=1)
    chosen = (iota((cells, slots), 0) + step * cells == place_ref[0:1, :]).astype(jnp.bfloat16)
    high = x.astype(jnp.bfloat16)
    middle, low = halves(x - high.astype(jnp.float32))
    got = dot(high, chosen) + dot(middle, chosen) + dot(low, chosen)

    @pl.when(step == 0)
    def _():
        out_ref[...] = got

    @pl.when(step > 0)
    def _():
        out_ref[...] += got


def sample(pieces, place, after):
    _, fields, piece, _ = pieces[0][0].shape
    members = COUNT * piece // HEIGHT
    slots = place.shape[1]
    return pl.pallas_call(
        sample_kernel,
        grid=(fields,),
        in_specs=[pl.BlockSpec((1, slots), lambda i: (0, 0))]
        + piece_specs(pieces)
        + [pl.BlockSpec(memory_space=pl.ANY) for _ in after],
        out_specs=pl.BlockSpec((members, slots), lambda i: (0, 0)),
        out_shape=jax.ShapeDtypeStruct((members, slots), jnp.float32),
        compiler_params=pltpu.CompilerParams(vmem_limit_bytes=VMEM_LIMIT),
        cost_estimate=pl.CostEstimate(
            flops=fields * members * HEIGHT * LANES * slots * 6,
            bytes_accessed=fields * members * HEIGHT * LANES * 4,
            transcendentals=0,
        ),
        name="sample",
    )(place, *arrays(pieces), *after)


def transform_kernel(mix_ref, *refs):
    x_refs, out_refs, (high_s, low_s) = refs[:COUNT], refs[COUNT:-2], refs[-2:]

    @pl.when(pl.program_id(0) == 0)
    def _():
        high_s[...], low_s[...] = halves(mix_ref[...])

    tall = x_refs[0].shape[2] // HEIGHT
    members = COUNT * tall
    for half in range(HEIGHT // 2):
        x = jnp.concatenate([tile_rows(x_refs, 2 * half + i) for i in range(2)], axis=1)
        centre = jnp.sum(x, axis=0, keepdims=True) / members
        high, low = halves(x - centre)
        result = dot(high_s[...], high) + (dot(high_s[...], low) + dot(low_s[...], high)) + centre
        for i in range(2):
            at = (2 * half + i) * tall
            for o in range(COUNT):
                out_refs[o // 2][o % 2, 0, at : at + tall, :] = result[
                    o * tall : (o + 1) * tall, i * LANES : (i + 1) * LANES
                ]


def transform(pieces, mixing_t):
    _, fields, piece, _ = pieces[0][0].shape
    members = mixing_t.shape[0]
    return pl.pallas_call(
        transform_kernel,
        grid=(fields,),
        in_specs=[pl.BlockSpec((members, members), lambda i: (0, 0))] + piece_specs(pieces),
        out_specs=[pair_spec(piece)] * len(CHIPS),
        out_shape=[jax.ShapeDtypeStruct((2, fields, piece, LANES), jnp.float32)] * len(CHIPS),
        scratch_shapes=[
            pltpu.VMEM((members, members), jnp.bfloat16),
            pltpu.VMEM((members, members), jnp.bfloat16),
        ],
        compiler_params=pltpu.CompilerParams(vmem_limit_bytes=VMEM_LIMIT),
        cost_estimate=pl.CostEstimate(
            flops=fields * members * members * HEIGHT * LANES * 6,
            bytes_accessed=fields * members * HEIGHT * LANES * 8,
            transcendentals=0,
        ),
        name="transform",
    )(mixing_t, *arrays(pieces))


def unpack_kernel(members, rows, dest_ref, *refs):
    x_refs, out_ref, held = refs[:COUNT], refs[-2], refs[-1]
    pitch = rows + 4
    for i in range(COUNT):
        base = dest_ref[i] * HEIGHT
        for r in range(HEIGHT):
            held[pl.ds(base + r, members, stride=pitch), :] = x_refs[i][0, 0, r * members : (r + 1) * members, :]
    for m in range(members):
        out_ref[0, m * rows : (m + 1) * rows, :] = held[m * pitch : m * pitch + rows, :]


def unpack(pieces, so_far, dest, first, total, members, rows):
    _, fields, piece, _ = pieces[0][0].shape
    flat = members * rows
    more = () if so_far is None else (so_far,)
    return pl.pallas_call(
        functools.partial(unpack_kernel, members, rows),
        grid=(fields,),
        in_specs=[pl.BlockSpec(memory_space=pltpu.SMEM)]
        + piece_specs(pieces)
        + [pl.BlockSpec(memory_space=pl.ANY) for _ in more],
        out_specs=pl.BlockSpec((1, flat, LANES), lambda i: (first + i, 0, 0)),
        out_shape=jax.ShapeDtypeStruct((total, flat, LANES), jnp.float32),
        scratch_shapes=[pltpu.VMEM((members * (rows + 4), LANES), jnp.float32)],
        input_output_aliases={COUNT + 1: 0} if more else {},
        compiler_params=pltpu.CompilerParams(vmem_limit_bytes=VMEM_LIMIT),
        cost_estimate=pl.CostEstimate(
            flops=0, bytes_accessed=fields * flat * LANES * 8, transcendentals=0
        ),
        name="unpack",
    )(dest, *arrays(pieces), *more)


def hop(value, offset, sign):
    return lax.ppermute(value, "mem", [(i, shifted(i, offset, sign)) for i in range(COUNT)])


def travel(sent, sign, skip=0):
    return [
        value if chip == (0, 0) else hop(value, chip + (0,), sign)
        for value, chip in zip(sent, CHIPS[skip:])
    ]


def trade(arrived, group):
    return hop(jnp.concatenate([arrived[o][1:2] for o in group], axis=0), (0, 0, 1), 1)


def settled(arrived, traded):
    pieces = []
    for group, value in zip(GROUPS, traded):
        for at, o in enumerate(group):
            pieces += [(arrived[o], 0), (value, at)]
    return pieces


def spread_out(sent, sign):
    arrived = travel(sent, sign)
    return settled(arrived, [trade(arrived, group) for group in GROUPS])


def dot3(a, b, dims=(1, 0)):
    (ah, al), (bh, bl) = halves(a), halves(b)

    def one(u, v):
        return lax.dot_general(
            u, v, (((dims[0],), (dims[1],)), ((), ())), preferred_element_type=jnp.float32
        )

    return one(ah, bh) + (one(ah, bl) + one(al, bh))


def mixing_kernel(count_ref, raw_ref, value_ref, precision_ref, class_ref, out_ref):
    members, slots = raw_ref.shape
    raw = raw_ref[...]
    centre_obs = jnp.sum(raw, axis=0, keepdims=True) / members
    usable = iota((1, slots), 1) < count_ref[0]
    weight = jnp.where(usable, precision_ref[...] / (1.0 + class_ref[...].astype(jnp.float32)), 0.0)
    root_weight = jnp.sqrt(weight)
    spread = (raw - centre_obs) * root_weight
    small = dot3(spread, spread, (0, 0))
    inflation = members - 1.0
    scale = jnp.sqrt(
        inflation * inflation * members
        + 2.0 * inflation * jnp.sum(spread * spread, keepdims=True)
        + jnp.sum(small * small, keepdims=True)
    )
    eye = (iota((slots, slots), 0) == iota((slots, slots), 1)).astype(jnp.float32)
    start = inflation / scale
    y, z = start, jnp.ones_like(start)
    root_y = start * eye + small / scale
    factor = 1.5 * eye - 0.5 * root_y
    p = 1.5 - 0.5 * y
    root_z, part_z, z = factor, -0.5 * eye, p
    root_y, y = dot3(root_y, factor), y * p
    for iteration in range(1, NEWTON):
        both = dot3(jnp.concatenate([root_z, part_z], axis=0), root_y)
        part = z * (start * part_z + root_z) + both[slots:]
        factor = 1.5 * eye - 0.5 * both[:slots]
        p = 1.5 - 0.5 * z * y
        both = dot3(jnp.concatenate([factor, -0.5 * part], axis=0), root_z)
        if iteration + 1 < NEWTON:
            root_y, y = dot3(root_y, factor), y * p
        root_z, part_z, z = both[:slots], p * part_z + both[slots:], z * p
    driven = jnp.broadcast_to(root_weight * (value_ref[...] - centre_obs), (8, slots))
    driven = dot3(dot3(driven, root_z), root_z)
    shift = dot3(driven, spread, (1, 1))[0:1] / scale
    gain = jnp.sqrt(inflation / scale)
    low_rank = dot3(dot3(spread, part_z * (gain / scale)), spread, (1, 1))
    whole = iota((members, members), 0) == iota((members, members), 1)
    out_ref[...] = low_rank + jnp.where(whole, gain * z, 0.0) + shift


def mixing_transposed(raw_values, report_value, report_precision, report_class, slot_count):
    members, slots = raw_values.shape
    row = pl.BlockSpec((1, slots), lambda: (0, 0))
    return pl.pallas_call(
        mixing_kernel,
        in_specs=[
            pl.BlockSpec(memory_space=pltpu.SMEM),
            pl.BlockSpec((members, slots), lambda: (0, 0)),
            row,
            row,
            row,
        ],
        out_specs=pl.BlockSpec((members, members), lambda: (0, 0)),
        out_shape=jax.ShapeDtypeStruct((members, members), jnp.float32),
        compiler_params=pltpu.CompilerParams(vmem_limit_bytes=VMEM_LIMIT),
        cost_estimate=pl.CostEstimate(
            flops=NEWTON * 5 * 6 * slots**3, bytes_accessed=4 * members * members, transcendentals=0
        ),
        name="mixing",
    )(
        slot_count.reshape(1),
        raw_values,
        report_value[None, :],
        report_precision[None, :],
        report_class[None, :],
    )


def own_row(table, tile):
    flat_table = table.reshape((table.shape[0] * table.shape[1],) + table.shape[2:])
    return lax.dynamic_index_in_dim(flat_table, tile, 0, keepdims=False)


def on_device(
    prior_members,
    courant_x,
    courant_y,
    diffusion,
    report_level,
    report_cell,
    report_value,
    report_precision,
    report_class,
    report_count,
):
    total, members, rows, _ = prior_members.shape
    coefficients = (courant_x, courant_y, diffusion)
    tile = lax.axis_index("mem")
    dest = jnp.stack([shifted(tile, o) for o in OFFSETS]).astype(jnp.int32)
    half = total // 2

    def fields_sent(packed, moved, moved_k, first):
        return list(
            forecast(prior_members, coefficients, packed[0], moved, moved_k, dest, first, half)
        )

    packed = pack(prior_members, coefficients, 0, half)
    moved_k = exchange(packed)
    sent = fields_sent(packed, moved_k, moved_k[:3], 0)
    arrived = travel(sent[:EARLY], 1)
    traded = [trade(arrived, GROUPS[0])]
    later = pack(prior_members, coefficients, half, half, traded)
    later, sent[EARLY:] = lax.optimization_barrier((later, sent[EARLY:]))
    moved = exchange(later)
    following = fields_sent(later, moved, moved_k[:3], half)
    following, sent[LATE:] = lax.optimization_barrier((following, sent[LATE:]))
    arrived += travel(sent[EARLY:], 1, EARLY)
    traded += [trade(arrived, group) for group in GROUPS[1:]]
    sent = following
    traded, sent[EARLY:] = lax.optimization_barrier((traded, sent[EARLY:]))
    gathered = settled(arrived, traded)

    level, cell = own_row(report_level, tile), own_row(report_cell, tile)
    place = (level * (HEIGHT * LANES) + cell)[None, :]
    mixing_t = mixing_transposed(
        sample(gathered, place, sent[:1]),
        own_row(report_value, tile),
        own_row(report_precision, tile),
        own_row(report_class, tile),
        own_row(report_count, tile),
    )
    mixing_t, sent[EARLY:] = lax.optimization_barrier((mixing_t, sent[EARLY:]))
    analysed = list(transform(gathered, mixing_t))
    analysed, sent[LATE:] = lax.optimization_barrier((analysed, sent[LATE:]))
    gathered = spread_out(sent, 1)

    arrived = travel(analysed[:EARLY], -1)
    traded = [trade(arrived, GROUPS[0])]
    ready = list(transform(gathered, mixing_t))
    ready, analysed[EARLY:] = lax.optimization_barrier((ready, analysed[EARLY:]))
    arrived += travel(analysed[EARLY:], -1, EARLY)
    traded += [trade(arrived, group) for group in GROUPS[1:]]
    traded, ready[EARLY:] = lax.optimization_barrier((traded, ready[EARLY:]))
    returned = [settled(arrived, traded), spread_out(ready, -1)]
    result = unpack(returned[0], None, dest, 0, total, members, rows)
    result = unpack(returned[1], result, dest, half, total, members, rows)
    return result.reshape(prior_members.shape)


def solution(mesh):
    in_specs = (
        P(None, "mem", "gx", "gy"),
        P("gx", "gy"),
        P("gx", "gy"),
        P("gx", "gy"),
        P("gx", "gy", None),
        P("gx", "gy", None),
        P("gx", "gy", None),
        P("gx", "gy", None),
        P("gx", "gy", None),
        P("gx", "gy"),
    )
    out_specs = P(None, "mem", "gx", "gy")
    return jax.shard_map(
        on_device, mesh=mesh, in_specs=in_specs, out_specs=out_specs, check_vma=False
    )
```

```python
import functools

import jax
import jax.numpy as jnp
from jax import lax
from jax.experimental import pallas as pl
from jax.experimental.pallas import tpu as pltpu
from jax.sharding import PartitionSpec as P

NEWTON = 8
LANES = 128
VMEM_LIMIT = 60 * 1024 * 1024
PACK_LIMIT = 60 * 1024 * 1024


def iota(shape, dim):
    return lax.broadcasted_iota(jnp.int32, shape, dim)


HEIGHT = 4
SPREAD = 32
PITCH = 8
CHIPS = ((0, 0), (1, 0), (0, 2), (1, 1), (0, 3), (1, 3), (0, 1), (1, 2))
OFFSETS = tuple(chip + (core,) for chip in CHIPS for core in range(2))
COUNT = len(OFFSETS)
EARLY, LATE = 5, 7
GROUPS = ((0,), (1, 2), (3, 4), (5, 6), (7,))


def shifted(index, offset, sign=1):
    z, y, core = index // 8, index // 2 % 4, index % 2
    dz, dy, dc = offset
    return (z + dz) % 2 * 8 + (y + sign * dy + 4) % 4 * 2 + (core + dc) % 2


def pair_spec(piece):
    return pl.BlockSpec((2, 1, piece, LANES), lambda i: (0, i, 0, 0))


def piece_specs(pieces):
    def spec(array, lead):
        return pl.BlockSpec((1, 1) + array.shape[2:], lambda i: (lead, i, 0, 0))

    return [spec(*p) for p in pieces]


def arrays(pieces):
    return [p[0] for p in pieces]


def pack_kernel(first, fields, rows, members, x_ref, cx_ref, cy_ref, df_ref, *refs):
    edge_ref, row_ref, corner_ref, held, sems = refs[-5:]
    step = pl.program_id(0)
    pitch = rows + PITCH
    picked = (0, 1, rows - 2, rows - 1)
    groups = rows // SPREAD

    def copy(field):
        return pltpu.make_async_copy(
            x_ref.at[first + field], held.at[field, :, pl.ds(0, rows), :], sems.at[field]
        )

    @pl.when(step == 0)
    def _():
        for field in range(fields):
            copy(field).start()

    def gather(read, tall):
        lane = iota((tall, LANES), 1)
        packed = []
        for group in range(groups):
            parts = [jnp.zeros((tall, LANES), jnp.float32) for _ in range(4)]
            for i in range(SPREAD):
                moved = pltpu.roll(read(group * SPREAD + i), (4 * i + 2) % LANES, 1)
                parts[i % 4] = jnp.where(lane // 4 == i, moved, parts[i % 4])
            packed.append((parts[0] + parts[1]) + (parts[2] + parts[3]))
            edge_ref[0, group, 0:tall, :] = packed[group]
        corner_ref[0, 0:tall, :] = jnp.where(lane < LANES // 2, packed[0], packed[-1])

    for field in range(fields):

        @pl.when(step == field)
        def _():
            copy(field).wait()
            flat = held.at[field].reshape(members * pitch, LANES)

            def read(row):
                value = flat[pl.ds(row, members, stride=pitch), :]
                if row in picked:
                    row_ref[0, picked.index(row)] = value
                return value

            gather(read, members)

    @pl.when(step == fields)
    def _():
        sub = iota((8, LANES), 0)
        row_ref[0] = jnp.zeros((4, members, LANES), jnp.float32)
        edge_ref[0] = jnp.zeros((groups, members, LANES), jnp.float32)
        corner_ref[0] = jnp.zeros((members, LANES), jnp.float32)

        def read(row):
            at = slice(row, row + 1)
            value = jnp.where(
                sub == 0, cx_ref[at, :], jnp.where(sub == 1, cy_ref[at, :], df_ref[at, :])
            )
            if row in picked:
                row_ref[0, picked.index(row), 0:8, :] = value
            return value

        gather(read, 8)


def pack(x, coefficients, first, fields, after=()):
    _, members, rows, _ = x.shape
    small = pl.BlockSpec((rows, LANES), lambda i: (0, 0))
    groups = rows // SPREAD
    return pl.pallas_call(
        functools.partial(pack_kernel, first, fields, rows, members),
        grid=(fields + 1,),
        in_specs=[pl.BlockSpec(memory_space=pl.ANY), small, small, small]
        + [pl.BlockSpec(memory_space=pl.ANY) for _ in after],
        out_specs=[
            pl.BlockSpec((1, groups, members, LANES), lambda i: (i, 0, 0, 0)),
            pl.BlockSpec((1, 4, members, LANES), lambda i: (i, 0, 0, 0)),
            pl.BlockSpec((1, members, LANES), lambda i: (i, 0, 0)),
        ],
        out_shape=[
            jax.ShapeDtypeStruct((fields + 1, groups, members, LANES), jnp.float32),
            jax.ShapeDtypeStruct((fields + 1, 4, members, LANES), jnp.float32),
            jax.ShapeDtypeStruct((fields + 1, members, LANES), jnp.float32),
        ],
        scratch_shapes=[
            pltpu.VMEM((fields, members, rows + PITCH, LANES), jnp.float32),
            pltpu.SemaphoreType.DMA((fields,)),
        ],
        compiler_params=pltpu.CompilerParams(vmem_limit_bytes=PACK_LIMIT),
        cost_estimate=pl.CostEstimate(
            flops=fields * members * rows * LANES * 2,
            bytes_accessed=fields * members * rows * LANES * 8,
            transcendentals=0,
        ),
        name="pack_edges",
    )(x, *coefficients, *after)


def exchange(packed):
    edge, row, corner = packed
    nx, ny = lax.axis_size("gx"), lax.axis_size("gy")
    right = [(i, (i + 1) % ny) for i in range(ny)]
    left = [(i, (i - 1) % ny) for i in range(ny)]

    def diagonal(step):
        return [
            (a * ny + b, ((a + 1) % nx) * ny + (b + step) % ny) for a in range(nx) for b in range(ny)
        ]

    return (
        lax.ppermute(row, "gx", [(i, (i + 1) % nx) for i in range(nx)]),
        lax.ppermute(edge, "gy", right),
        lax.ppermute(edge, "gy", left),
        lax.ppermute(corner, ("gx", "gy"), diagonal(1)),
        lax.ppermute(corner, ("gx", "gy"), diagonal(-1)),
    )


def weights_of(cx, cy, spread):
    plus_x, minus_x = jnp.maximum(cx, 0.0), jnp.minimum(cx, 0.0)
    plus_y, minus_y = jnp.maximum(cy, 0.0), jnp.minimum(cy, 0.0)
    centre = 1.0 - (plus_x - minus_x) - (plus_y - minus_y) - 4.0 * spread
    return centre, plus_x + spread, spread - minus_x, plus_y + spread, spread - minus_y


def stencil(k, centre, west, east, south, north):
    return k[0] * centre + k[1] * west + k[2] * east + k[3] * south + k[4] * north


def forecast_kernel(first, fields, rows, members, dest_ref, x_hbm, cx_ref, cy_ref, df_ref, own_ref, left_ref, right_ref, left_k_ref, right_k_ref, row_ref, row_k_ref, dl_ref, dr_ref, *refs):
    k_main, k_edge, k_row, edge_s, first_s, x_s, second_s, beside_s, held, sems = refs[-10:]
    out_refs = refs[-10 - len(CHIPS) : -10]
    step = pl.program_id(0)
    pitch = rows + PITCH

    def copy(field):
        slot = lax.rem(field, 2)
        return pltpu.make_async_copy(
            x_hbm.at[first + field], held.at[slot, :, pl.ds(0, rows), :], sems.at[slot]
        )

    @pl.when(step == 0)
    def _():
        copy(step).start()

    @pl.when(step + 1 < fields)
    def _():
        copy(step + 1).start()

    copy(step).wait()
    flat = held.at[lax.rem(step, 2)].reshape(members * pitch, LANES)
    for row in range(rows):
        x_s[row] = flat[pl.ds(row, members, stride=pitch), :]
    lane = iota((members, LANES), 1)
    from_left = lane % 4 < 2
    groups = rows // SPREAD

    @pl.when(pl.program_id(0) == 0)
    def _():
        for i, w in enumerate(weights_of(cx_ref[...], cy_ref[...], df_ref[...])):
            k_main[i] = w
        for group in range(groups):
            both = jnp.where(from_left[0:8], left_k_ref[0, group, 0:8, :], right_k_ref[0, group, 0:8, :])
            for i, w in enumerate(weights_of(*[both[j : j + 1, :] for j in range(3)])):
                k_edge[group, i : i + 1, :] = w
        for side, at in ((0, 3), (1, 0)):
            for i, w in enumerate(weights_of(*[row_k_ref[0, at, j : j + 1, :] for j in range(3)])):
                k_row[side, i : i + 1, :] = w

    edges = [jnp.where(from_left, left_ref[0, g], right_ref[0, g]) for g in range(groups)]
    corner = jnp.where(from_left, dl_ref[0], dr_ref[0])
    chain = [corner] + edges + [corner]
    up = [pltpu.roll(v, 4, 1) for v in chain]
    down = [pltpu.roll(v, LANES - 4, 1) for v in chain]
    for group, edge in enumerate(edges):
        own = own_ref[0, group]
        edge_s[0, group] = edge
        edge_s[1, group] = stencil(
            [k_edge[group, i : i + 1, :] for i in range(5)],
            edge,
            jnp.where(lane < 4, up[group], up[group + 1]),
            jnp.where(lane >= LANES - 4, down[group + 2], down[group + 1]),
            pltpu.roll(jnp.where(lane % 4 == 0, edge, own), 1, 1),
            pltpu.roll(jnp.where(lane % 4 == 3, edge, own), LANES - 1, 1),
        )

    def sides(centre, beside):
        return (
            pltpu.roll(jnp.where(lane == LANES - 1, beside, centre), 1, 1),
            pltpu.roll(jnp.where(lane == 0, beside, centre), LANES - 1, 1),
        )

    for side, (centre, west, east, turn, at) in enumerate(
        (
            (row_ref[0, 3], row_ref[0, 2], x_s[0], 2, 0),
            (row_ref[0, 0], x_s[rows - 1], row_ref[0, 1], LANES - 2, rows + 1),
        )
    ):
        k = [k_row[side, i : i + 1, :] for i in range(5)]
        first_s[at] = stencil(k, centre, west, east, *sides(centre, pltpu.roll(corner, turn, 1)))

    def lay_sides(stage):
        for row in range(rows):
            turn = (126 - row % SPREAD * 4) % LANES
            beside_s[row] = pltpu.roll(edge_s[stage, row // SPREAD], turn, 1)

    def one(row, centre, west, east):
        k = [k_main[i, row : row + 1, :] for i in range(5)]
        return stencil(k, centre, west, east, *sides(centre, beside_s[row]))

    lay_sides(0)
    for row in range(rows):
        west = row_ref[0, 3] if row == 0 else x_s[row - 1]
        east = row_ref[0, 0] if row == rows - 1 else x_s[row + 1]
        first_s[row + 1] = one(row, x_s[row], west, east)
    lay_sides(1)
    for row in range(rows):
        second_s[row] = one(row, first_s[row + 1], first_s[row], first_s[row + 2])
    for i in range(COUNT):
        base = dest_ref[i] * HEIGHT
        for r in range(HEIGHT):
            out_refs[i // 2][i % 2, 0, r * members : (r + 1) * members, :] = second_s[base + r]


def forecast(x, coefficients, edge, moved, dest, first, fields, after):
    _, members, rows, _ = x.shape
    row, left, right, corner_l, corner_r = moved
    last = row.shape[0] - 1
    groups = rows // SPREAD
    small = pl.BlockSpec((rows, LANES), lambda i: (0, 0))
    edge_spec = pl.BlockSpec((1, groups, members, LANES), lambda i: (first + i, 0, 0, 0))
    edge_last = pl.BlockSpec((1, groups, members, LANES), lambda i: (last, 0, 0, 0))
    corner_spec = pl.BlockSpec((1, members, LANES), lambda i: (first + i, 0, 0))
    piece = HEIGHT * members
    return pl.pallas_call(
        functools.partial(forecast_kernel, first, fields, rows, members),
        grid=(fields,),
        in_specs=[
            pl.BlockSpec(memory_space=pltpu.SMEM),
            pl.BlockSpec(memory_space=pl.ANY),
            small,
            small,
            small,
            edge_spec,
            edge_spec,
            edge_spec,
            edge_last,
            edge_last,
            pl.BlockSpec((1, 4, members, LANES), lambda i: (first + i, 0, 0, 0)),
            pl.BlockSpec((1, 4, members, LANES), lambda i: (last, 0, 0, 0)),
            corner_spec,
            corner_spec,
        ]
        + [pl.BlockSpec(memory_space=pl.ANY) for _ in after],
        out_specs=[pair_spec(piece)] * len(CHIPS),
        out_shape=[jax.ShapeDtypeStruct((2, fields, piece, LANES), jnp.float32)] * len(CHIPS),
        scratch_shapes=[
            pltpu.VMEM((5, rows, LANES), jnp.float32),
            pltpu.VMEM((groups, 8, LANES), jnp.float32),
            pltpu.VMEM((2, 8, LANES), jnp.float32),
            pltpu.VMEM((2, groups, members, LANES), jnp.float32),
            pltpu.VMEM((rows + 2, members, LANES), jnp.float32),
            pltpu.VMEM((rows, members, LANES), jnp.float32),
            pltpu.VMEM((rows, members, LANES), jnp.float32),
            pltpu.VMEM((rows, members, LANES), jnp.float32),
            pltpu.VMEM((2, members, rows + PITCH, LANES), jnp.float32),
            pltpu.SemaphoreType.DMA((2,)),
        ],
        compiler_params=pltpu.CompilerParams(vmem_limit_bytes=PACK_LIMIT),
        cost_estimate=pl.CostEstimate(
            flops=fields * rows * members * LANES * 18,
            bytes_accessed=fields * rows * members * LANES * 8,
            transcendentals=0,
        ),
        name="forecast",
    )(dest, x, *coefficients, edge, left, right, left, right, row, row, corner_l, corner_r, *after)


def halves(value):
    high = value.astype(jnp.bfloat16)
    return high, (value - high.astype(jnp.float32)).astype(jnp.bfloat16)


def dot(a, b):
    return jnp.dot(a, b, preferred_element_type=jnp.float32)


def tile_rows(refs, r):
    tall = refs[0].shape[2] // HEIGHT
    return jnp.concatenate([ref[0, 0, r * tall : (r + 1) * tall, :] for ref in refs], axis=0)


def sample_kernel(place_ref, *refs):
    step = pl.program_id(0)
    x_refs, out_ref = refs[:COUNT], refs[-1]
    slots = place_ref.shape[1]
    cells = HEIGHT * LANES
    x = jnp.concatenate([tile_rows(x_refs, r) for r in range(HEIGHT)], axis=1)
    chosen = (iota((cells, slots), 0) + step * cells == place_ref[0:1, :]).astype(jnp.bfloat16)
    high = x.astype(jnp.bfloat16)
    middle, low = halves(x - high.astype(jnp.float32))
    got = dot(high, chosen) + dot(middle, chosen) + dot(low, chosen)

    @pl.when(step == 0)
    def _():
        out_ref[...] = got

    @pl.when(step > 0)
    def _():
        out_ref[...] += got


def sample(pieces, place, after):
    _, fields, piece, _ = pieces[0][0].shape
    members = COUNT * piece // HEIGHT
    slots = place.shape[1]
    return pl.pallas_call(
        sample_kernel,
        grid=(fields,),
        in_specs=[pl.BlockSpec((1, slots), lambda i: (0, 0))]
        + piece_specs(pieces)
        + [pl.BlockSpec(memory_space=pl.ANY) for _ in after],
        out_specs=pl.BlockSpec((members, slots), lambda i: (0, 0)),
        out_shape=jax.ShapeDtypeStruct((members, slots), jnp.float32),
        compiler_params=pltpu.CompilerParams(vmem_limit_bytes=VMEM_LIMIT),
        cost_estimate=pl.CostEstimate(
            flops=fields * members * HEIGHT * LANES * slots * 6,
            bytes_accessed=fields * members * HEIGHT * LANES * 4,
            transcendentals=0,
        ),
        name="sample",
    )(place, *arrays(pieces), *after)


def transform_kernel(mix_ref, *refs):
    x_refs, out_refs, (high_s, low_s) = refs[:COUNT], refs[COUNT:-2], refs[-2:]

    @pl.when(pl.program_id(0) == 0)
    def _():
        high_s[...], low_s[...] = halves(mix_ref[...])

    tall = x_refs[0].shape[2] // HEIGHT
    members = COUNT * tall
    for half in range(HEIGHT // 2):
        x = jnp.concatenate([tile_rows(x_refs, 2 * half + i) for i in range(2)], axis=1)
        centre = jnp.sum(x, axis=0, keepdims=True) / members
        high, low = halves(x - centre)
        result = dot(high_s[...], high) + (dot(high_s[...], low) + dot(low_s[...], high)) + centre
        for i in range(2):
            at = (2 * half + i) * tall
            for o in range(COUNT):
                out_refs[o // 2][o % 2, 0, at : at + tall, :] = result[
                    o * tall : (o + 1) * tall, i * LANES : (i + 1) * LANES
                ]


def transform(pieces, mixing_t):
    _, fields, piece, _ = pieces[0][0].shape
    members = mixing_t.shape[0]
    return pl.pallas_call(
        transform_kernel,
        grid=(fields,),
        in_specs=[pl.BlockSpec((members, members), lambda i: (0, 0))] + piece_specs(pieces),
        out_specs=[pair_spec(piece)] * len(CHIPS),
        out_shape=[jax.ShapeDtypeStruct((2, fields, piece, LANES), jnp.float32)] * len(CHIPS),
        scratch_shapes=[
            pltpu.VMEM((members, members), jnp.bfloat16),
            pltpu.VMEM((members, members), jnp.bfloat16),
        ],
        compiler_params=pltpu.CompilerParams(vmem_limit_bytes=VMEM_LIMIT),
        cost_estimate=pl.CostEstimate(
            flops=fields * members * members * HEIGHT * LANES * 6,
            bytes_accessed=fields * members * HEIGHT * LANES * 8,
            transcendentals=0,
        ),
        name="transform",
    )(mixing_t, *arrays(pieces))


def unpack_kernel(members, rows, dest_ref, *refs):
    x_refs, out_ref, held = refs[:COUNT], refs[-2], refs[-1]
    pitch = rows + 4
    for i in range(COUNT):
        base = dest_ref[i] * HEIGHT
        for r in range(HEIGHT):
            held[pl.ds(base + r, members, stride=pitch), :] = x_refs[i][0, 0, r * members : (r + 1) * members, :]
    for m in range(members):
        out_ref[0, m * rows : (m + 1) * rows, :] = held[m * pitch : m * pitch + rows, :]


def unpack(pieces, so_far, dest, first, total, members, rows):
    _, fields, piece, _ = pieces[0][0].shape
    flat = members * rows
    more = () if so_far is None else (so_far,)
    return pl.pallas_call(
        functools.partial(unpack_kernel, members, rows),
        grid=(fields,),
        in_specs=[pl.BlockSpec(memory_space=pltpu.SMEM)]
        + piece_specs(pieces)
        + [pl.BlockSpec(memory_space=pl.ANY) for _ in more],
        out_specs=pl.BlockSpec((1, flat, LANES), lambda i: (first + i, 0, 0)),
        out_shape=jax.ShapeDtypeStruct((total, flat, LANES), jnp.float32),
        scratch_shapes=[pltpu.VMEM((members * (rows + 4), LANES), jnp.float32)],
        input_output_aliases={COUNT + 1: 0} if more else {},
        compiler_params=pltpu.CompilerParams(vmem_limit_bytes=VMEM_LIMIT),
        cost_estimate=pl.CostEstimate(
            flops=0, bytes_accessed=fields * flat * LANES * 8, transcendentals=0
        ),
        name="unpack",
    )(dest, *arrays(pieces), *more)


def hop(value, offset, sign):
    return lax.ppermute(value, "mem", [(i, shifted(i, offset, sign)) for i in range(COUNT)])


def travel(sent, sign, skip=0):
    return [
        value if chip == (0, 0) else hop(value, chip + (0,), sign)
        for value, chip in zip(sent, CHIPS[skip:])
    ]


def trade(arrived, group):
    return hop(jnp.concatenate([arrived[o][1:2] for o in group], axis=0), (0, 0, 1), 1)


def settled(arrived, traded):
    pieces = []
    for group, value in zip(GROUPS, traded):
        for at, o in enumerate(group):
            pieces += [(arrived[o], 0), (value, at)]
    return pieces


def spread_out(sent, sign):
    arrived = travel(sent, sign)
    return settled(arrived, [trade(arrived, group) for group in GROUPS])


def dot3(a, b, dims=(1, 0)):
    (ah, al), (bh, bl) = halves(a), halves(b)

    def one(u, v):
        return lax.dot_general(
            u, v, (((dims[0],), (dims[1],)), ((), ())), preferred_element_type=jnp.float32
        )

    return one(ah, bh) + (one(ah, bl) + one(al, bh))


def mixing_kernel(count_ref, raw_ref, value_ref, precision_ref, class_ref, out_ref):
    members, slots = raw_ref.shape
    raw = raw_ref[...]
    centre_obs = jnp.sum(raw, axis=0, keepdims=True) / members
    usable = iota((1, slots), 1) < count_ref[0]
    weight = jnp.where(usable, precision_ref[...] / (1.0 + class_ref[...].astype(jnp.float32)), 0.0)
    root_weight = jnp.sqrt(weight)
    spread = (raw - centre_obs) * root_weight
    small = dot3(spread, spread, (0, 0))
    inflation = members - 1.0
    scale = jnp.sqrt(
        inflation * inflation * members
        + 2.0 * inflation * jnp.sum(spread * spread, keepdims=True)
        + jnp.sum(small * small, keepdims=True)
    )
    eye = (iota((slots, slots), 0) == iota((slots, slots), 1)).astype(jnp.float32)
    start = inflation / scale
    y, z = start, jnp.ones_like(start)
    root_y = start * eye + small / scale
    factor = 1.5 * eye - 0.5 * root_y
    p = 1.5 - 0.5 * y
    root_z, part_z, z = factor, -0.5 * eye, p
    root_y, y = dot3(root_y, factor), y * p
    for iteration in range(1, NEWTON):
        both = dot3(jnp.concatenate([root_z, part_z], axis=0), root_y)
        part = z * (start * part_z + root_z) + both[slots:]
        factor = 1.5 * eye - 0.5 * both[:slots]
        p = 1.5 - 0.5 * z * y
        both = dot3(jnp.concatenate([factor, -0.5 * part], axis=0), root_z)
        if iteration + 1 < NEWTON:
            root_y, y = dot3(root_y, factor), y * p
        root_z, part_z, z = both[:slots], p * part_z + both[slots:], z * p
    driven = jnp.broadcast_to(root_weight * (value_ref[...] - centre_obs), (8, slots))
    driven = dot3(dot3(driven, root_z), root_z)
    shift = dot3(driven, spread, (1, 1))[0:1] / scale
    gain = jnp.sqrt(inflation / scale)
    low_rank = dot3(dot3(spread, part_z * (gain / scale)), spread, (1, 1))
    whole = iota((members, members), 0) == iota((members, members), 1)
    out_ref[...] = low_rank + jnp.where(whole, gain * z, 0.0) + shift


def mixing_transposed(raw_values, report_value, report_precision, report_class, slot_count):
    members, slots = raw_values.shape
    row = pl.BlockSpec((1, slots), lambda: (0, 0))
    return pl.pallas_call(
        mixing_kernel,
        in_specs=[
            pl.BlockSpec(memory_space=pltpu.SMEM),
            pl.BlockSpec((members, slots), lambda: (0, 0)),
            row,
            row,
            row,
        ],
        out_specs=pl.BlockSpec((members, members), lambda: (0, 0)),
        out_shape=jax.ShapeDtypeStruct((members, members), jnp.float32),
        compiler_params=pltpu.CompilerParams(vmem_limit_bytes=VMEM_LIMIT),
        cost_estimate=pl.CostEstimate(
            flops=NEWTON * 5 * 6 * slots**3, bytes_accessed=4 * members * members, transcendentals=0
        ),
        name="mixing",
    )(
        slot_count.reshape(1),
        raw_values,
        report_value[None, :],
        report_precision[None, :],
        report_class[None, :],
    )


def own_row(table, tile):
    flat_table = table.reshape((table.shape[0] * table.shape[1],) + table.shape[2:])
    return lax.dynamic_index_in_dim(flat_table, tile, 0, keepdims=False)


def on_device(
    prior_members,
    courant_x,
    courant_y,
    diffusion,
    report_level,
    report_cell,
    report_value,
    report_precision,
    report_class,
    report_count,
):
    total, members, rows, _ = prior_members.shape
    coefficients = (courant_x, courant_y, diffusion)
    tile = lax.axis_index("mem")
    dest = jnp.stack([shifted(tile, o) for o in OFFSETS]).astype(jnp.int32)
    half = total // 2

    def fields_sent(first, after=()):
        return list(
            forecast(prior_members, coefficients, packed[0], moved, dest, first, half, after)
        )

    packed = pack(prior_members, coefficients, 0, total)
    moved = exchange(packed)
    sent = fields_sent(0)
    arrived = travel(sent[:EARLY], 1)
    traded = [trade(arrived, GROUPS[0])]
    following = fields_sent(half, sent[:1])
    following, sent[EARLY:] = lax.optimization_barrier((following, sent[EARLY:]))
    arrived += travel(sent[EARLY:], 1, EARLY)
    traded += [trade(arrived, group) for group in GROUPS[1:]]
    sent = following
    traded, sent[EARLY:] = lax.optimization_barrier((traded, sent[EARLY:]))
    gathered = settled(arrived, traded)

    level, cell = own_row(report_level, tile), own_row(report_cell, tile)
    place = (level * (HEIGHT * LANES) + cell)[None, :]
    mixing_t = mixing_transposed(
        sample(gathered, place, sent[:1]),
        own_row(report_value, tile),
        own_row(report_precision, tile),
        own_row(report_class, tile),
        own_row(report_count, tile),
    )
    mixing_t, sent[EARLY:] = lax.optimization_barrier((mixing_t, sent[EARLY:]))
    analysed = list(transform(gathered, mixing_t))
    analysed, sent[LATE:] = lax.optimization_barrier((analysed, sent[LATE:]))
    gathered = spread_out(sent, 1)

    arrived = travel(analysed[:EARLY], -1)
    traded = [trade(arrived, GROUPS[0])]
    ready = list(transform(gathered, mixing_t))
    ready, analysed[EARLY:] = lax.optimization_barrier((ready, analysed[EARLY:]))
    arrived += travel(analysed[EARLY:], -1, EARLY)
    traded += [trade(arrived, group) for group in GROUPS[1:]]
    traded, ready[EARLY:] = lax.optimization_barrier((traded, ready[EARLY:]))
    returned = [settled(arrived, traded), spread_out(ready, -1)]
    result = unpack(returned[0], None, dest, 0, total, members, rows)
    result = unpack(returned[1], result, dest, half, total, members, rows)
    return result.reshape(prior_members.shape)


def solution(mesh):
    in_specs = (
        P(None, "mem", "gx", "gy"),
        P("gx", "gy"),
        P("gx", "gy"),
        P("gx", "gy"),
        P("gx", "gy", None),
        P("gx", "gy", None),
        P("gx", "gy", None),
        P("gx", "gy", None),
        P("gx", "gy", None),
        P("gx", "gy"),
    )
    out_specs = P(None, "mem", "gx", "gy")
    return jax.shard_map(
        on_device, mesh=mesh, in_specs=in_specs, out_specs=out_specs, check_vma=False
    )
```

```python
import functools

import jax
import jax.numpy as jnp
from jax import lax
from jax.experimental import pallas as pl
from jax.experimental.pallas import tpu as pltpu
from jax.sharding import PartitionSpec as P

NEWTON = 8
LANES = 128
VMEM_LIMIT = 60 * 1024 * 1024
PACK_LIMIT = 60 * 1024 * 1024


def iota(shape, dim):
    return lax.broadcasted_iota(jnp.int32, shape, dim)


HEIGHT = 4
SPREAD = 32
PITCH = 8
CHIPS = ((0, 0), (1, 0), (0, 2), (1, 1), (0, 3), (1, 3), (0, 1), (1, 2))
OFFSETS = tuple(chip + (core,) for chip in CHIPS for core in range(2))
COUNT = len(OFFSETS)
EARLY, LATE = 5, 7
GROUPS = ((0,), (1, 2), (3, 4), (5, 6), (7,))


def shifted(index, offset, sign=1):
    z, y, core = index // 8, index // 2 % 4, index % 2
    dz, dy, dc = offset
    return (z + dz) % 2 * 8 + (y + sign * dy + 4) % 4 * 2 + (core + dc) % 2


def pair_spec(piece, count=2):
    return pl.BlockSpec((count, 1, piece, LANES), lambda i, *_: (0, i, 0, 0))


def piece_specs(pieces):
    def spec(array, lead):
        return pl.BlockSpec((1, 1) + array.shape[2:], lambda i: (lead, i, 0, 0))

    return [spec(*p) for p in pieces]


def arrays(pieces):
    return [p[0] for p in pieces]


def pack_kernel(first, fields, rows, members, x_ref, cx_ref, cy_ref, df_ref, *refs):
    edge_ref, row_ref, corner_ref, held, sems = refs[-5:]
    step = pl.program_id(0)
    pitch = rows + PITCH
    picked = (0, 1, rows - 2, rows - 1)
    groups = rows // SPREAD

    def copy(field):
        return pltpu.make_async_copy(
            x_ref.at[first + field], held.at[field, :, pl.ds(0, rows), :], sems.at[field]
        )

    @pl.when(step == 0)
    def _():
        for field in range(fields):
            copy(field).start()

    def gather(read, tall):
        lane = iota((tall, LANES), 1)
        packed = []
        for group in range(groups):
            parts = [jnp.zeros((tall, LANES), jnp.float32) for _ in range(4)]
            for i in range(SPREAD):
                moved = pltpu.roll(read(group * SPREAD + i), (4 * i + 2) % LANES, 1)
                parts[i % 4] = jnp.where(lane // 4 == i, moved, parts[i % 4])
            packed.append((parts[0] + parts[1]) + (parts[2] + parts[3]))
            edge_ref[0, group, 0:tall, :] = packed[group]
        corner_ref[0, 0:tall, :] = jnp.where(lane < LANES // 2, packed[0], packed[-1])

    for field in range(fields):

        @pl.when(step == field)
        def _():
            copy(field).wait()
            flat = held.at[field].reshape(members * pitch, LANES)

            def read(row):
                value = flat[pl.ds(row, members, stride=pitch), :]
                if row in picked:
                    row_ref[0, picked.index(row)] = value
                return value

            gather(read, members)

    @pl.when(step == fields)
    def _():
        sub = iota((8, LANES), 0)
        row_ref[0] = jnp.zeros((4, members, LANES), jnp.float32)
        edge_ref[0] = jnp.zeros((groups, members, LANES), jnp.float32)
        corner_ref[0] = jnp.zeros((members, LANES), jnp.float32)

        def read(row):
            at = slice(row, row + 1)
            value = jnp.where(
                sub == 0, cx_ref[at, :], jnp.where(sub == 1, cy_ref[at, :], df_ref[at, :])
            )
            if row in picked:
                row_ref[0, picked.index(row), 0:8, :] = value
            return value

        gather(read, 8)


def pack(x, coefficients, first, fields, after=()):
    _, members, rows, _ = x.shape
    small = pl.BlockSpec((rows, LANES), lambda i: (0, 0))
    groups = rows // SPREAD
    return pl.pallas_call(
        functools.partial(pack_kernel, first, fields, rows, members),
        grid=(fields + 1,),
        in_specs=[pl.BlockSpec(memory_space=pl.ANY), small, small, small]
        + [pl.BlockSpec(memory_space=pl.ANY) for _ in after],
        out_specs=[
            pl.BlockSpec((1, groups, members, LANES), lambda i: (i, 0, 0, 0)),
            pl.BlockSpec((1, 4, members, LANES), lambda i: (i, 0, 0, 0)),
            pl.BlockSpec((1, members, LANES), lambda i: (i, 0, 0)),
        ],
        out_shape=[
            jax.ShapeDtypeStruct((fields + 1, groups, members, LANES), jnp.float32),
            jax.ShapeDtypeStruct((fields + 1, 4, members, LANES), jnp.float32),
            jax.ShapeDtypeStruct((fields + 1, members, LANES), jnp.float32),
        ],
        scratch_shapes=[
            pltpu.VMEM((fields, members, rows + PITCH, LANES), jnp.float32),
            pltpu.SemaphoreType.DMA((fields,)),
        ],
        compiler_params=pltpu.CompilerParams(vmem_limit_bytes=PACK_LIMIT),
        cost_estimate=pl.CostEstimate(
            flops=fields * members * rows * LANES * 2,
            bytes_accessed=fields * members * rows * LANES * 8,
            transcendentals=0,
        ),
        name="pack_edges",
    )(x, *coefficients, *after)


def exchange(packed):
    edge, row, corner = packed
    nx, ny = lax.axis_size("gx"), lax.axis_size("gy")
    right = [(i, (i + 1) % ny) for i in range(ny)]
    left = [(i, (i - 1) % ny) for i in range(ny)]

    def diagonal(step):
        return [
            (a * ny + b, ((a + 1) % nx) * ny + (b + step) % ny) for a in range(nx) for b in range(ny)
        ]

    return (
        lax.ppermute(row, "gx", [(i, (i + 1) % nx) for i in range(nx)]),
        lax.ppermute(edge, "gy", right),
        lax.ppermute(edge, "gy", left),
        lax.ppermute(corner, ("gx", "gy"), diagonal(1)),
        lax.ppermute(corner, ("gx", "gy"), diagonal(-1)),
    )


def weights_of(cx, cy, spread):
    plus_x, minus_x = jnp.maximum(cx, 0.0), jnp.minimum(cx, 0.0)
    plus_y, minus_y = jnp.maximum(cy, 0.0), jnp.minimum(cy, 0.0)
    centre = 1.0 - (plus_x - minus_x) - (plus_y - minus_y) - 4.0 * spread
    return centre, plus_x + spread, spread - minus_x, plus_y + spread, spread - minus_y


def stencil(k, centre, west, east, south, north):
    return k[0] * centre + k[1] * west + k[2] * east + k[3] * south + k[4] * north


def forecast_kernel(first, fields, rows, members, outs, dest_ref, x_hbm, cx_ref, cy_ref, df_ref, own_ref, left_ref, right_ref, left_k_ref, right_k_ref, row_ref, row_k_ref, dl_ref, dr_ref, *refs):
    k_main, k_edge, k_row, edge_s, first_s, x_s, second_s, beside_s, held, sems = refs[-10:]
    out_refs = refs[-10 - outs : -10]
    step = pl.program_id(0)
    pitch = rows + PITCH

    def copy(field):
        slot = lax.rem(field, 2)
        return pltpu.make_async_copy(
            x_hbm.at[first + field], held.at[slot, :, pl.ds(0, rows), :], sems.at[slot]
        )

    @pl.when(step == 0)
    def _():
        copy(step).start()

    @pl.when(step + 1 < fields)
    def _():
        copy(step + 1).start()

    copy(step).wait()
    flat = held.at[lax.rem(step, 2)].reshape(members * pitch, LANES)
    for row in range(rows):
        x_s[row] = flat[pl.ds(row, members, stride=pitch), :]
    lane = iota((members, LANES), 1)
    from_left = lane % 4 < 2
    groups = rows // SPREAD

    @pl.when(pl.program_id(0) == 0)
    def _():
        for i, w in enumerate(weights_of(cx_ref[...], cy_ref[...], df_ref[...])):
            k_main[i] = w
        for group in range(groups):
            both = jnp.where(from_left[0:8], left_k_ref[0, group, 0:8, :], right_k_ref[0, group, 0:8, :])
            for i, w in enumerate(weights_of(*[both[j : j + 1, :] for j in range(3)])):
                k_edge[group, i : i + 1, :] = w
        for side, at in ((0, 3), (1, 0)):
            for i, w in enumerate(weights_of(*[row_k_ref[0, at, j : j + 1, :] for j in range(3)])):
                k_row[side, i : i + 1, :] = w

    edges = [jnp.where(from_left, left_ref[0, g], right_ref[0, g]) for g in range(groups)]
    corner = jnp.where(from_left, dl_ref[0], dr_ref[0])
    chain = [corner] + edges + [corner]
    up = [pltpu.roll(v, 4, 1) for v in chain]
    down = [pltpu.roll(v, LANES - 4, 1) for v in chain]
    for group, edge in enumerate(edges):
        own = own_ref[0, group]
        edge_s[0, group] = edge
        edge_s[1, group] = stencil(
            [k_edge[group, i : i + 1, :] for i in range(5)],
            edge,
            jnp.where(lane < 4, up[group], up[group + 1]),
            jnp.where(lane >= LANES - 4, down[group + 2], down[group + 1]),
            pltpu.roll(jnp.where(lane % 4 == 0, edge, own), 1, 1),
            pltpu.roll(jnp.where(lane % 4 == 3, edge, own), LANES - 1, 1),
        )

    def sides(centre, beside):
        return (
            pltpu.roll(jnp.where(lane == LANES - 1, beside, centre), 1, 1),
            pltpu.roll(jnp.where(lane == 0, beside, centre), LANES - 1, 1),
        )

    for side, (centre, west, east, turn, at) in enumerate(
        (
            (row_ref[0, 3], row_ref[0, 2], x_s[0], 2, 0),
            (row_ref[0, 0], x_s[rows - 1], row_ref[0, 1], LANES - 2, rows + 1),
        )
    ):
        k = [k_row[side, i : i + 1, :] for i in range(5)]
        first_s[at] = stencil(k, centre, west, east, *sides(centre, pltpu.roll(corner, turn, 1)))

    def lay_sides(stage):
        for row in range(rows):
            turn = (126 - row % SPREAD * 4) % LANES
            beside_s[row] = pltpu.roll(edge_s[stage, row // SPREAD], turn, 1)

    def one(row, centre, west, east):
        k = [k_main[i, row : row + 1, :] for i in range(5)]
        return stencil(k, centre, west, east, *sides(centre, beside_s[row]))

    lay_sides(0)
    for row in range(rows):
        west = row_ref[0, 3] if row == 0 else x_s[row - 1]
        east = row_ref[0, 0] if row == rows - 1 else x_s[row + 1]
        first_s[row + 1] = one(row, x_s[row], west, east)
    lay_sides(1)
    for row in range(rows):
        second_s[row] = one(row, first_s[row + 1], first_s[row], first_s[row + 2])
    for i in range(COUNT):
        base = dest_ref[i] * HEIGHT
        for r in range(HEIGHT):
            if outs == 1:
                out_refs[0][i, 0, r * members : (r + 1) * members, :] = second_s[i * HEIGHT + r]
            else:
                out_refs[i // 2][i % 2, 0, r * members : (r + 1) * members, :] = second_s[base + r]


def forecast(x, coefficients, edge, moved, dest, first, fields, after, outs):
    _, members, rows, _ = x.shape
    row, left, right, corner_l, corner_r = moved
    last = row.shape[0] - 1
    groups = rows // SPREAD
    small = pl.BlockSpec((rows, LANES), lambda i: (0, 0))
    edge_spec = pl.BlockSpec((1, groups, members, LANES), lambda i: (first + i, 0, 0, 0))
    edge_last = pl.BlockSpec((1, groups, members, LANES), lambda i: (last, 0, 0, 0))
    corner_spec = pl.BlockSpec((1, members, LANES), lambda i: (first + i, 0, 0))
    piece = HEIGHT * members
    return pl.pallas_call(
        functools.partial(forecast_kernel, first, fields, rows, members, outs),
        grid=(fields,),
        in_specs=[
            pl.BlockSpec(memory_space=pltpu.SMEM),
            pl.BlockSpec(memory_space=pl.ANY),
            small,
            small,
            small,
            edge_spec,
            edge_spec,
            edge_spec,
            edge_last,
            edge_last,
            pl.BlockSpec((1, 4, members, LANES), lambda i: (first + i, 0, 0, 0)),
            pl.BlockSpec((1, 4, members, LANES), lambda i: (last, 0, 0, 0)),
            corner_spec,
            corner_spec,
        ]
        + [pl.BlockSpec(memory_space=pl.ANY) for _ in after],
        out_specs=[pair_spec(piece, COUNT if outs == 1 else 2)] * outs,
        out_shape=[
            jax.ShapeDtypeStruct((COUNT if outs == 1 else 2, fields, piece, LANES), jnp.float32)
        ]
        * outs,
        scratch_shapes=[
            pltpu.VMEM((5, rows, LANES), jnp.float32),
            pltpu.VMEM((groups, 8, LANES), jnp.float32),
            pltpu.VMEM((2, 8, LANES), jnp.float32),
            pltpu.VMEM((2, groups, members, LANES), jnp.float32),
            pltpu.VMEM((rows + 2, members, LANES), jnp.float32),
            pltpu.VMEM((rows, members, LANES), jnp.float32),
            pltpu.VMEM((rows, members, LANES), jnp.float32),
            pltpu.VMEM((rows, members, LANES), jnp.float32),
            pltpu.VMEM((2, members, rows + PITCH, LANES), jnp.float32),
            pltpu.SemaphoreType.DMA((2,)),
        ],
        compiler_params=pltpu.CompilerParams(vmem_limit_bytes=PACK_LIMIT),
        cost_estimate=pl.CostEstimate(
            flops=fields * rows * members * LANES * 18,
            bytes_accessed=fields * rows * members * LANES * 8,
            transcendentals=0,
        ),
        name="forecast",
    )(dest, x, *coefficients, edge, left, right, left, right, row, row, corner_l, corner_r, *after)


def halves(value):
    high = value.astype(jnp.bfloat16)
    return high, (value - high.astype(jnp.float32)).astype(jnp.bfloat16)


def dot(a, b):
    return jnp.dot(a, b, preferred_element_type=jnp.float32)


def tile_rows(refs, r):
    tall = refs[0].shape[2] // HEIGHT
    return jnp.concatenate([ref[0, 0, r * tall : (r + 1) * tall, :] for ref in refs], axis=0)


def sample_kernel(place_ref, *refs):
    step = pl.program_id(0)
    x_refs, out_ref = refs[:COUNT], refs[-1]
    slots = place_ref.shape[1]
    cells = HEIGHT * LANES
    x = jnp.concatenate([tile_rows(x_refs, r) for r in range(HEIGHT)], axis=1)
    chosen = (iota((cells, slots), 0) + step * cells == place_ref[0:1, :]).astype(jnp.bfloat16)
    high = x.astype(jnp.bfloat16)
    middle, low = halves(x - high.astype(jnp.float32))
    got = dot(high, chosen) + dot(middle, chosen) + dot(low, chosen)

    @pl.when(step == 0)
    def _():
        out_ref[...] = got

    @pl.when(step > 0)
    def _():
        out_ref[...] += got


def sample(pieces, place, after):
    _, fields, piece, _ = pieces[0][0].shape
    members = COUNT * piece // HEIGHT
    slots = place.shape[1]
    return pl.pallas_call(
        sample_kernel,
        grid=(fields,),
        in_specs=[pl.BlockSpec((1, slots), lambda i: (0, 0))]
        + piece_specs(pieces)
        + [pl.BlockSpec(memory_space=pl.ANY) for _ in after],
        out_specs=pl.BlockSpec((members, slots), lambda i: (0, 0)),
        out_shape=jax.ShapeDtypeStruct((members, slots), jnp.float32),
        compiler_params=pltpu.CompilerParams(vmem_limit_bytes=VMEM_LIMIT),
        cost_estimate=pl.CostEstimate(
            flops=fields * members * HEIGHT * LANES * slots * 6,
            bytes_accessed=fields * members * HEIGHT * LANES * 4,
            transcendentals=0,
        ),
        name="sample",
    )(place, *arrays(pieces), *after)


def transform_kernel(places_ref, mix_ref, *refs):
    x_refs, out_refs, (high_s, low_s) = refs[:COUNT], refs[COUNT:-2], refs[-2:]

    @pl.when(pl.program_id(0) == 0)
    def _():
        high_s[...], low_s[...] = halves(mix_ref[...])

    tall = x_refs[0].shape[2] // HEIGHT
    members = COUNT * tall
    for half in range(HEIGHT // 2):
        x = jnp.concatenate([tile_rows(x_refs, 2 * half + i) for i in range(2)], axis=1)
        centre = jnp.sum(x, axis=0, keepdims=True) / members
        high, low = halves(x - centre)
        result = dot(high_s[...], high) + (dot(high_s[...], low) + dot(low_s[...], high)) + centre
        for i in range(2):
            at = (2 * half + i) * tall
            for o in range(COUNT):
                out_refs[o // 2][o % 2, 0, at : at + tall, :] = result[
                    o * tall : (o + 1) * tall, i * LANES : (i + 1) * LANES
                ]


def transform(pieces, mixing_t, places):
    _, fields, piece, _ = pieces[0].shape
    members = mixing_t.shape[0]

    def spec(i):
        return pl.BlockSpec((1, 1, piece, LANES), lambda f, at: (at[i], f, 0, 0))

    return pl.pallas_call(
        transform_kernel,
        grid_spec=pltpu.PrefetchScalarGridSpec(
            num_scalar_prefetch=1,
            grid=(fields,),
            in_specs=[pl.BlockSpec((members, members), lambda f, at: (0, 0))]
            + [spec(i) for i in range(COUNT)],
            out_specs=[pair_spec(piece)] * len(CHIPS),
            scratch_shapes=[
                pltpu.VMEM((members, members), jnp.bfloat16),
                pltpu.VMEM((members, members), jnp.bfloat16),
            ],
        ),
        out_shape=[jax.ShapeDtypeStruct((2, fields, piece, LANES), jnp.float32)] * len(CHIPS),
        compiler_params=pltpu.CompilerParams(vmem_limit_bytes=VMEM_LIMIT),
        cost_estimate=pl.CostEstimate(
            flops=fields * members * members * HEIGHT * LANES * 6,
            bytes_accessed=fields * members * HEIGHT * LANES * 8,
            transcendentals=0,
        ),
        name="transform",
    )(places, mixing_t, *pieces)


def unpack_kernel(members, rows, dest_ref, *refs):
    x_refs, out_ref, held = refs[:COUNT], refs[-2], refs[-1]
    pitch = rows + 4
    for i in range(COUNT):
        base = dest_ref[i] * HEIGHT
        for r in range(HEIGHT):
            held[pl.ds(base + r, members, stride=pitch), :] = x_refs[i][0, 0, r * members : (r + 1) * members, :]
    for m in range(members):
        out_ref[0, m * rows : (m + 1) * rows, :] = held[m * pitch : m * pitch + rows, :]


def unpack(pieces, so_far, dest, first, total, members, rows):
    _, fields, piece, _ = pieces[0][0].shape
    flat = members * rows
    more = () if so_far is None else (so_far,)
    return pl.pallas_call(
        functools.partial(unpack_kernel, members, rows),
        grid=(fields,),
        in_specs=[pl.BlockSpec(memory_space=pltpu.SMEM)]
        + piece_specs(pieces)
        + [pl.BlockSpec(memory_space=pl.ANY) for _ in more],
        out_specs=pl.BlockSpec((1, flat, LANES), lambda i: (first + i, 0, 0)),
        out_shape=jax.ShapeDtypeStruct((total, flat, LANES), jnp.float32),
        scratch_shapes=[pltpu.VMEM((members * (rows + 4), LANES), jnp.float32)],
        input_output_aliases={COUNT + 1: 0} if more else {},
        compiler_params=pltpu.CompilerParams(vmem_limit_bytes=VMEM_LIMIT),
        cost_estimate=pl.CostEstimate(
            flops=0, bytes_accessed=fields * flat * LANES * 8, transcendentals=0
        ),
        name="unpack",
    )(dest, *arrays(pieces), *more)


def hop(value, offset, sign):
    return lax.ppermute(value, "mem", [(i, shifted(i, offset, sign)) for i in range(COUNT)])


def travel(sent, sign, skip=0):
    return [
        value if chip == (0, 0) else hop(value, chip + (0,), sign)
        for value, chip in zip(sent, CHIPS[skip:])
    ]


def trade(arrived, group):
    return hop(jnp.concatenate([arrived[o][1:2] for o in group], axis=0), (0, 0, 1), 1)


def settled(arrived, traded):
    pieces = []
    for group, value in zip(GROUPS, traded):
        for at, o in enumerate(group):
            pieces += [(arrived[o], 0), (value, at)]
    return pieces


def spread_out(sent, sign):
    arrived = travel(sent, sign)
    return settled(arrived, [trade(arrived, group) for group in GROUPS])


def dot3(a, b, dims=(1, 0)):
    (ah, al), (bh, bl) = halves(a), halves(b)

    def one(u, v):
        return lax.dot_general(
            u, v, (((dims[0],), (dims[1],)), ((), ())), preferred_element_type=jnp.float32
        )

    return one(ah, bh) + (one(ah, bl) + one(al, bh))


def mixing_kernel(count_ref, raw_ref, value_ref, precision_ref, class_ref, out_ref):
    members, slots = raw_ref.shape
    raw = raw_ref[...]
    centre_obs = jnp.sum(raw, axis=0, keepdims=True) / members
    usable = iota((1, slots), 1) < count_ref[0]
    weight = jnp.where(usable, precision_ref[...] / (1.0 + class_ref[...].astype(jnp.float32)), 0.0)
    root_weight = jnp.sqrt(weight)
    spread = (raw - centre_obs) * root_weight
    small = dot3(spread, spread, (0, 0))
    inflation = members - 1.0
    scale = jnp.sqrt(
        inflation * inflation * members
        + 2.0 * inflation * jnp.sum(spread * spread, keepdims=True)
        + jnp.sum(small * small, keepdims=True)
    )
    eye = (iota((slots, slots), 0) == iota((slots, slots), 1)).astype(jnp.float32)
    start = inflation / scale
    y, z = start, jnp.ones_like(start)
    root_y = start * eye + small / scale
    factor = 1.5 * eye - 0.5 * root_y
    p = 1.5 - 0.5 * y
    root_z, part_z, z = factor, -0.5 * eye, p
    root_y, y = dot3(root_y, factor), y * p
    for iteration in range(1, NEWTON):
        both = dot3(jnp.concatenate([root_z, part_z], axis=0), root_y)
        part = z * (start * part_z + root_z) + both[slots:]
        factor = 1.5 * eye - 0.5 * both[:slots]
        p = 1.5 - 0.5 * z * y
        both = dot3(jnp.concatenate([factor, -0.5 * part], axis=0), root_z)
        if iteration + 1 < NEWTON:
            root_y, y = dot3(root_y, factor), y * p
        root_z, part_z, z = both[:slots], p * part_z + both[slots:], z * p
    driven = jnp.broadcast_to(root_weight * (value_ref[...] - centre_obs), (8, slots))
    driven = dot3(dot3(driven, root_z), root_z)
    shift = dot3(driven, spread, (1, 1))[0:1] / scale
    gain = jnp.sqrt(inflation / scale)
    low_rank = dot3(dot3(spread, part_z * (gain / scale)), spread, (1, 1))
    whole = iota((members, members), 0) == iota((members, members), 1)
    out_ref[...] = low_rank + jnp.where(whole, gain * z, 0.0) + shift


def mixing_transposed(raw_values, report_value, report_precision, report_class, slot_count):
    members, slots = raw_values.shape
    row = pl.BlockSpec((1, slots), lambda: (0, 0))
    return pl.pallas_call(
        mixing_kernel,
        in_specs=[
            pl.BlockSpec(memory_space=pltpu.SMEM),
            pl.BlockSpec((members, slots), lambda: (0, 0)),
            row,
            row,
            row,
        ],
        out_specs=pl.BlockSpec((members, members), lambda: (0, 0)),
        out_shape=jax.ShapeDtypeStruct((members, members), jnp.float32),
        compiler_params=pltpu.CompilerParams(vmem_limit_bytes=VMEM_LIMIT),
        cost_estimate=pl.CostEstimate(
            flops=NEWTON * 5 * 6 * slots**3, bytes_accessed=4 * members * members, transcendentals=0
        ),
        name="mixing",
    )(
        slot_count.reshape(1),
        raw_values,
        report_value[None, :],
        report_precision[None, :],
        report_class[None, :],
    )


def own_row(table, tile):
    flat_table = table.reshape((table.shape[0] * table.shape[1],) + table.shape[2:])
    return lax.dynamic_index_in_dim(flat_table, tile, 0, keepdims=False)


def on_device(
    prior_members,
    courant_x,
    courant_y,
    diffusion,
    report_level,
    report_cell,
    report_value,
    report_precision,
    report_class,
    report_count,
):
    total, members, rows, _ = prior_members.shape
    coefficients = (courant_x, courant_y, diffusion)
    tile = lax.axis_index("mem")
    dest = jnp.stack([shifted(tile, o) for o in OFFSETS]).astype(jnp.int32)
    half = total // 2

    source = jnp.stack([shifted(tile, o, -1) for o in OFFSETS]).astype(jnp.int32)
    packed = pack(prior_members, coefficients, 0, total)
    moved = exchange(packed)

    def fields_sent(first, after, outs):
        return list(
            forecast(prior_members, coefficients, packed[0], moved, dest, first, half, after, outs)
        )

    sent = fields_sent(0, (), len(CHIPS))
    arrived = travel(sent[:EARLY], 1)
    traded = [trade(arrived, GROUPS[0])]
    following = fields_sent(half, arrived[1:2], 1)
    following, sent[EARLY:] = lax.optimization_barrier((following, sent[EARLY:]))
    arrived += travel(sent[EARLY:], 1, EARLY)
    following, arrived[1:] = lax.optimization_barrier((following, arrived[1:]))
    traded += [trade(arrived, group) for group in GROUPS[1:]]
    second = lax.all_to_all(following[0], "mem", split_axis=0, concat_axis=0, tiled=True)
    gathered = settled(arrived, traded)

    level, cell = own_row(report_level, tile), own_row(report_cell, tile)
    place = (level * (HEIGHT * LANES) + cell)[None, :]
    mixing_t = mixing_transposed(
        sample(gathered, place, following),
        own_row(report_value, tile),
        own_row(report_precision, tile),
        own_row(report_class, tile),
        own_row(report_count, tile),
    )
    leads = jnp.array([p[1] for p in gathered], jnp.int32)
    analysed = list(transform(arrays(gathered), mixing_t, leads))

    arrived = travel(analysed[:EARLY], -1)
    traded = [trade(arrived, GROUPS[0])]
    ready = list(transform([second] * COUNT, mixing_t, source))
    ready, analysed[EARLY:] = lax.optimization_barrier((ready, analysed[EARLY:]))
    arrived += travel(analysed[EARLY:], -1, EARLY)
    traded += [trade(arrived, group) for group in GROUPS[1:]]
    traded, ready[EARLY:] = lax.optimization_barrier((traded, ready[EARLY:]))
    result = unpack(settled(arrived, traded), None, dest, 0, total, members, rows)
    result, ready[LATE:] = lax.optimization_barrier((result, ready[LATE:]))
    result = unpack(spread_out(ready, -1), result, dest, half, total, members, rows)
    return result.reshape(prior_members.shape)


def solution(mesh):
    in_specs = (
        P(None, "mem", "gx", "gy"),
        P("gx", "gy"),
        P("gx", "gy"),
        P("gx", "gy"),
        P("gx", "gy", None),
        P("gx", "gy", None),
        P("gx", "gy", None),
        P("gx", "gy", None),
        P("gx", "gy", None),
        P("gx", "gy"),
    )
    out_specs = P(None, "mem", "gx", "gy")
    return jax.shard_map(
        on_device, mesh=mesh, in_specs=in_specs, out_specs=out_specs, check_vma=False
    )
```

```python
import functools

import jax
import jax.numpy as jnp
from jax import lax
from jax.experimental import pallas as pl
from jax.experimental.pallas import tpu as pltpu
from jax.sharding import PartitionSpec as P

NEWTON = 8
LANES = 128
VMEM_LIMIT = 60 * 1024 * 1024
PACK_LIMIT = 60 * 1024 * 1024


def iota(shape, dim):
    return lax.broadcasted_iota(jnp.int32, shape, dim)


HEIGHT = 4
SPREAD = 32
PITCH = 8
CHIPS = ((0, 0), (1, 0), (0, 2), (1, 1), (0, 3), (1, 3), (0, 1), (1, 2))
OFFSETS = tuple(chip + (core,) for chip in CHIPS for core in range(2))
COUNT = len(OFFSETS)
EARLY, LATE = 5, 7
GROUPS = ((0,), (1, 2), (3, 4), (5, 6), (7,))


def shifted(index, offset, sign=1):
    z, y, core = index // 8, index // 2 % 4, index % 2
    dz, dy, dc = offset
    return (z + dz) % 2 * 8 + (y + sign * dy + 4) % 4 * 2 + (core + dc) % 2


def pair_spec(piece, count=2):
    return pl.BlockSpec((count, 1, piece, LANES), lambda i, *_: (0, i, 0, 0))


def piece_specs(pieces):
    def spec(array, lead):
        return pl.BlockSpec((1, 1) + array.shape[2:], lambda i: (lead, i, 0, 0))

    return [spec(*p) for p in pieces]


def arrays(pieces):
    return [p[0] for p in pieces]


def pack_kernel(first, fields, rows, members, x_ref, cx_ref, cy_ref, df_ref, *refs):
    edge_ref, row_ref, corner_ref, held, sems = refs[-5:]
    step = pl.program_id(0)
    pitch = rows + PITCH
    picked = (0, 1, rows - 2, rows - 1)
    groups = rows // SPREAD

    def copy(field):
        return pltpu.make_async_copy(
            x_ref.at[first + field], held.at[field, :, pl.ds(0, rows), :], sems.at[field]
        )

    @pl.when(step == 0)
    def _():
        for field in range(fields):
            copy(field).start()

    def gather(read, tall):
        lane = iota((tall, LANES), 1)
        packed = []
        for group in range(groups):
            parts = [jnp.zeros((tall, LANES), jnp.float32) for _ in range(4)]
            for i in range(SPREAD):
                moved = pltpu.roll(read(group * SPREAD + i), (4 * i + 2) % LANES, 1)
                parts[i % 4] = jnp.where(lane // 4 == i, moved, parts[i % 4])
            packed.append((parts[0] + parts[1]) + (parts[2] + parts[3]))
            edge_ref[0, group, 0:tall, :] = packed[group]
        return packed

    for field in range(fields):

        @pl.when(step == field)
        def _():
            copy(field).wait()
            flat = held.at[field].reshape(members * pitch, LANES)

            def read(row):
                value = flat[pl.ds(row, members, stride=pitch), :]
                if row in picked:
                    row_ref[0, picked.index(row)] = value
                return value

            packed = gather(read, members)
            lane = iota((members, LANES), 1)
            top = pltpu.roll(packed[0], 8 * field % LANES, 1)
            bottom = pltpu.roll(packed[-1], (8 * field + 8) % LANES, 1)
            corner = jnp.where(lane % 8 < 4, top, bottom)
            before = jnp.zeros_like(corner) if field == 0 else corner_ref[...]
            corner_ref[...] = jnp.where(lane // 8 == field, corner, before)

    @pl.when(step == fields)
    def _():
        sub = iota((8, LANES), 0)
        row_ref[0] = jnp.zeros((4, members, LANES), jnp.float32)
        edge_ref[0] = jnp.zeros((groups, members, LANES), jnp.float32)

        def read(row):
            at = slice(row, row + 1)
            value = jnp.where(
                sub == 0, cx_ref[at, :], jnp.where(sub == 1, cy_ref[at, :], df_ref[at, :])
            )
            if row in picked:
                row_ref[0, picked.index(row), 0:8, :] = value
            return value

        gather(read, 8)


def pack(x, coefficients, first, fields, after=()):
    _, members, rows, _ = x.shape
    small = pl.BlockSpec((rows, LANES), lambda i: (0, 0))
    groups = rows // SPREAD
    return pl.pallas_call(
        functools.partial(pack_kernel, first, fields, rows, members),
        grid=(fields + 1,),
        in_specs=[pl.BlockSpec(memory_space=pl.ANY), small, small, small]
        + [pl.BlockSpec(memory_space=pl.ANY) for _ in after],
        out_specs=[
            pl.BlockSpec((1, groups, members, LANES), lambda i: (i, 0, 0, 0)),
            pl.BlockSpec((1, 4, members, LANES), lambda i: (i, 0, 0, 0)),
            pl.BlockSpec((members, LANES), lambda i: (0, 0)),
        ],
        out_shape=[
            jax.ShapeDtypeStruct((fields + 1, groups, members, LANES), jnp.float32),
            jax.ShapeDtypeStruct((fields + 1, 4, members, LANES), jnp.float32),
            jax.ShapeDtypeStruct((members, LANES), jnp.float32),
        ],
        scratch_shapes=[
            pltpu.VMEM((fields, members, rows + PITCH, LANES), jnp.float32),
            pltpu.SemaphoreType.DMA((fields,)),
        ],
        compiler_params=pltpu.CompilerParams(vmem_limit_bytes=PACK_LIMIT),
        cost_estimate=pl.CostEstimate(
            flops=fields * members * rows * LANES * 2,
            bytes_accessed=fields * members * rows * LANES * 8,
            transcendentals=0,
        ),
        name="pack_edges",
    )(x, *coefficients, *after)


def exchange(packed):
    edge, row, corner = packed
    nx, ny = lax.axis_size("gx"), lax.axis_size("gy")
    right = [(i, (i + 1) % ny) for i in range(ny)]
    left = [(i, (i - 1) % ny) for i in range(ny)]

    def diagonal(step):
        return [
            (a * ny + b, ((a + 1) % nx) * ny + (b + step) % ny) for a in range(nx) for b in range(ny)
        ]

    return (
        lax.ppermute(row, "gx", [(i, (i + 1) % nx) for i in range(nx)]),
        lax.ppermute(edge, "gy", right),
        lax.ppermute(edge, "gy", left),
        lax.ppermute(corner, ("gx", "gy"), diagonal(1)),
        lax.ppermute(corner, ("gx", "gy"), diagonal(-1)),
    )


def weights_of(cx, cy, spread):
    plus_x, minus_x = jnp.maximum(cx, 0.0), jnp.minimum(cx, 0.0)
    plus_y, minus_y = jnp.maximum(cy, 0.0), jnp.minimum(cy, 0.0)
    centre = 1.0 - (plus_x - minus_x) - (plus_y - minus_y) - 4.0 * spread
    return centre, plus_x + spread, spread - minus_x, plus_y + spread, spread - minus_y


def stencil(k, centre, west, east, south, north):
    return k[0] * centre + k[1] * west + k[2] * east + k[3] * south + k[4] * north


def forecast_kernel(first, fields, rows, members, outs, dest_ref, x_hbm, cx_ref, cy_ref, df_ref, own_ref, left_ref, right_ref, left_k_ref, right_k_ref, row_ref, row_k_ref, dl_ref, dr_ref, *refs):
    k_main, k_edge, k_row, edge_s, first_s, x_s, second_s, beside_s, held, sems = refs[-10:]
    out_refs = refs[-10 - outs : -10]
    step = pl.program_id(0)
    pitch = rows + PITCH

    def copy(field):
        slot = lax.rem(field, 2)
        return pltpu.make_async_copy(
            x_hbm.at[first + field], held.at[slot, :, pl.ds(0, rows), :], sems.at[slot]
        )

    @pl.when(step == 0)
    def _():
        copy(step).start()

    @pl.when(step + 1 < fields)
    def _():
        copy(step + 1).start()

    copy(step).wait()
    flat = held.at[lax.rem(step, 2)].reshape(members * pitch, LANES)
    for row in range(rows):
        x_s[row] = flat[pl.ds(row, members, stride=pitch), :]
    lane = iota((members, LANES), 1)
    from_left = lane % 4 < 2
    groups = rows // SPREAD

    @pl.when(pl.program_id(0) == 0)
    def _():
        for i, w in enumerate(weights_of(cx_ref[...], cy_ref[...], df_ref[...])):
            k_main[i] = w
        for group in range(groups):
            both = jnp.where(from_left[0:8], left_k_ref[0, group, 0:8, :], right_k_ref[0, group, 0:8, :])
            for i, w in enumerate(weights_of(*[both[j : j + 1, :] for j in range(3)])):
                k_edge[group, i : i + 1, :] = w
        for side, at in ((0, 3), (1, 0)):
            for i, w in enumerate(weights_of(*[row_k_ref[0, at, j : j + 1, :] for j in range(3)])):
                k_row[side, i : i + 1, :] = w

    edges = [jnp.where(from_left, left_ref[0, g], right_ref[0, g]) for g in range(groups)]
    corner = jnp.where(from_left, dl_ref[...], dr_ref[...])
    turn = 8 * (first + step)
    corner = jnp.where(
        lane < LANES // 2,
        pltpu.roll(corner, lax.rem(LANES - turn, LANES), 1),
        pltpu.roll(corner, LANES - 8 - turn, 1),
    )
    chain = [corner] + edges + [corner]
    up = [pltpu.roll(v, 4, 1) for v in chain]
    down = [pltpu.roll(v, LANES - 4, 1) for v in chain]
    for group, edge in enumerate(edges):
        own = own_ref[0, group]
        edge_s[0, group] = edge
        edge_s[1, group] = stencil(
            [k_edge[group, i : i + 1, :] for i in range(5)],
            edge,
            jnp.where(lane < 4, up[group], up[group + 1]),
            jnp.where(lane >= LANES - 4, down[group + 2], down[group + 1]),
            pltpu.roll(jnp.where(lane % 4 == 0, edge, own), 1, 1),
            pltpu.roll(jnp.where(lane % 4 == 3, edge, own), LANES - 1, 1),
        )

    def sides(centre, beside):
        return (
            pltpu.roll(jnp.where(lane == LANES - 1, beside, centre), 1, 1),
            pltpu.roll(jnp.where(lane == 0, beside, centre), LANES - 1, 1),
        )

    for side, (centre, west, east, turn, at) in enumerate(
        (
            (row_ref[0, 3], row_ref[0, 2], x_s[0], 2, 0),
            (row_ref[0, 0], x_s[rows - 1], row_ref[0, 1], LANES - 2, rows + 1),
        )
    ):
        k = [k_row[side, i : i + 1, :] for i in range(5)]
        first_s[at] = stencil(k, centre, west, east, *sides(centre, pltpu.roll(corner, turn, 1)))

    def lay_sides(stage):
        for row in range(rows):
            turn = (126 - row % SPREAD * 4) % LANES
            beside_s[row] = pltpu.roll(edge_s[stage, row // SPREAD], turn, 1)

    def one(row, centre, west, east):
        k = [k_main[i, row : row + 1, :] for i in range(5)]
        return stencil(k, centre, west, east, *sides(centre, beside_s[row]))

    lay_sides(0)
    for row in range(rows):
        west = row_ref[0, 3] if row == 0 else x_s[row - 1]
        east = row_ref[0, 0] if row == rows - 1 else x_s[row + 1]
        first_s[row + 1] = one(row, x_s[row], west, east)
    lay_sides(1)
    for row in range(rows):
        second_s[row] = one(row, first_s[row + 1], first_s[row], first_s[row + 2])
    for i in range(COUNT):
        base = dest_ref[i] * HEIGHT
        for r in range(HEIGHT):
            if outs == 1:
                out_refs[0][i, 0, r * members : (r + 1) * members, :] = second_s[i * HEIGHT + r]
            else:
                out_refs[i // 2][i % 2, 0, r * members : (r + 1) * members, :] = second_s[base + r]


def forecast(x, coefficients, edge, moved, dest, first, fields, after, outs):
    _, members, rows, _ = x.shape
    row, left, right, corner_l, corner_r = moved
    last = row.shape[0] - 1
    groups = rows // SPREAD
    small = pl.BlockSpec((rows, LANES), lambda i: (0, 0))
    edge_spec = pl.BlockSpec((1, groups, members, LANES), lambda i: (first + i, 0, 0, 0))
    edge_last = pl.BlockSpec((1, groups, members, LANES), lambda i: (last, 0, 0, 0))
    corner_spec = pl.BlockSpec((members, LANES), lambda i: (0, 0))
    piece = HEIGHT * members
    return pl.pallas_call(
        functools.partial(forecast_kernel, first, fields, rows, members, outs),
        grid=(fields,),
        in_specs=[
            pl.BlockSpec(memory_space=pltpu.SMEM),
            pl.BlockSpec(memory_space=pl.ANY),
            small,
            small,
            small,
            edge_spec,
            edge_spec,
            edge_spec,
            edge_last,
            edge_last,
            pl.BlockSpec((1, 4, members, LANES), lambda i: (first + i, 0, 0, 0)),
            pl.BlockSpec((1, 4, members, LANES), lambda i: (last, 0, 0, 0)),
            corner_spec,
            corner_spec,
        ]
        + [pl.BlockSpec(memory_space=pl.ANY) for _ in after],
        out_specs=[pair_spec(piece, COUNT if outs == 1 else 2)] * outs,
        out_shape=[
            jax.ShapeDtypeStruct((COUNT if outs == 1 else 2, fields, piece, LANES), jnp.float32)
        ]
        * outs,
        scratch_shapes=[
            pltpu.VMEM((5, rows, LANES), jnp.float32),
            pltpu.VMEM((groups, 8, LANES), jnp.float32),
            pltpu.VMEM((2, 8, LANES), jnp.float32),
            pltpu.VMEM((2, groups, members, LANES), jnp.float32),
            pltpu.VMEM((rows + 2, members, LANES), jnp.float32),
            pltpu.VMEM((rows, members, LANES), jnp.float32),
            pltpu.VMEM((rows, members, LANES), jnp.float32),
            pltpu.VMEM((rows, members, LANES), jnp.float32),
            pltpu.VMEM((2, members, rows + PITCH, LANES), jnp.float32),
            pltpu.SemaphoreType.DMA((2,)),
        ],
        compiler_params=pltpu.CompilerParams(vmem_limit_bytes=PACK_LIMIT),
        cost_estimate=pl.CostEstimate(
            flops=fields * rows * members * LANES * 18,
            bytes_accessed=fields * rows * members * LANES * 8,
            transcendentals=0,
        ),
        name="forecast",
    )(dest, x, *coefficients, edge, left, right, left, right, row, row, corner_l, corner_r, *after)


def halves(value):
    high = value.astype(jnp.bfloat16)
    return high, (value - high.astype(jnp.float32)).astype(jnp.bfloat16)


def dot(a, b):
    return jnp.dot(a, b, preferred_element_type=jnp.float32)


def tile_rows(refs, r):
    tall = refs[0].shape[2] // HEIGHT
    return jnp.concatenate([ref[0, 0, r * tall : (r + 1) * tall, :] for ref in refs], axis=0)


def sample_kernel(place_ref, *refs):
    step = pl.program_id(0)
    x_refs, out_ref = refs[:COUNT], refs[-1]
    slots = place_ref.shape[1]
    cells = HEIGHT * LANES
    x = jnp.concatenate([tile_rows(x_refs, r) for r in range(HEIGHT)], axis=1)
    chosen = (iota((cells, slots), 0) + step * cells == place_ref[0:1, :]).astype(jnp.bfloat16)
    high = x.astype(jnp.bfloat16)
    middle, low = halves(x - high.astype(jnp.float32))
    got = dot(high, chosen) + dot(middle, chosen) + dot(low, chosen)

    @pl.when(step == 0)
    def _():
        out_ref[...] = got

    @pl.when(step > 0)
    def _():
        out_ref[...] += got


def sample(pieces, place, after):
    _, fields, piece, _ = pieces[0][0].shape
    members = COUNT * piece // HEIGHT
    slots = place.shape[1]
    return pl.pallas_call(
        sample_kernel,
        grid=(fields,),
        in_specs=[pl.BlockSpec((1, slots), lambda i: (0, 0))]
        + piece_specs(pieces)
        + [pl.BlockSpec(memory_space=pl.ANY) for _ in after],
        out_specs=pl.BlockSpec((members, slots), lambda i: (0, 0)),
        out_shape=jax.ShapeDtypeStruct((members, slots), jnp.float32),
        compiler_params=pltpu.CompilerParams(vmem_limit_bytes=VMEM_LIMIT),
        cost_estimate=pl.CostEstimate(
            flops=fields * members * HEIGHT * LANES * slots * 6,
            bytes_accessed=fields * members * HEIGHT * LANES * 4,
            transcendentals=0,
        ),
        name="sample",
    )(place, *arrays(pieces), *after)


def transform_kernel(places_ref, mix_ref, *refs):
    x_refs, out_refs, (high_s, low_s) = refs[:COUNT], refs[COUNT:-2], refs[-2:]

    @pl.when(pl.program_id(0) == 0)
    def _():
        high_s[...], low_s[...] = halves(mix_ref[...])

    tall = x_refs[0].shape[2] // HEIGHT
    members = COUNT * tall
    for half in range(HEIGHT // 2):
        x = jnp.concatenate([tile_rows(x_refs, 2 * half + i) for i in range(2)], axis=1)
        centre = jnp.sum(x, axis=0, keepdims=True) / members
        high, low = halves(x - centre)
        result = dot(high_s[...], high) + (dot(high_s[...], low) + dot(low_s[...], high)) + centre
        for i in range(2):
            at = (2 * half + i) * tall
            for o in range(COUNT):
                out_refs[o // 2][o % 2, 0, at : at + tall, :] = result[
                    o * tall : (o + 1) * tall, i * LANES : (i + 1) * LANES
                ]


def transform(pieces, mixing_t, places):
    _, fields, piece, _ = pieces[0].shape
    members = mixing_t.shape[0]

    def spec(i):
        return pl.BlockSpec((1, 1, piece, LANES), lambda f, at: (at[i], f, 0, 0))

    return pl.pallas_call(
        transform_kernel,
        grid_spec=pltpu.PrefetchScalarGridSpec(
            num_scalar_prefetch=1,
            grid=(fields,),
            in_specs=[pl.BlockSpec((members, members), lambda f, at: (0, 0))]
            + [spec(i) for i in range(COUNT)],
            out_specs=[pair_spec(piece)] * len(CHIPS),
            scratch_shapes=[
                pltpu.VMEM((members, members), jnp.bfloat16),
                pltpu.VMEM((members, members), jnp.bfloat16),
            ],
        ),
        out_shape=[jax.ShapeDtypeStruct((2, fields, piece, LANES), jnp.float32)] * len(CHIPS),
        compiler_params=pltpu.CompilerParams(vmem_limit_bytes=VMEM_LIMIT),
        cost_estimate=pl.CostEstimate(
            flops=fields * members * members * HEIGHT * LANES * 6,
            bytes_accessed=fields * members * HEIGHT * LANES * 8,
            transcendentals=0,
        ),
        name="transform",
    )(places, mixing_t, *pieces)


def unpack_kernel(members, rows, dest_ref, *refs):
    x_refs, out_ref, held = refs[:COUNT], refs[-2], refs[-1]
    pitch = rows + 4
    for i in range(COUNT):
        base = dest_ref[i] * HEIGHT
        for r in range(HEIGHT):
            held[pl.ds(base + r, members, stride=pitch), :] = x_refs[i][0, 0, r * members : (r + 1) * members, :]
    for m in range(members):
        out_ref[0, m * rows : (m + 1) * rows, :] = held[m * pitch : m * pitch + rows, :]


def unpack(pieces, so_far, dest, first, total, members, rows):
    _, fields, piece, _ = pieces[0][0].shape
    flat = members * rows
    more = () if so_far is None else (so_far,)
    return pl.pallas_call(
        functools.partial(unpack_kernel, members, rows),
        grid=(fields,),
        in_specs=[pl.BlockSpec(memory_space=pltpu.SMEM)]
        + piece_specs(pieces)
        + [pl.BlockSpec(memory_space=pl.ANY) for _ in more],
        out_specs=pl.BlockSpec((1, flat, LANES), lambda i: (first + i, 0, 0)),
        out_shape=jax.ShapeDtypeStruct((total, flat, LANES), jnp.float32),
        scratch_shapes=[pltpu.VMEM((members * (rows + 4), LANES), jnp.float32)],
        input_output_aliases={COUNT + 1: 0} if more else {},
        compiler_params=pltpu.CompilerParams(vmem_limit_bytes=VMEM_LIMIT),
        cost_estimate=pl.CostEstimate(
            flops=0, bytes_accessed=fields * flat * LANES * 8, transcendentals=0
        ),
        name="unpack",
    )(dest, *arrays(pieces), *more)


def hop(value, offset, sign):
    return lax.ppermute(value, "mem", [(i, shifted(i, offset, sign)) for i in range(COUNT)])


def travel(sent, sign, skip=0):
    return [
        value if chip == (0, 0) else hop(value, chip + (0,), sign)
        for value, chip in zip(sent, CHIPS[skip:])
    ]


def trade(arrived, group):
    return hop(jnp.concatenate([arrived[o][1:2] for o in group], axis=0), (0, 0, 1), 1)


def settled(arrived, traded):
    pieces = []
    for group, value in zip(GROUPS, traded):
        for at, o in enumerate(group):
            pieces += [(arrived[o], 0), (value, at)]
    return pieces


def dot3(a, b, dims=(1, 0)):
    (ah, al), (bh, bl) = halves(a), halves(b)

    def one(u, v):
        return lax.dot_general(
            u, v, (((dims[0],), (dims[1],)), ((), ())), preferred_element_type=jnp.float32
        )

    return one(ah, bh) + (one(ah, bl) + one(al, bh))


def mixing_kernel(count_ref, raw_ref, value_ref, precision_ref, class_ref, out_ref):
    members, slots = raw_ref.shape
    raw = raw_ref[...]
    centre_obs = jnp.sum(raw, axis=0, keepdims=True) / members
    usable = iota((1, slots), 1) < count_ref[0]
    weight = jnp.where(usable, precision_ref[...] / (1.0 + class_ref[...].astype(jnp.float32)), 0.0)
    root_weight = jnp.sqrt(weight)
    spread = (raw - centre_obs) * root_weight
    small = dot3(spread, spread, (0, 0))
    inflation = members - 1.0
    scale = jnp.sqrt(
        inflation * inflation * members
        + 2.0 * inflation * jnp.sum(spread * spread, keepdims=True)
        + jnp.sum(small * small, keepdims=True)
    )
    eye = (iota((slots, slots), 0) == iota((slots, slots), 1)).astype(jnp.float32)
    start = inflation / scale
    y, z = start, jnp.ones_like(start)
    root_y = start * eye + small / scale
    factor = 1.5 * eye - 0.5 * root_y
    p = 1.5 - 0.5 * y
    root_z, part_z, z = factor, -0.5 * eye, p
    root_y, y = dot3(root_y, factor), y * p
    for iteration in range(1, NEWTON):
        both = dot3(jnp.concatenate([root_z, part_z], axis=0), root_y)
        part = z * (start * part_z + root_z) + both[slots:]
        factor = 1.5 * eye - 0.5 * both[:slots]
        p = 1.5 - 0.5 * z * y
        both = dot3(jnp.concatenate([factor, -0.5 * part], axis=0), root_z)
        if iteration + 1 < NEWTON:
            root_y, y = dot3(root_y, factor), y * p
        root_z, part_z, z = both[:slots], p * part_z + both[slots:], z * p
    driven = jnp.broadcast_to(root_weight * (value_ref[...] - centre_obs), (8, slots))
    driven = dot3(dot3(driven, root_z), root_z)
    shift = dot3(driven, spread, (1, 1))[0:1] / scale
    gain = jnp.sqrt(inflation / scale)
    low_rank = dot3(dot3(spread, part_z * (gain / scale)), spread, (1, 1))
    whole = iota((members, members), 0) == iota((members, members), 1)
    out_ref[...] = low_rank + jnp.where(whole, gain * z, 0.0) + shift


def mixing_transposed(raw_values, report_value, report_precision, report_class, slot_count):
    members, slots = raw_values.shape
    row = pl.BlockSpec((1, slots), lambda: (0, 0))
    return pl.pallas_call(
        mixing_kernel,
        in_specs=[
            pl.BlockSpec(memory_space=pltpu.SMEM),
            pl.BlockSpec((members, slots), lambda: (0, 0)),
            row,
            row,
            row,
        ],
        out_specs=pl.BlockSpec((members, members), lambda: (0, 0)),
        out_shape=jax.ShapeDtypeStruct((members, members), jnp.float32),
        compiler_params=pltpu.CompilerParams(vmem_limit_bytes=VMEM_LIMIT),
        cost_estimate=pl.CostEstimate(
            flops=NEWTON * 5 * 6 * slots**3, bytes_accessed=4 * members * members, transcendentals=0
        ),
        name="mixing",
    )(
        slot_count.reshape(1),
        raw_values,
        report_value[None, :],
        report_precision[None, :],
        report_class[None, :],
    )


def own_row(table, tile):
    flat_table = table.reshape((table.shape[0] * table.shape[1],) + table.shape[2:])
    return lax.dynamic_index_in_dim(flat_table, tile, 0, keepdims=False)


def on_device(
    prior_members,
    courant_x,
    courant_y,
    diffusion,
    report_level,
    report_cell,
    report_value,
    report_precision,
    report_class,
    report_count,
):
    total, members, rows, _ = prior_members.shape
    coefficients = (courant_x, courant_y, diffusion)
    tile = lax.axis_index("mem")
    dest = jnp.stack([shifted(tile, o) for o in OFFSETS]).astype(jnp.int32)
    half = total // 2

    source = jnp.stack([shifted(tile, o, -1) for o in OFFSETS]).astype(jnp.int32)
    packed = pack(prior_members, coefficients, 0, total)
    moved = exchange(packed)

    def fields_sent(first, after, outs):
        return list(
            forecast(prior_members, coefficients, packed[0], moved, dest, first, half, after, outs)
        )

    sent = fields_sent(0, (), len(CHIPS))
    arrived = travel(sent[:EARLY], 1)
    traded = [trade(arrived, GROUPS[0])]
    following = fields_sent(half, traded, 1)
    following, sent[EARLY:] = lax.optimization_barrier((following, sent[EARLY:]))
    arrived += travel(sent[EARLY:], 1, EARLY)
    following, arrived[1:] = lax.optimization_barrier((following, arrived[1:]))
    traded += [trade(arrived, group) for group in GROUPS[1:]]
    second = lax.all_to_all(following[0], "mem", split_axis=0, concat_axis=0, tiled=True)
    gathered = settled(arrived, traded)

    level, cell = own_row(report_level, tile), own_row(report_cell, tile)
    place = (level * (HEIGHT * LANES) + cell)[None, :]
    mixing_t = mixing_transposed(
        sample(gathered, place, following),
        own_row(report_value, tile),
        own_row(report_precision, tile),
        own_row(report_class, tile),
        own_row(report_count, tile),
    )
    leads = jnp.array([p[1] for p in gathered], jnp.int32)
    analysed = list(transform(arrays(gathered), mixing_t, leads))

    arrived = travel(analysed[:EARLY], -1)
    traded = [trade(arrived, GROUPS[0])]
    ready = list(transform([second] * COUNT, mixing_t, source))
    ready, analysed[EARLY:] = lax.optimization_barrier((ready, analysed[EARLY:]))
    arrived += travel(analysed[EARLY:], -1, EARLY)
    traded += [trade(arrived, group) for group in GROUPS[1:]]
    traded, ready[EARLY:] = lax.optimization_barrier((traded, ready[EARLY:]))
    result = unpack(settled(arrived, traded), None, dest, 0, total, members, rows)
    arrived = travel(ready, -1)
    result, arrived[EARLY] = lax.optimization_barrier((result, arrived[EARLY]))
    traded = [trade(arrived, group) for group in GROUPS]
    result = unpack(settled(arrived, traded), result, dest, half, total, members, rows)
    return result.reshape(prior_members.shape)


def solution(mesh):
    in_specs = (
        P(None, "mem", "gx", "gy"),
        P("gx", "gy"),
        P("gx", "gy"),
        P("gx", "gy"),
        P("gx", "gy", None),
        P("gx", "gy", None),
        P("gx", "gy", None),
        P("gx", "gy", None),
        P("gx", "gy", None),
        P("gx", "gy"),
    )
    out_specs = P(None, "mem", "gx", "gy")
    return jax.shard_map(
        on_device, mesh=mesh, in_specs=in_specs, out_specs=out_specs, check_vma=False
    )
```

```python
import functools

import jax
import jax.numpy as jnp
from jax import lax
from jax.experimental import pallas as pl
from jax.experimental.pallas import tpu as pltpu
from jax.sharding import PartitionSpec as P

NEWTON = 8
LANES = 128
VMEM_LIMIT = 60 * 1024 * 1024
PACK_LIMIT = 60 * 1024 * 1024


def iota(shape, dim):
    return lax.broadcasted_iota(jnp.int32, shape, dim)


HEIGHT = 4
SPREAD = 32
PITCH = 8
CHIPS = ((0, 0), (1, 0), (0, 2), (1, 1), (0, 3), (1, 3), (0, 1), (1, 2))
OFFSETS = tuple(chip + (core,) for chip in CHIPS for core in range(2))
COUNT = len(OFFSETS)
EARLY, LATE = 5, 7
GROUPS = ((0,), (1, 2), (3, 4), (5, 6), (7,))


def shifted(index, offset, sign=1):
    z, y, core = index // 8, index // 2 % 4, index % 2
    dz, dy, dc = offset
    return (z + dz) % 2 * 8 + (y + sign * dy + 4) % 4 * 2 + (core + dc) % 2


def pair_spec(piece, count=2):
    return pl.BlockSpec((count, 1, piece, LANES), lambda i, *_: (0, i, 0, 0))


def piece_specs(pieces):
    def spec(array, lead):
        return pl.BlockSpec((1, 1) + array.shape[2:], lambda i: (lead, i, 0, 0))

    return [spec(*p) for p in pieces]


def arrays(pieces):
    return [p[0] for p in pieces]


def pack_kernel(first, fields, rows, members, x_ref, cx_ref, cy_ref, df_ref, *refs):
    edge_ref, row_ref, corner_ref, held, sems = refs[-5:]
    step = pl.program_id(0)
    pitch = rows + PITCH
    picked = (0, 1, rows - 2, rows - 1)
    groups = rows // SPREAD

    def copy(field):
        return pltpu.make_async_copy(
            x_ref.at[first + field], held.at[field, :, pl.ds(0, rows), :], sems.at[field]
        )

    @pl.when(step == 0)
    def _():
        for field in range(fields):
            copy(field).start()

    def gather(read, tall):
        lane = iota((tall, LANES), 1)
        packed = []
        for group in range(groups):
            parts = [jnp.zeros((tall, LANES), jnp.float32) for _ in range(4)]
            for i in range(SPREAD):
                moved = pltpu.roll(read(group * SPREAD + i), (4 * i + 2) % LANES, 1)
                parts[i % 4] = jnp.where(lane // 4 == i, moved, parts[i % 4])
            packed.append((parts[0] + parts[1]) + (parts[2] + parts[3]))
            edge_ref[0, group, 0:tall, :] = packed[group]
        return packed

    for field in range(fields):

        @pl.when(step == field)
        def _():
            copy(field).wait()
            flat = held.at[field].reshape(members * pitch, LANES)

            def read(row):
                value = flat[pl.ds(row, members, stride=pitch), :]
                if row in picked:
                    row_ref[0, picked.index(row)] = value
                return value

            packed = gather(read, members)
            lane = iota((members, LANES), 1)
            top = pltpu.roll(packed[0], 8 * field % LANES, 1)
            bottom = pltpu.roll(packed[-1], (8 * field + 8) % LANES, 1)
            corner = jnp.where(lane % 8 < 4, top, bottom)
            before = jnp.zeros_like(corner) if field == 0 else corner_ref[...]
            corner_ref[...] = jnp.where(lane // 8 == field, corner, before)

    @pl.when(step == fields)
    def _():
        sub = iota((8, LANES), 0)
        row_ref[0] = jnp.zeros((4, members, LANES), jnp.float32)
        edge_ref[0] = jnp.zeros((groups, members, LANES), jnp.float32)

        def read(row):
            at = slice(row, row + 1)
            value = jnp.where(
                sub == 0, cx_ref[at, :], jnp.where(sub == 1, cy_ref[at, :], df_ref[at, :])
            )
            if row in picked:
                row_ref[0, picked.index(row), 0:8, :] = value
            return value

        gather(read, 8)


def pack(x, coefficients, first, fields, after=()):
    _, members, rows, _ = x.shape
    small = pl.BlockSpec((rows, LANES), lambda i: (0, 0))
    groups = rows // SPREAD
    return pl.pallas_call(
        functools.partial(pack_kernel, first, fields, rows, members),
        grid=(fields + 1,),
        in_specs=[pl.BlockSpec(memory_space=pl.ANY), small, small, small]
        + [pl.BlockSpec(memory_space=pl.ANY) for _ in after],
        out_specs=[
            pl.BlockSpec((1, groups, members, LANES), lambda i: (i, 0, 0, 0)),
            pl.BlockSpec((1, 4, members, LANES), lambda i: (i, 0, 0, 0)),
            pl.BlockSpec((members, LANES), lambda i: (0, 0)),
        ],
        out_shape=[
            jax.ShapeDtypeStruct((fields + 1, groups, members, LANES), jnp.float32),
            jax.ShapeDtypeStruct((fields + 1, 4, members, LANES), jnp.float32),
            jax.ShapeDtypeStruct((members, LANES), jnp.float32),
        ],
        scratch_shapes=[
            pltpu.VMEM((fields, members, rows + PITCH, LANES), jnp.float32),
            pltpu.SemaphoreType.DMA((fields,)),
        ],
        compiler_params=pltpu.CompilerParams(vmem_limit_bytes=PACK_LIMIT),
        cost_estimate=pl.CostEstimate(
            flops=fields * members * rows * LANES * 2,
            bytes_accessed=fields * members * rows * LANES * 8,
            transcendentals=0,
        ),
        name="pack_edges",
    )(x, *coefficients, *after)


def exchange(packed):
    edge, row, corner = packed
    nx, ny = lax.axis_size("gx"), lax.axis_size("gy")
    right = [(i, (i + 1) % ny) for i in range(ny)]
    left = [(i, (i - 1) % ny) for i in range(ny)]

    def diagonal(step):
        return [
            (a * ny + b, ((a + 1) % nx) * ny + (b + step) % ny) for a in range(nx) for b in range(ny)
        ]

    return (
        lax.ppermute(row, "gx", [(i, (i + 1) % nx) for i in range(nx)]),
        lax.ppermute(edge, "gy", right),
        lax.ppermute(edge, "gy", left),
        lax.ppermute(corner, ("gx", "gy"), diagonal(1)),
        lax.ppermute(corner, ("gx", "gy"), diagonal(-1)),
    )


def weights_of(cx, cy, spread):
    plus_x, minus_x = jnp.maximum(cx, 0.0), jnp.minimum(cx, 0.0)
    plus_y, minus_y = jnp.maximum(cy, 0.0), jnp.minimum(cy, 0.0)
    centre = 1.0 - (plus_x - minus_x) - (plus_y - minus_y) - 4.0 * spread
    return centre, plus_x + spread, spread - minus_x, plus_y + spread, spread - minus_y


def stencil(k, centre, west, east, south, north):
    return k[0] * centre + k[1] * west + k[2] * east + k[3] * south + k[4] * north


def forecast_kernel(first, fields, rows, members, outs, dest_ref, x_hbm, cx_ref, cy_ref, df_ref, own_ref, left_ref, right_ref, left_k_ref, right_k_ref, row_ref, row_k_ref, dl_ref, dr_ref, *refs):
    k_main, k_edge, k_row, edge_s, first_s, x_s, second_s, beside_s, held, sems = refs[-10:]
    out_refs = refs[-10 - outs : -10]
    step = pl.program_id(0)
    pitch = rows + PITCH

    def copy(field):
        slot = lax.rem(field, 2)
        return pltpu.make_async_copy(
            x_hbm.at[first + field], held.at[slot, :, pl.ds(0, rows), :], sems.at[slot]
        )

    @pl.when(step == 0)
    def _():
        copy(step).start()

    @pl.when(step + 1 < fields)
    def _():
        copy(step + 1).start()

    copy(step).wait()
    flat = held.at[lax.rem(step, 2)].reshape(members * pitch, LANES)
    for row in range(rows):
        x_s[row] = flat[pl.ds(row, members, stride=pitch), :]
    lane = iota((members, LANES), 1)
    from_left = lane % 4 < 2
    groups = rows // SPREAD

    @pl.when(pl.program_id(0) == 0)
    def _():
        for i, w in enumerate(weights_of(cx_ref[...], cy_ref[...], df_ref[...])):
            k_main[i] = w
        for group in range(groups):
            both = jnp.where(from_left[0:8], left_k_ref[0, group, 0:8, :], right_k_ref[0, group, 0:8, :])
            for i, w in enumerate(weights_of(*[both[j : j + 1, :] for j in range(3)])):
                k_edge[group, i : i + 1, :] = w
        for side, at in ((0, 3), (1, 0)):
            for i, w in enumerate(weights_of(*[row_k_ref[0, at, j : j + 1, :] for j in range(3)])):
                k_row[side, i : i + 1, :] = w

    edges = [jnp.where(from_left, left_ref[0, g], right_ref[0, g]) for g in range(groups)]
    corner = jnp.where(from_left, dl_ref[...], dr_ref[...])
    turn = 8 * (first + step)
    corner = jnp.where(
        lane < LANES // 2,
        pltpu.roll(corner, lax.rem(LANES - turn, LANES), 1),
        pltpu.roll(corner, LANES - 8 - turn, 1),
    )
    chain = [corner] + edges + [corner]
    up = [pltpu.roll(v, 4, 1) for v in chain]
    down = [pltpu.roll(v, LANES - 4, 1) for v in chain]
    for group, edge in enumerate(edges):
        own = own_ref[0, group]
        edge_s[0, group] = edge
        edge_s[1, group] = stencil(
            [k_edge[group, i : i + 1, :] for i in range(5)],
            edge,
            jnp.where(lane < 4, up[group], up[group + 1]),
            jnp.where(lane >= LANES - 4, down[group + 2], down[group + 1]),
            pltpu.roll(jnp.where(lane % 4 == 0, edge, own), 1, 1),
            pltpu.roll(jnp.where(lane % 4 == 3, edge, own), LANES - 1, 1),
        )

    def sides(centre, beside):
        return (
            pltpu.roll(jnp.where(lane == LANES - 1, beside, centre), 1, 1),
            pltpu.roll(jnp.where(lane == 0, beside, centre), LANES - 1, 1),
        )

    for side, (centre, west, east, turn, at) in enumerate(
        (
            (row_ref[0, 3], row_ref[0, 2], x_s[0], 2, 0),
            (row_ref[0, 0], x_s[rows - 1], row_ref[0, 1], LANES - 2, rows + 1),
        )
    ):
        k = [k_row[side, i : i + 1, :] for i in range(5)]
        first_s[at] = stencil(k, centre, west, east, *sides(centre, pltpu.roll(corner, turn, 1)))

    def lay_sides(stage):
        for row in range(rows):
            turn = (126 - row % SPREAD * 4) % LANES
            beside_s[row] = pltpu.roll(edge_s[stage, row // SPREAD], turn, 1)

    def one(row, centre, west, east):
        k = [k_main[i, row : row + 1, :] for i in range(5)]
        return stencil(k, centre, west, east, *sides(centre, beside_s[row]))

    lay_sides(0)
    for row in range(rows):
        west = row_ref[0, 3] if row == 0 else x_s[row - 1]
        east = row_ref[0, 0] if row == rows - 1 else x_s[row + 1]
        first_s[row + 1] = one(row, x_s[row], west, east)
    lay_sides(1)
    for row in range(rows):
        second_s[row] = one(row, first_s[row + 1], first_s[row], first_s[row + 2])
    for i in range(COUNT):
        base = dest_ref[i] * HEIGHT
        for r in range(HEIGHT):
            if outs == 1:
                out_refs[0][i, 0, r * members : (r + 1) * members, :] = second_s[i * HEIGHT + r]
            else:
                out_refs[i // 2][i % 2, 0, r * members : (r + 1) * members, :] = second_s[base + r]


def forecast(x, coefficients, edge, moved, dest, first, fields, after, outs):
    _, members, rows, _ = x.shape
    row, left, right, corner_l, corner_r = moved
    last = row.shape[0] - 1
    groups = rows // SPREAD
    small = pl.BlockSpec((rows, LANES), lambda i: (0, 0))
    edge_spec = pl.BlockSpec((1, groups, members, LANES), lambda i: (first + i, 0, 0, 0))
    edge_last = pl.BlockSpec((1, groups, members, LANES), lambda i: (last, 0, 0, 0))
    corner_spec = pl.BlockSpec((members, LANES), lambda i: (0, 0))
    piece = HEIGHT * members
    return pl.pallas_call(
        functools.partial(forecast_kernel, first, fields, rows, members, outs),
        grid=(fields,),
        in_specs=[
            pl.BlockSpec(memory_space=pltpu.SMEM),
            pl.BlockSpec(memory_space=pl.ANY),
            small,
            small,
            small,
            edge_spec,
            edge_spec,
            edge_spec,
            edge_last,
            edge_last,
            pl.BlockSpec((1, 4, members, LANES), lambda i: (first + i, 0, 0, 0)),
            pl.BlockSpec((1, 4, members, LANES), lambda i: (last, 0, 0, 0)),
            corner_spec,
            corner_spec,
        ]
        + [pl.BlockSpec(memory_space=pl.ANY) for _ in after],
        out_specs=[pair_spec(piece, COUNT if outs == 1 else 2)] * outs,
        out_shape=[
            jax.ShapeDtypeStruct((COUNT if outs == 1 else 2, fields, piece, LANES), jnp.float32)
        ]
        * outs,
        scratch_shapes=[
            pltpu.VMEM((5, rows, LANES), jnp.float32),
            pltpu.VMEM((groups, 8, LANES), jnp.float32),
            pltpu.VMEM((2, 8, LANES), jnp.float32),
            pltpu.VMEM((2, groups, members, LANES), jnp.float32),
            pltpu.VMEM((rows + 2, members, LANES), jnp.float32),
            pltpu.VMEM((rows, members, LANES), jnp.float32),
            pltpu.VMEM((rows, members, LANES), jnp.float32),
            pltpu.VMEM((rows, members, LANES), jnp.float32),
            pltpu.VMEM((2, members, rows + PITCH, LANES), jnp.float32),
            pltpu.SemaphoreType.DMA((2,)),
        ],
        compiler_params=pltpu.CompilerParams(vmem_limit_bytes=PACK_LIMIT),
        cost_estimate=pl.CostEstimate(
            flops=fields * rows * members * LANES * 18,
            bytes_accessed=fields * rows * members * LANES * 8,
            transcendentals=0,
        ),
        name="forecast",
    )(dest, x, *coefficients, edge, left, right, left, right, row, row, corner_l, corner_r, *after)


def halves(value):
    high = value.astype(jnp.bfloat16)
    return high, (value - high.astype(jnp.float32)).astype(jnp.bfloat16)


def dot(a, b):
    return jnp.dot(a, b, preferred_element_type=jnp.float32)


def tile_rows(refs, r):
    tall = refs[0].shape[2] // HEIGHT
    return jnp.concatenate([ref[0, 0, r * tall : (r + 1) * tall, :] for ref in refs], axis=0)


def sample_kernel(place_ref, *refs):
    step = pl.program_id(0)
    x_refs, out_ref = refs[:COUNT], refs[-1]
    slots = place_ref.shape[1]
    cells = HEIGHT * LANES
    x = jnp.concatenate([tile_rows(x_refs, r) for r in range(HEIGHT)], axis=1)
    chosen = (iota((cells, slots), 0) + step * cells == place_ref[0:1, :]).astype(jnp.bfloat16)
    high = x.astype(jnp.bfloat16)
    middle, low = halves(x - high.astype(jnp.float32))
    got = dot(high, chosen) + dot(middle, chosen) + dot(low, chosen)

    @pl.when(step == 0)
    def _():
        out_ref[...] = got

    @pl.when(step > 0)
    def _():
        out_ref[...] += got


def sample(pieces, place, after):
    _, fields, piece, _ = pieces[0][0].shape
    members = COUNT * piece // HEIGHT
    slots = place.shape[1]
    return pl.pallas_call(
        sample_kernel,
        grid=(fields,),
        in_specs=[pl.BlockSpec((1, slots), lambda i: (0, 0))]
        + piece_specs(pieces)
        + [pl.BlockSpec(memory_space=pl.ANY) for _ in after],
        out_specs=pl.BlockSpec((members, slots), lambda i: (0, 0)),
        out_shape=jax.ShapeDtypeStruct((members, slots), jnp.float32),
        compiler_params=pltpu.CompilerParams(vmem_limit_bytes=VMEM_LIMIT),
        cost_estimate=pl.CostEstimate(
            flops=fields * members * HEIGHT * LANES * slots * 6,
            bytes_accessed=fields * members * HEIGHT * LANES * 4,
            transcendentals=0,
        ),
        name="sample",
    )(place, *arrays(pieces), *after)


def transform_kernel(places_ref, mix_ref, *refs):
    x_refs, out_refs, (high_s, low_s) = refs[:COUNT], refs[COUNT:-2], refs[-2:]

    @pl.when(pl.program_id(0) == 0)
    def _():
        high_s[...], low_s[...] = halves(mix_ref[...])

    tall = x_refs[0].shape[2] // HEIGHT
    members = COUNT * tall
    for half in range(HEIGHT // 2):
        x = jnp.concatenate([tile_rows(x_refs, 2 * half + i) for i in range(2)], axis=1)
        centre = jnp.sum(x, axis=0, keepdims=True) / members
        high, low = halves(x - centre)
        result = dot(high_s[...], high) + (dot(high_s[...], low) + dot(low_s[...], high)) + centre
        for i in range(2):
            at = (2 * half + i) * tall
            for o in range(COUNT):
                out_refs[o // 2][o % 2, 0, at : at + tall, :] = result[
                    o * tall : (o + 1) * tall, i * LANES : (i + 1) * LANES
                ]


def transform(pieces, mixing_t, places):
    _, fields, piece, _ = pieces[0].shape
    members = mixing_t.shape[0]

    def spec(i):
        return pl.BlockSpec((1, 1, piece, LANES), lambda f, at: (at[i], f, 0, 0))

    return pl.pallas_call(
        transform_kernel,
        grid_spec=pltpu.PrefetchScalarGridSpec(
            num_scalar_prefetch=1,
            grid=(fields,),
            in_specs=[pl.BlockSpec((members, members), lambda f, at: (0, 0))]
            + [spec(i) for i in range(COUNT)],
            out_specs=[pair_spec(piece)] * len(CHIPS),
            scratch_shapes=[
                pltpu.VMEM((members, members), jnp.bfloat16),
                pltpu.VMEM((members, members), jnp.bfloat16),
            ],
        ),
        out_shape=[jax.ShapeDtypeStruct((2, fields, piece, LANES), jnp.float32)] * len(CHIPS),
        compiler_params=pltpu.CompilerParams(vmem_limit_bytes=VMEM_LIMIT),
        cost_estimate=pl.CostEstimate(
            flops=fields * members * members * HEIGHT * LANES * 6,
            bytes_accessed=fields * members * HEIGHT * LANES * 8,
            transcendentals=0,
        ),
        name="transform",
    )(places, mixing_t, *pieces)


def unpack_kernel(members, rows, dest_ref, *refs):
    x_refs, out_ref, held = refs[:COUNT], refs[-2], refs[-1]
    pitch = rows + 4
    for i in range(COUNT):
        base = dest_ref[i] * HEIGHT
        for r in range(HEIGHT):
            held[pl.ds(base + r, members, stride=pitch), :] = x_refs[i][0, 0, r * members : (r + 1) * members, :]
    for m in range(members):
        out_ref[0, m * rows : (m + 1) * rows, :] = held[m * pitch : m * pitch + rows, :]


def unpack(pieces, so_far, dest, first, total, members, rows):
    _, fields, piece, _ = pieces[0][0].shape
    flat = members * rows
    more = () if so_far is None else (so_far,)
    return pl.pallas_call(
        functools.partial(unpack_kernel, members, rows),
        grid=(fields,),
        in_specs=[pl.BlockSpec(memory_space=pltpu.SMEM)]
        + piece_specs(pieces)
        + [pl.BlockSpec(memory_space=pl.ANY) for _ in more],
        out_specs=pl.BlockSpec((1, flat, LANES), lambda i: (first + i, 0, 0)),
        out_shape=jax.ShapeDtypeStruct((total, flat, LANES), jnp.float32),
        scratch_shapes=[pltpu.VMEM((members * (rows + 4), LANES), jnp.float32)],
        input_output_aliases={COUNT + 1: 0} if more else {},
        compiler_params=pltpu.CompilerParams(vmem_limit_bytes=VMEM_LIMIT),
        cost_estimate=pl.CostEstimate(
            flops=0, bytes_accessed=fields * flat * LANES * 8, transcendentals=0
        ),
        name="unpack",
    )(dest, *arrays(pieces), *more)


def hop(value, offset, sign):
    return lax.ppermute(value, "mem", [(i, shifted(i, offset, sign)) for i in range(COUNT)])


def travel(sent, sign, skip=0):
    return [
        value if chip == (0, 0) else hop(value, chip + (0,), sign)
        for value, chip in zip(sent, CHIPS[skip:])
    ]


def trade(arrived, group):
    return hop(jnp.concatenate([arrived[o][1:2] for o in group], axis=0), (0, 0, 1), 1)


def settled(arrived, traded):
    pieces = []
    for group, value in zip(GROUPS, traded):
        for at, o in enumerate(group):
            pieces += [(arrived[o], 0), (value, at)]
    return pieces


def dot3(a, b, dims=(1, 0)):
    (ah, al), (bh, bl) = halves(a), halves(b)

    def one(u, v):
        return lax.dot_general(
            u, v, (((dims[0],), (dims[1],)), ((), ())), preferred_element_type=jnp.float32
        )

    return one(ah, bh) + (one(ah, bl) + one(al, bh))


def mixing_kernel(count_ref, raw_ref, value_ref, precision_ref, class_ref, out_ref):
    members, slots = raw_ref.shape
    raw = raw_ref[...]
    centre_obs = jnp.sum(raw, axis=0, keepdims=True) / members
    usable = iota((1, slots), 1) < count_ref[0]
    weight = jnp.where(usable, precision_ref[...] / (1.0 + class_ref[...].astype(jnp.float32)), 0.0)
    root_weight = jnp.sqrt(weight)
    spread = (raw - centre_obs) * root_weight
    small = dot3(spread, spread, (0, 0))
    inflation = members - 1.0
    scale = jnp.sqrt(
        inflation * inflation * members
        + 2.0 * inflation * jnp.sum(spread * spread, keepdims=True)
        + jnp.sum(small * small, keepdims=True)
    )
    eye = (iota((slots, slots), 0) == iota((slots, slots), 1)).astype(jnp.float32)
    start = inflation / scale
    y, z = start, jnp.ones_like(start)
    root_y = start * eye + small / scale
    factor = 1.5 * eye - 0.5 * root_y
    p = 1.5 - 0.5 * y
    root_z, part_z, z = factor, -0.5 * eye, p
    root_y, y = dot3(root_y, factor), y * p
    for iteration in range(1, NEWTON):
        both = dot3(jnp.concatenate([root_z, part_z], axis=0), root_y)
        part = z * (start * part_z + root_z) + both[slots:]
        factor = 1.5 * eye - 0.5 * both[:slots]
        p = 1.5 - 0.5 * z * y
        both = dot3(jnp.concatenate([factor, -0.5 * part], axis=0), root_z)
        if iteration + 1 < NEWTON:
            root_y, y = dot3(root_y, factor), y * p
        root_z, part_z, z = both[:slots], p * part_z + both[slots:], z * p
    driven = jnp.broadcast_to(root_weight * (value_ref[...] - centre_obs), (8, slots))
    driven = dot3(dot3(driven, root_z), root_z)
    shift = dot3(driven, spread, (1, 1))[0:1] / scale
    gain = jnp.sqrt(inflation / scale)
    low_rank = dot3(dot3(spread, part_z * (gain / scale)), spread, (1, 1))
    whole = iota((members, members), 0) == iota((members, members), 1)
    out_ref[...] = low_rank + jnp.where(whole, gain * z, 0.0) + shift


def mixing_transposed(raw_values, report_value, report_precision, report_class, slot_count):
    members, slots = raw_values.shape
    row = pl.BlockSpec((1, slots), lambda: (0, 0))
    return pl.pallas_call(
        mixing_kernel,
        in_specs=[
            pl.BlockSpec(memory_space=pltpu.SMEM),
            pl.BlockSpec((members, slots), lambda: (0, 0)),
            row,
            row,
            row,
        ],
        out_specs=pl.BlockSpec((members, members), lambda: (0, 0)),
        out_shape=jax.ShapeDtypeStruct((members, members), jnp.float32),
        compiler_params=pltpu.CompilerParams(vmem_limit_bytes=VMEM_LIMIT),
        cost_estimate=pl.CostEstimate(
            flops=NEWTON * 5 * 6 * slots**3, bytes_accessed=4 * members * members, transcendentals=0
        ),
        name="mixing",
    )(
        slot_count.reshape(1),
        raw_values,
        report_value[None, :],
        report_precision[None, :],
        report_class[None, :],
    )


def own_row(table, tile):
    flat_table = table.reshape((table.shape[0] * table.shape[1],) + table.shape[2:])
    return lax.dynamic_index_in_dim(flat_table, tile, 0, keepdims=False)


def on_device(
    prior_members,
    courant_x,
    courant_y,
    diffusion,
    report_level,
    report_cell,
    report_value,
    report_precision,
    report_class,
    report_count,
):
    total, members, rows, _ = prior_members.shape
    coefficients = (courant_x, courant_y, diffusion)
    tile = lax.axis_index("mem")
    dest = jnp.stack([shifted(tile, o) for o in OFFSETS]).astype(jnp.int32)
    half = total // 2

    source = jnp.stack([shifted(tile, o, -1) for o in OFFSETS]).astype(jnp.int32)
    packed = pack(prior_members, coefficients, 0, total)
    moved = exchange(packed)

    def fields_sent(first, after, outs):
        return list(
            forecast(prior_members, coefficients, packed[0], moved, dest, first, half, after, outs)
        )

    sent = fields_sent(0, (), len(CHIPS))
    arrived = travel(sent[:EARLY], 1)
    traded = [trade(arrived, GROUPS[0])]
    following = fields_sent(half, traded, 1)
    following, sent[EARLY:] = lax.optimization_barrier((following, sent[EARLY:]))
    arrived += travel(sent[EARLY:], 1, EARLY)
    following, arrived[1:] = lax.optimization_barrier((following, arrived[1:]))
    traded += [trade(arrived, group) for group in GROUPS[1:]]
    second = lax.all_to_all(following[0], "mem", split_axis=0, concat_axis=0, tiled=True)
    gathered = settled(arrived, traded)

    level, cell = own_row(report_level, tile), own_row(report_cell, tile)
    place = (level * (HEIGHT * LANES) + cell)[None, :]
    mixing_t = mixing_transposed(
        sample(gathered, place, following),
        own_row(report_value, tile),
        own_row(report_precision, tile),
        own_row(report_class, tile),
        own_row(report_count, tile),
    )
    leads = jnp.array([p[1] for p in gathered], jnp.int32)
    analysed = list(transform(arrays(gathered), mixing_t, leads))

    arrived = travel(analysed[:EARLY], -1)
    traded = [trade(arrived, GROUPS[0])]
    ready = list(transform([second] * COUNT, mixing_t, source))
    ready, analysed[EARLY:] = lax.optimization_barrier((ready, analysed[EARLY:]))
    arrived += travel(analysed[EARLY:], -1, EARLY)
    final = travel(ready[:EARLY], -1)
    arrived[1:], final[1:] = lax.optimization_barrier((arrived[1:], final[1:]))
    traded += [trade(arrived, group) for group in GROUPS[1:]]
    result = unpack(settled(arrived, traded), None, dest, 0, total, members, rows)
    arrived = final + travel(ready[EARLY:], -1, EARLY)
    result, arrived[EARLY] = lax.optimization_barrier((result, arrived[EARLY]))
    traded = [trade(arrived, group) for group in GROUPS]
    result = unpack(settled(arrived, traded), result, dest, half, total, members, rows)
    return result.reshape(prior_members.shape)


def solution(mesh):
    in_specs = (
        P(None, "mem", "gx", "gy"),
        P("gx", "gy"),
        P("gx", "gy"),
        P("gx", "gy"),
        P("gx", "gy", None),
        P("gx", "gy", None),
        P("gx", "gy", None),
        P("gx", "gy", None),
        P("gx", "gy", None),
        P("gx", "gy"),
    )
    out_specs = P(None, "mem", "gx", "gy")
    return jax.shard_map(
        on_device, mesh=mesh, in_specs=in_specs, out_specs=out_specs, check_vma=False
    )
```

```python
import functools

import jax
import jax.numpy as jnp
from jax import lax
from jax.experimental import pallas as pl
from jax.experimental.pallas import tpu as pltpu
from jax.sharding import PartitionSpec as P

NEWTON = 8
LANES = 128
VMEM_LIMIT = 60 * 1024 * 1024
PACK_LIMIT = 60 * 1024 * 1024


def iota(shape, dim):
    return lax.broadcasted_iota(jnp.int32, shape, dim)


HEIGHT = 4
SPREAD = 32
PITCH = 8
CHIPS = ((0, 0), (1, 0), (0, 2), (1, 1), (0, 3), (1, 3), (0, 1), (1, 2))
OFFSETS = tuple(chip + (core,) for chip in CHIPS for core in range(2))
COUNT = len(OFFSETS)
EARLY, LATE = 5, 7
GROUPS = ((0,), (1, 2), (3, 4), (5, 6), (7,))


def shifted(index, offset, sign=1):
    z, y, core = index // 8, index // 2 % 4, index % 2
    dz, dy, dc = offset
    return (z + dz) % 2 * 8 + (y + sign * dy + 4) % 4 * 2 + (core + dc) % 2


def pair_spec(piece, count=2):
    return pl.BlockSpec((count, 1, piece, LANES), lambda i, *_: (0, i, 0, 0))


def piece_specs(pieces):
    def spec(array, lead):
        return pl.BlockSpec((1, 1) + array.shape[2:], lambda i: (lead, i, 0, 0))

    return [spec(*p) for p in pieces]


def arrays(pieces):
    return [p[0] for p in pieces]


def pack_kernel(first, fields, rows, members, x_ref, cx_ref, cy_ref, df_ref, *refs):
    edge_ref, row_ref, corner_ref, held, sems = refs[-5:]
    step = pl.program_id(0)
    pitch = rows + PITCH
    picked = (0, 1, rows - 2, rows - 1)
    groups = rows // SPREAD

    def copy(field):
        return pltpu.make_async_copy(
            x_ref.at[first + field], held.at[field, :, pl.ds(0, rows), :], sems.at[field]
        )

    @pl.when(step == 0)
    def _():
        for field in range(fields):
            copy(field).start()

    def gather(read, tall):
        lane = iota((tall, LANES), 1)
        packed = []
        for group in range(groups):
            parts = [jnp.zeros((tall, LANES), jnp.float32) for _ in range(4)]
            for i in range(SPREAD):
                moved = pltpu.roll(read(group * SPREAD + i), (4 * i + 2) % LANES, 1)
                parts[i % 4] = jnp.where(lane // 4 == i, moved, parts[i % 4])
            packed.append((parts[0] + parts[1]) + (parts[2] + parts[3]))
            edge_ref[0, group, 0:tall, :] = packed[group]
        return packed

    for field in range(fields):

        @pl.when(step == field)
        def _():
            copy(field).wait()
            flat = held.at[field].reshape(members * pitch, LANES)

            def read(row):
                value = flat[pl.ds(row, members, stride=pitch), :]
                if row in picked:
                    row_ref[0, picked.index(row)] = value
                return value

            packed = gather(read, members)
            lane = iota((members, LANES), 1)
            top = pltpu.roll(packed[0], 8 * field % LANES, 1)
            bottom = pltpu.roll(packed[-1], (8 * field + 8) % LANES, 1)
            corner = jnp.where(lane % 8 < 4, top, bottom)
            before = jnp.zeros_like(corner) if field == 0 else corner_ref[...]
            corner_ref[...] = jnp.where(lane // 8 == field, corner, before)

    @pl.when(step == fields)
    def _():
        sub = iota((8, LANES), 0)
        row_ref[0] = jnp.zeros((4, members, LANES), jnp.float32)
        edge_ref[0] = jnp.zeros((groups, members, LANES), jnp.float32)

        def read(row):
            at = slice(row, row + 1)
            value = jnp.where(
                sub == 0, cx_ref[at, :], jnp.where(sub == 1, cy_ref[at, :], df_ref[at, :])
            )
            if row in picked:
                row_ref[0, picked.index(row), 0:8, :] = value
            return value

        gather(read, 8)


def pack(x, coefficients, first, fields, after=()):
    _, members, rows, _ = x.shape
    small = pl.BlockSpec((rows, LANES), lambda i: (0, 0))
    groups = rows // SPREAD
    return pl.pallas_call(
        functools.partial(pack_kernel, first, fields, rows, members),
        grid=(fields + 1,),
        in_specs=[pl.BlockSpec(memory_space=pl.ANY), small, small, small]
        + [pl.BlockSpec(memory_space=pl.ANY) for _ in after],
        out_specs=[
            pl.BlockSpec((1, groups, members, LANES), lambda i: (i, 0, 0, 0)),
            pl.BlockSpec((1, 4, members, LANES), lambda i: (i, 0, 0, 0)),
            pl.BlockSpec((members, LANES), lambda i: (0, 0)),
        ],
        out_shape=[
            jax.ShapeDtypeStruct((fields + 1, groups, members, LANES), jnp.float32),
            jax.ShapeDtypeStruct((fields + 1, 4, members, LANES), jnp.float32),
            jax.ShapeDtypeStruct((members, LANES), jnp.float32),
        ],
        scratch_shapes=[
            pltpu.VMEM((fields, members, rows + PITCH, LANES), jnp.float32),
            pltpu.SemaphoreType.DMA((fields,)),
        ],
        compiler_params=pltpu.CompilerParams(vmem_limit_bytes=PACK_LIMIT),
        cost_estimate=pl.CostEstimate(
            flops=fields * members * rows * LANES * 2,
            bytes_accessed=fields * members * rows * LANES * 8,
            transcendentals=0,
        ),
        name="pack_edges",
    )(x, *coefficients, *after)


def exchange(packed):
    edge, row, corner = packed
    nx, ny = lax.axis_size("gx"), lax.axis_size("gy")
    right = [(i, (i + 1) % ny) for i in range(ny)]
    left = [(i, (i - 1) % ny) for i in range(ny)]

    def diagonal(step):
        return [
            (a * ny + b, ((a + 1) % nx) * ny + (b + step) % ny) for a in range(nx) for b in range(ny)
        ]

    return (
        lax.ppermute(row, "gx", [(i, (i + 1) % nx) for i in range(nx)]),
        lax.ppermute(edge, "gy", right),
        lax.ppermute(edge, "gy", left),
        lax.ppermute(corner, ("gx", "gy"), diagonal(1)),
        lax.ppermute(corner, ("gx", "gy"), diagonal(-1)),
    )


def weights_of(cx, cy, spread):
    plus_x, minus_x = jnp.maximum(cx, 0.0), jnp.minimum(cx, 0.0)
    plus_y, minus_y = jnp.maximum(cy, 0.0), jnp.minimum(cy, 0.0)
    centre = 1.0 - (plus_x - minus_x) - (plus_y - minus_y) - 4.0 * spread
    return centre, plus_x + spread, spread - minus_x, plus_y + spread, spread - minus_y


def stencil(k, centre, west, east, south, north):
    return k[0] * centre + k[1] * west + k[2] * east + k[3] * south + k[4] * north


def forecast_kernel(first, fields, rows, members, outs, dest_ref, x_hbm, cx_ref, cy_ref, df_ref, own_ref, left_ref, right_ref, left_k_ref, right_k_ref, row_ref, row_k_ref, dl_ref, dr_ref, *refs):
    k_main, k_edge, k_row, edge_s, first_s, x_s, second_s, beside_s, held, sems = refs[-10:]
    out_refs = refs[-10 - outs : -10]
    step = pl.program_id(0)
    pitch = rows + PITCH

    def copy(field):
        slot = lax.rem(field, 2)
        return pltpu.make_async_copy(
            x_hbm.at[first + field], held.at[slot, :, pl.ds(0, rows), :], sems.at[slot]
        )

    @pl.when(step == 0)
    def _():
        copy(step).start()

    @pl.when(step + 1 < fields)
    def _():
        copy(step + 1).start()

    copy(step).wait()
    flat = held.at[lax.rem(step, 2)].reshape(members * pitch, LANES)
    for row in range(rows):
        x_s[row] = flat[pl.ds(row, members, stride=pitch), :]
    lane = iota((members, LANES), 1)
    from_left = lane % 4 < 2
    groups = rows // SPREAD

    @pl.when(pl.program_id(0) == 0)
    def _():
        for i, w in enumerate(weights_of(cx_ref[...], cy_ref[...], df_ref[...])):
            k_main[i] = w
        for group in range(groups):
            both = jnp.where(from_left[0:8], left_k_ref[0, group, 0:8, :], right_k_ref[0, group, 0:8, :])
            for i, w in enumerate(weights_of(*[both[j : j + 1, :] for j in range(3)])):
                k_edge[group, i : i + 1, :] = w
        for side, at in ((0, 3), (1, 0)):
            for i, w in enumerate(weights_of(*[row_k_ref[0, at, j : j + 1, :] for j in range(3)])):
                k_row[side, i : i + 1, :] = w

    edges = [jnp.where(from_left, left_ref[0, g], right_ref[0, g]) for g in range(groups)]
    corner = jnp.where(from_left, dl_ref[...], dr_ref[...])
    turn = 8 * (first + step)
    corner = jnp.where(
        lane < LANES // 2,
        pltpu.roll(corner, lax.rem(LANES - turn, LANES), 1),
        pltpu.roll(corner, LANES - 8 - turn, 1),
    )
    chain = [corner] + edges + [corner]
    up = [pltpu.roll(v, 4, 1) for v in chain]
    down = [pltpu.roll(v, LANES - 4, 1) for v in chain]
    for group, edge in enumerate(edges):
        own = own_ref[0, group]
        edge_s[0, group] = edge
        edge_s[1, group] = stencil(
            [k_edge[group, i : i + 1, :] for i in range(5)],
            edge,
            jnp.where(lane < 4, up[group], up[group + 1]),
            jnp.where(lane >= LANES - 4, down[group + 2], down[group + 1]),
            pltpu.roll(jnp.where(lane % 4 == 0, edge, own), 1, 1),
            pltpu.roll(jnp.where(lane % 4 == 3, edge, own), LANES - 1, 1),
        )

    def sides(centre, beside):
        return (
            pltpu.roll(jnp.where(lane == LANES - 1, beside, centre), 1, 1),
            pltpu.roll(jnp.where(lane == 0, beside, centre), LANES - 1, 1),
        )

    for side, (centre, west, east, turn, at) in enumerate(
        (
            (row_ref[0, 3], row_ref[0, 2], x_s[0], 2, 0),
            (row_ref[0, 0], x_s[rows - 1], row_ref[0, 1], LANES - 2, rows + 1),
        )
    ):
        k = [k_row[side, i : i + 1, :] for i in range(5)]
        first_s[at] = stencil(k, centre, west, east, *sides(centre, pltpu.roll(corner, turn, 1)))

    def lay_sides(stage):
        for row in range(rows):
            turn = (126 - row % SPREAD * 4) % LANES
            beside_s[row] = pltpu.roll(edge_s[stage, row // SPREAD], turn, 1)

    def one(row, centre, west, east):
        k = [k_main[i, row : row + 1, :] for i in range(5)]
        return stencil(k, centre, west, east, *sides(centre, beside_s[row]))

    lay_sides(0)
    for row in range(rows):
        west = row_ref[0, 3] if row == 0 else x_s[row - 1]
        east = row_ref[0, 0] if row == rows - 1 else x_s[row + 1]
        first_s[row + 1] = one(row, x_s[row], west, east)
    lay_sides(1)
    for row in range(rows):
        second_s[row] = one(row, first_s[row + 1], first_s[row], first_s[row + 2])
    for i in range(COUNT):
        base = dest_ref[i] * HEIGHT
        for r in range(HEIGHT):
            if outs == 1:
                out_refs[0][i, 0, r * members : (r + 1) * members, :] = second_s[i * HEIGHT + r]
            else:
                out_refs[i // 2][i % 2, 0, r * members : (r + 1) * members, :] = second_s[base + r]


def forecast(x, coefficients, edge, moved, dest, first, fields, after, outs):
    _, members, rows, _ = x.shape
    row, left, right, corner_l, corner_r = moved
    last = row.shape[0] - 1
    groups = rows // SPREAD
    small = pl.BlockSpec((rows, LANES), lambda i: (0, 0))
    edge_spec = pl.BlockSpec((1, groups, members, LANES), lambda i: (first + i, 0, 0, 0))
    edge_last = pl.BlockSpec((1, groups, members, LANES), lambda i: (last, 0, 0, 0))
    corner_spec = pl.BlockSpec((members, LANES), lambda i: (0, 0))
    piece = HEIGHT * members
    return pl.pallas_call(
        functools.partial(forecast_kernel, first, fields, rows, members, outs),
        grid=(fields,),
        in_specs=[
            pl.BlockSpec(memory_space=pltpu.SMEM),
            pl.BlockSpec(memory_space=pl.ANY),
            small,
            small,
            small,
            edge_spec,
            edge_spec,
            edge_spec,
            edge_last,
            edge_last,
            pl.BlockSpec((1, 4, members, LANES), lambda i: (first + i, 0, 0, 0)),
            pl.BlockSpec((1, 4, members, LANES), lambda i: (last, 0, 0, 0)),
            corner_spec,
            corner_spec,
        ]
        + [pl.BlockSpec(memory_space=pl.ANY) for _ in after],
        out_specs=[pair_spec(piece, COUNT if outs == 1 else 2)] * outs,
        out_shape=[
            jax.ShapeDtypeStruct((COUNT if outs == 1 else 2, fields, piece, LANES), jnp.float32)
        ]
        * outs,
        scratch_shapes=[
            pltpu.VMEM((5, rows, LANES), jnp.float32),
            pltpu.VMEM((groups, 8, LANES), jnp.float32),
            pltpu.VMEM((2, 8, LANES), jnp.float32),
            pltpu.VMEM((2, groups, members, LANES), jnp.float32),
            pltpu.VMEM((rows + 2, members, LANES), jnp.float32),
            pltpu.VMEM((rows, members, LANES), jnp.float32),
            pltpu.VMEM((rows, members, LANES), jnp.float32),
            pltpu.VMEM((rows, members, LANES), jnp.float32),
            pltpu.VMEM((2, members, rows + PITCH, LANES), jnp.float32),
            pltpu.SemaphoreType.DMA((2,)),
        ],
        compiler_params=pltpu.CompilerParams(vmem_limit_bytes=PACK_LIMIT),
        cost_estimate=pl.CostEstimate(
            flops=fields * rows * members * LANES * 18,
            bytes_accessed=fields * rows * members * LANES * 8,
            transcendentals=0,
        ),
        name="forecast",
    )(dest, x, *coefficients, edge, left, right, left, right, row, row, corner_l, corner_r, *after)


def halves(value):
    high = value.astype(jnp.bfloat16)
    return high, (value - high.astype(jnp.float32)).astype(jnp.bfloat16)


def dot(a, b):
    return jnp.dot(a, b, preferred_element_type=jnp.float32)


def tile_rows(refs, r):
    tall = refs[0].shape[2] // HEIGHT
    return jnp.concatenate([ref[0, 0, r * tall : (r + 1) * tall, :] for ref in refs], axis=0)


def sample_kernel(place_ref, *refs):
    step = pl.program_id(0)
    x_refs, out_ref = refs[:COUNT], refs[-1]
    slots = place_ref.shape[1]
    cells = HEIGHT * LANES
    x = jnp.concatenate([tile_rows(x_refs, r) for r in range(HEIGHT)], axis=1)
    chosen = (iota((cells, slots), 0) + step * cells == place_ref[0:1, :]).astype(jnp.bfloat16)
    high = x.astype(jnp.bfloat16)
    middle, low = halves(x - high.astype(jnp.float32))
    got = dot(high, chosen) + dot(middle, chosen) + dot(low, chosen)

    @pl.when(step == 0)
    def _():
        out_ref[...] = got

    @pl.when(step > 0)
    def _():
        out_ref[...] += got


def sample(pieces, place, after):
    _, fields, piece, _ = pieces[0][0].shape
    members = COUNT * piece // HEIGHT
    slots = place.shape[1]
    return pl.pallas_call(
        sample_kernel,
        grid=(fields,),
        in_specs=[pl.BlockSpec((1, slots), lambda i: (0, 0))]
        + piece_specs(pieces)
        + [pl.BlockSpec(memory_space=pl.ANY) for _ in after],
        out_specs=pl.BlockSpec((members, slots), lambda i: (0, 0)),
        out_shape=jax.ShapeDtypeStruct((members, slots), jnp.float32),
        compiler_params=pltpu.CompilerParams(vmem_limit_bytes=VMEM_LIMIT),
        cost_estimate=pl.CostEstimate(
            flops=fields * members * HEIGHT * LANES * slots * 6,
            bytes_accessed=fields * members * HEIGHT * LANES * 4,
            transcendentals=0,
        ),
        name="sample",
    )(place, *arrays(pieces), *after)


def transform_kernel(places_ref, mix_ref, *refs):
    x_refs, out_refs, (high_s, low_s) = refs[:COUNT], refs[COUNT:-2], refs[-2:]

    @pl.when(pl.program_id(0) == 0)
    def _():
        high_s[...], low_s[...] = halves(mix_ref[...])

    tall = x_refs[0].shape[2] // HEIGHT
    members = COUNT * tall
    for half in range(HEIGHT // 2):
        x = jnp.concatenate([tile_rows(x_refs, 2 * half + i) for i in range(2)], axis=1)
        centre = jnp.sum(x, axis=0, keepdims=True) / members
        high, low = halves(x - centre)
        result = dot(high_s[...], high) + (dot(high_s[...], low) + dot(low_s[...], high)) + centre
        for i in range(2):
            at = (2 * half + i) * tall
            for o in range(COUNT):
                out_refs[o // 2][o % 2, 0, at : at + tall, :] = result[
                    o * tall : (o + 1) * tall, i * LANES : (i + 1) * LANES
                ]


def transform(pieces, mixing_t, places):
    _, fields, piece, _ = pieces[0].shape
    members = mixing_t.shape[0]

    def spec(i):
        return pl.BlockSpec((1, 1, piece, LANES), lambda f, at: (at[i], f, 0, 0))

    return pl.pallas_call(
        transform_kernel,
        grid_spec=pltpu.PrefetchScalarGridSpec(
            num_scalar_prefetch=1,
            grid=(fields,),
            in_specs=[pl.BlockSpec((members, members), lambda f, at: (0, 0))]
            + [spec(i) for i in range(COUNT)],
            out_specs=[pair_spec(piece)] * len(CHIPS),
            scratch_shapes=[
                pltpu.VMEM((members, members), jnp.bfloat16),
                pltpu.VMEM((members, members), jnp.bfloat16),
            ],
        ),
        out_shape=[jax.ShapeDtypeStruct((2, fields, piece, LANES), jnp.float32)] * len(CHIPS),
        compiler_params=pltpu.CompilerParams(vmem_limit_bytes=VMEM_LIMIT),
        cost_estimate=pl.CostEstimate(
            flops=fields * members * members * HEIGHT * LANES * 6,
            bytes_accessed=fields * members * HEIGHT * LANES * 8,
            transcendentals=0,
        ),
        name="transform",
    )(places, mixing_t, *pieces)


def unpack_kernel(members, rows, dest_ref, *refs):
    x_refs, out_ref, held = refs[:COUNT], refs[-2], refs[-1]
    pitch = rows + 4
    for i in range(COUNT):
        base = dest_ref[i] * HEIGHT
        for r in range(HEIGHT):
            held[pl.ds(base + r, members, stride=pitch), :] = x_refs[i][0, 0, r * members : (r + 1) * members, :]
    for m in range(members):
        out_ref[0, m * rows : (m + 1) * rows, :] = held[m * pitch : m * pitch + rows, :]


def unpack(pieces, so_far, dest, first, total, members, rows):
    _, fields, piece, _ = pieces[0][0].shape
    flat = members * rows
    more = () if so_far is None else (so_far,)
    return pl.pallas_call(
        functools.partial(unpack_kernel, members, rows),
        grid=(fields,),
        in_specs=[pl.BlockSpec(memory_space=pltpu.SMEM)]
        + piece_specs(pieces)
        + [pl.BlockSpec(memory_space=pl.ANY) for _ in more],
        out_specs=pl.BlockSpec((1, flat, LANES), lambda i: (first + i, 0, 0)),
        out_shape=jax.ShapeDtypeStruct((total, flat, LANES), jnp.float32),
        scratch_shapes=[pltpu.VMEM((members * (rows + 4), LANES), jnp.float32)],
        input_output_aliases={COUNT + 1: 0} if more else {},
        compiler_params=pltpu.CompilerParams(vmem_limit_bytes=VMEM_LIMIT),
        cost_estimate=pl.CostEstimate(
            flops=0, bytes_accessed=fields * flat * LANES * 8, transcendentals=0
        ),
        name="unpack",
    )(dest, *arrays(pieces), *more)


def hop(value, offset, sign):
    return lax.ppermute(value, "mem", [(i, shifted(i, offset, sign)) for i in range(COUNT)])


def travel(sent, sign, skip=0):
    return [
        value if chip == (0, 0) else hop(value, chip + (0,), sign)
        for value, chip in zip(sent, CHIPS[skip:])
    ]


def trade(arrived, group):
    return hop(jnp.concatenate([arrived[o][1:2] for o in group], axis=0), (0, 0, 1), 1)


def settled(arrived, traded):
    pieces = []
    for group, value in zip(GROUPS, traded):
        for at, o in enumerate(group):
            pieces += [(arrived[o], 0), (value, at)]
    return pieces


def dot3(a, b, dims=(1, 0)):
    (ah, al), (bh, bl) = halves(a), halves(b)

    def one(u, v):
        return lax.dot_general(
            u, v, (((dims[0],), (dims[1],)), ((), ())), preferred_element_type=jnp.float32
        )

    return one(ah, bh) + (one(ah, bl) + one(al, bh))


def mixing_kernel(count_ref, raw_ref, value_ref, precision_ref, class_ref, out_ref):
    members, slots = raw_ref.shape
    raw = raw_ref[...]
    centre_obs = jnp.sum(raw, axis=0, keepdims=True) / members
    usable = iota((1, slots), 1) < count_ref[0]
    weight = jnp.where(usable, precision_ref[...] / (1.0 + class_ref[...].astype(jnp.float32)), 0.0)
    root_weight = jnp.sqrt(weight)
    spread = (raw - centre_obs) * root_weight
    small = dot3(spread, spread, (0, 0))
    inflation = members - 1.0
    scale = jnp.sqrt(
        inflation * inflation * members
        + 2.0 * inflation * jnp.sum(spread * spread, keepdims=True)
        + jnp.sum(small * small, keepdims=True)
    )
    eye = (iota((slots, slots), 0) == iota((slots, slots), 1)).astype(jnp.float32)
    start = inflation / scale
    y, z = start, jnp.ones_like(start)
    root_y = start * eye + small / scale
    factor = 1.5 * eye - 0.5 * root_y
    p = 1.5 - 0.5 * y
    root_z, part_z, z = factor, -0.5 * eye, p
    root_y, y = dot3(root_y, factor), y * p
    for iteration in range(1, NEWTON):
        both = dot3(jnp.concatenate([root_z, part_z], axis=0), root_y)
        part = z * (start * part_z + root_z) + both[slots:]
        factor = 1.5 * eye - 0.5 * both[:slots]
        p = 1.5 - 0.5 * z * y
        both = dot3(jnp.concatenate([factor, -0.5 * part], axis=0), root_z)
        if iteration + 1 < NEWTON:
            root_y, y = dot3(root_y, factor), y * p
        root_z, part_z, z = both[:slots], p * part_z + both[slots:], z * p
    driven = jnp.broadcast_to(root_weight * (value_ref[...] - centre_obs), (8, slots))
    driven = dot3(dot3(driven, root_z), root_z)
    shift = dot3(driven, spread, (1, 1))[0:1] / scale
    gain = jnp.sqrt(inflation / scale)
    low_rank = dot3(dot3(spread, part_z * (gain / scale)), spread, (1, 1))
    whole = iota((members, members), 0) == iota((members, members), 1)
    out_ref[...] = low_rank + jnp.where(whole, gain * z, 0.0) + shift


def mixing_transposed(raw_values, report_value, report_precision, report_class, slot_count):
    members, slots = raw_values.shape
    row = pl.BlockSpec((1, slots), lambda: (0, 0))
    return pl.pallas_call(
        mixing_kernel,
        in_specs=[
            pl.BlockSpec(memory_space=pltpu.SMEM),
            pl.BlockSpec((members, slots), lambda: (0, 0)),
            row,
            row,
            row,
        ],
        out_specs=pl.BlockSpec((members, members), lambda: (0, 0)),
        out_shape=jax.ShapeDtypeStruct((members, members), jnp.float32),
        compiler_params=pltpu.CompilerParams(vmem_limit_bytes=VMEM_LIMIT),
        cost_estimate=pl.CostEstimate(
            flops=NEWTON * 5 * 6 * slots**3, bytes_accessed=4 * members * members, transcendentals=0
        ),
        name="mixing",
    )(
        slot_count.reshape(1),
        raw_values,
        report_value[None, :],
        report_precision[None, :],
        report_class[None, :],
    )


def own_row(table, tile):
    flat_table = table.reshape((table.shape[0] * table.shape[1],) + table.shape[2:])
    return lax.dynamic_index_in_dim(flat_table, tile, 0, keepdims=False)


def on_device(
    prior_members,
    courant_x,
    courant_y,
    diffusion,
    report_level,
    report_cell,
    report_value,
    report_precision,
    report_class,
    report_count,
):
    total, members, rows, _ = prior_members.shape
    coefficients = (courant_x, courant_y, diffusion)
    tile = lax.axis_index("mem")
    dest = jnp.stack([shifted(tile, o) for o in OFFSETS]).astype(jnp.int32)
    half = total // 2

    source = jnp.stack([shifted(tile, o, -1) for o in OFFSETS]).astype(jnp.int32)
    packed = pack(prior_members, coefficients, 0, total)
    moved = exchange(packed)

    def fields_sent(first, after, outs):
        return list(
            forecast(prior_members, coefficients, packed[0], moved, dest, first, half, after, outs)
        )

    sent = fields_sent(0, (), len(CHIPS))
    arrived = travel(sent[:EARLY], 1)
    traded = [trade(arrived, GROUPS[0])]
    following = fields_sent(half, traded, 1)
    following, sent[EARLY:] = lax.optimization_barrier((following, sent[EARLY:]))
    arrived += travel(sent[EARLY:], 1, EARLY)
    following, arrived[1:] = lax.optimization_barrier((following, arrived[1:]))
    traded += [trade(arrived, group) for group in GROUPS[1:]]
    second = lax.all_to_all(following[0], "mem", split_axis=0, concat_axis=0, tiled=True)
    gathered = settled(arrived, traded)

    level, cell = own_row(report_level, tile), own_row(report_cell, tile)
    place = (level * (HEIGHT * LANES) + cell)[None, :]
    mixing_t = mixing_transposed(
        sample(gathered, place, following),
        own_row(report_value, tile),
        own_row(report_precision, tile),
        own_row(report_class, tile),
        own_row(report_count, tile),
    )
    leads = jnp.array([p[1] for p in gathered], jnp.int32)
    analysed = list(transform(arrays(gathered), mixing_t, leads))

    arrived = travel(analysed[:EARLY], -1)
    traded = [trade(arrived, GROUPS[0])]
    ready = list(transform([second] * COUNT, mixing_t, source))
    ready, analysed[EARLY:] = lax.optimization_barrier((ready, analysed[EARLY:]))
    arrived += travel(analysed[EARLY:], -1, EARLY)
    final = travel(ready[:EARLY], -1)
    arrived[1:], final[1:3] = lax.optimization_barrier((arrived[1:], final[1:3]))
    traded += [trade(arrived, group) for group in GROUPS[1:]]
    traded, ready[EARLY:] = lax.optimization_barrier((traded, ready[EARLY:]))
    result = unpack(settled(arrived, traded), None, dest, 0, total, members, rows)
    arrived = final + travel(ready[EARLY:], -1, EARLY)
    result, arrived[EARLY] = lax.optimization_barrier((result, arrived[EARLY]))
    traded = [trade(arrived, group) for group in GROUPS]
    result = unpack(settled(arrived, traded), result, dest, half, total, members, rows)
    return result.reshape(prior_members.shape)


def solution(mesh):
    in_specs = (
        P(None, "mem", "gx", "gy"),
        P("gx", "gy"),
        P("gx", "gy"),
        P("gx", "gy"),
        P("gx", "gy", None),
        P("gx", "gy", None),
        P("gx", "gy", None),
        P("gx", "gy", None),
        P("gx", "gy", None),
        P("gx", "gy"),
    )
    out_specs = P(None, "mem", "gx", "gy")
    return jax.shard_map(
        on_device, mesh=mesh, in_specs=in_specs, out_specs=out_specs, check_vma=False
    )
```
